256 devices in a mesh: dp: 16 (over z, y_hi), pipe: 2 (over core), tensor: 8 (over y_lo, x).
Axes of the slice: x: 4, y: 4 (y_hi: 2, y_lo: 2; y = y_hi * 2 + y_lo), z: 8, core: 2. Of those that a mesh axis runs over, the one named last changes fastest.
Arguments:
- section_input: bfloat16 [4, 2048, 6144], P(None, 'dp', 'tensor'), may hold values from -80 to 80
- gain: float32 [2, 6144], P('pipe', 'tensor'), may hold values from 0.5 to 1.5
- weight: bfloat16 [2, 6144, 6144], P('pipe', 'tensor'), may hold values from -0.078125 to 0.078125
- old_factor: float32 [2, 8, 48, 128, 128], P('pipe', 'tensor', 'dp'), may hold values from -0.09 to 0.09
- slot_table: int32 [48], replicated, may hold values from -1 to 20, as said below
- capture: int32 [2, 4], P('pipe'), may hold values from 0 to 1, as said below
Outputs:
- section_out: bfloat16 [2, 4, 2048, 6144], P('pipe', None, 'dp', 'tensor')
- new_factor: float32 [2, 8, 48, 128, 128], P('pipe', 'tensor', 'dp')
The draws below stay inside these ranges and needn't reach their ends.
Inputs may be any that keep to these rules, and one draw needn't show every extreme that they name: `slot_table`: each of the 21 block numbers stands in exactly one slot, every other slot holds -1; slots k * 3 to (k + 1) * 3 - 1 belong to owner k, and some owner has all 3 slots used. `capture`: every section captures on at least one micro-batch.
All inputs are finite; a program needn't handle non-finite values.
Results may differ from the reference program's by a relative error of at most 0.007.
Values may be sent and summed in bfloat16 or wider, within the bound.
No kernel may reach another device: no remote copies, remote signals or barrier semaphores. Data moves between devices by JAX's collectives and lax.ppermute only.
A program may use at most 128 MiB of HBM per device.

```python
import math
import jax
import jax.numpy as jnp
import numpy as np
from jax import lax

D = 6144
BLK = 128
MB = 4
SECTIONS = 2
TOKENS = 2048
NU = 21
CAP = 3
SLOTS = 48
N_TENSOR = 8


def draw_section_input(key, part):
    key = jax.random.fold_in(key, 5)
    key_value, key_scale = jax.random.split(key)
    feature = jnp.arange(D, dtype=jnp.float32) / (D - 1)
    scales = jnp.exp(jax.random.uniform(key_scale, (MB, 1, D), minval=0.0, maxval=math.log(10.0)))
    values = jnp.clip(jax.random.normal(key_value, (MB, TOKENS, D)), -4.0, 4.0)
    trend = jnp.sqrt(1.0 + 3.0 * feature)
    return (values * scales * trend).astype(jnp.bfloat16)


def draw_slot_table(key, part):
    key = jax.random.fold_in(key, 11)
    key_owner, key_score, key_perm = jax.random.split(key, 3)
    full_owner = jax.random.randint(key_owner, (), 0, SLOTS // CAP)
    positions = jnp.arange(SLOTS, dtype=jnp.int32)
    scores = jax.random.randint(key_score, (SLOTS,), 0, 1 << 20) * SLOTS + positions
    scores = jnp.where(positions // CAP == full_owner, scores + (1 << 30), scores)
    ordering = jnp.argsort(-scores, stable=True)
    blocks = jax.random.permutation(key_perm, NU).astype(jnp.int32)
    table = jnp.full((SLOTS,), -1, jnp.int32)
    return table.at[ordering[:NU]].set(blocks)


def draw_capture(key, part):
    key = jax.random.fold_in(key, 17)
    key_bits, key_pos = jax.random.split(key)
    bits = jax.random.randint(key_bits, (SECTIONS, MB), 0, 2)
    forced = jax.random.randint(key_pos, (SECTIONS, 1), 0, MB)
    chosen = (jnp.arange(MB, dtype=jnp.int32)[None, :] == forced).astype(jnp.int32)
    return jnp.maximum(bits, chosen).astype(jnp.int32)


def levels(stream_key, extent, cuts, smallest, largest):
    level, own = 1.0, jax.random.fold_in(stream_key, 6)
    for dim, parts in cuts:
        steps = jnp.exp(jax.random.uniform(jax.random.fold_in(own, dim), (parts,), jnp.float32, smallest / len(cuts), largest / len(cuts)))
        level = level * jnp.repeat(steps, extent[dim] // parts).reshape([-1 if axis == dim else 1 for axis in range(len(extent))])
    return level


def bell_draw(rng, shape, deviation, reach, pieces=(), kind=jnp.bfloat16):
    level = levels(rng, shape, pieces, -0.22, 0.18) if pieces else 1.0
    values = jax.random.normal(rng, shape, jnp.float32) * deviation * level
    return jnp.minimum(jnp.maximum(values, -reach), reach).astype(kind)


def setup_inputs(seed: int = 0) -> dict:
    key_of = jax.random.split(jax.random.key(seed), 7)
    section_input = draw_section_input(jax.random.fold_in(key_of[6], 71), 0)
    gain = jnp.clip(1.0 + 0.1 * jax.random.normal(key_of[1], (SECTIONS, D), jnp.float32), 0.5, 1.5)
    weight = bell_draw(key_of[2], (SECTIONS, D, D), D ** -0.5, 0.078125, ((0, 2), (1, 8)))
    old_factor = bell_draw(key_of[3], (SECTIONS, N_TENSOR, SLOTS, BLK, BLK), 0.015, 0.09, ((0, 2), (1, 8), (2, 16)), jnp.float32)
    slot_table = draw_slot_table(jax.random.fold_in(key_of[6], 71), 0)
    capture = draw_capture(jax.random.fold_in(key_of[6], 71), 0)
    return {"section_input": section_input, "gain": gain, "weight": weight, "old_factor": old_factor, "slot_table": slot_table, "capture": capture}


epsilon = 1e-06
factor_decay = 0.9

def upper_blocks(block_count):
    return np.array([row * block_count + col for row in range(block_count) for col in range(row, block_count)], dtype=np.int32)

def reference(section_input, gain, weight, old_factor, slot_table, capture):
    shard_width = D // N_TENSOR
    block_count = shard_width // BLK
    flat_table = jnp.asarray(upper_blocks(block_count))
    slot_live = (slot_table >= 0)[:, None, None]
    flat_slot = flat_table[jnp.clip(slot_table, 0, NU - 1)]
    current = section_input
    outputs = []
    factors = []
    for section_id in range(SECTIONS):
        widened = current.astype(jnp.float32)
        mean_square = lax.optimization_barrier(jnp.mean(widened * widened, axis=-1, keepdims=True))
        normed = (widened * lax.rsqrt(mean_square + epsilon) * gain[section_id]).astype(jnp.bfloat16)
        captured = capture[section_id].astype(jnp.float32)
        weighting = captured / (jnp.sum(captured) * TOKENS)
        total = widened
        shard_factors = []
        for shard in range(N_TENSOR):
            lower = shard * shard_width
            columns = normed[:, :, lower:lower + shard_width].astype(jnp.float32)
            rows = weight[section_id, lower:lower + shard_width, :].astype(jnp.float32)
            partial_value = jnp.einsum('mtf,fo->mto', columns, rows, precision=lax.Precision.HIGHEST)
            partial_value = lax.optimization_barrier(partial_value.astype(jnp.bfloat16)).astype(jnp.float32)
            total = total + partial_value
            gram = jnp.einsum('m,mtf,mtg->fg', weighting, columns, columns, precision=lax.Precision.HIGHEST)
            tiled = gram.reshape(block_count, BLK, block_count, BLK).transpose(0, 2, 1, 3).reshape(block_count * block_count, BLK, BLK)
            picked = jnp.where(slot_live, tiled[flat_slot], jnp.float32(0.0))
            updated = factor_decay * old_factor[section_id, shard] + (1.0 - factor_decay) * picked
            shard_factors.append(jnp.where(slot_live, updated, jnp.float32(0.0)))
        current = total.astype(jnp.bfloat16)
        outputs.append(current)
        factors.append(jnp.stack(shard_factors))
    return (jnp.stack(outputs), jnp.stack(factors))
```

```python
import jax
import jax.numpy as jnp
from jax import lax
from jax.experimental import pallas as pl
from jax.experimental.pallas import tpu as pltpu
from jax.sharding import PartitionSpec as P

EPS = 1e-06
DECAY = 0.9
BF = jnp.bfloat16
F32 = jnp.float32
NX, NYL, NZ, NYH = 4, 2, 8, 2
NT = NX * NYL
NDP = NZ * NYH
ROWS_A = 224
VMEM = 32 * 1024 * 1024


def tensor_perm(value, pipes, to):
    pairs = [(p * NT + t, p * NT + to(t)) for p in pipes for t in range(NT)]
    return lax.ppermute(value, ("pipe", "tensor"), pairs)


def x_by(k):
    return lambda t: (t // NX) * NX + (t % NX + k) % NX


def y_other(t):
    return t ^ NX


def core_perm(value, source):
    return lax.ppermute(value, "pipe", [(source, 1 - source)])


def dp_perm(value, pipe, pipe_to, to):
    pairs = [(d * 2 + pipe, to(d) * 2 + pipe_to) for d in range(NDP)]
    return lax.ppermute(value, ("dp", "pipe"), pairs)


def z_by(k):
    return lambda d: ((d // NYH + k) % NZ) * NYH + d % NYH


def project(rows, weight, ids, plan, shapes):
    count, (total, width) = len(plan), rows.shape
    half = total // 2

    def kernel(ids_ref, x_ref, w_ref, *outs):
        del ids_ref
        step = pl.program_id(0)
        y = jnp.dot(x_ref[...], w_ref[...], preferred_element_type=F32).astype(BF)
        for i, places in enumerate(plan):

            @pl.when(step == i)
            def _(places=places):
                for h, (o, at) in enumerate(places):
                    outs[o][at] = y[h * half : (h + 1) * half]

    out_shapes = [jax.ShapeDtypeStruct((n, half, width), BF) for n in shapes]
    return pl.pallas_call(
        kernel,
        grid_spec=pltpu.PrefetchScalarGridSpec(
            num_scalar_prefetch=1,
            grid=(count,),
            in_specs=[
                pl.BlockSpec((total, width), lambda i, ids: (0, 0)),
                pl.BlockSpec((width, width), lambda i, ids: (0, ids[i])),
            ],
            out_specs=[pl.BlockSpec(s.shape, lambda i, ids: (0, 0, 0)) for s in out_shapes],
        ),
        out_shape=out_shapes,
        compiler_params=pltpu.CompilerParams(
            dimension_semantics=("arbitrary",), vmem_limit_bytes=VMEM
        ),
        cost_estimate=pl.CostEstimate(
            flops=2 * total * width * width * count,
            bytes_accessed=2 * count * width * (width + total),
            transcendentals=0,
        ),
    )(ids, rows, weight)


def f32(v):
    return v.astype(F32)


def ring_reduce(pipe, first_p, first_m, next_p, next_m, own0, own1):
    n = first_p.shape[0] // 2
    got_p = tensor_perm(first_p, (pipe,), x_by(1))
    got_m = tensor_perm(first_m, (pipe,), x_by(-1))
    second_p = (f32(next_p) + f32(got_p[:n])).astype(BF)
    second_m = (f32(next_m) + f32(got_m[:n])).astype(BF)
    last_p = tensor_perm(second_p, (pipe,), x_by(1))
    last_m = tensor_perm(second_m, (pipe,), x_by(-1))
    h0 = f32(own0) + f32(got_m[n:]) + f32(last_p)
    h1 = f32(own1) + f32(got_p[n:]) + f32(last_m)
    return h0, h1


def reduce_projection(pipe, rows_a, rows_b, weight, t):
    yl, x = t // NX, t % NX
    ring = [(x + 2) % NX, (x + 1) % NX, (x + 3) % NX, x]
    mine = [yl * NX + r for r in ring]
    other = [(1 - yl) * NX + r for r in ring]
    width = rows_a.shape[1]
    plan_a = [((0, 0), (1, 0)), ((2, 0), (0, 1)), ((1, 1), (3, 0)), ((4, 0), (4, 1))]
    flat = [0, 2, 4, 5, 6]
    plan_y = [tuple((0, flat[o] + at) for o, at in places) for places in plan_a]
    (sent_y,) = project(rows_a, weight, jnp.stack(other), plan_y, [8])
    got_y = tensor_perm(sent_y, (pipe,), y_other)
    ids_b = [c for pair in zip(mine, other) for c in pair]
    plan_b = []
    for places in plan_a:
        for which in range(2):
            plan_b.append(tuple((o, 2 * at + which) for o, at in places))
    b_fp, b_fm, b_np, b_nm, b_own = project(
        rows_b, weight, jnp.stack(ids_b), plan_b, [4, 4, 2, 2, 4]
    )
    b0, b1 = ring_reduce(pipe, b_fp, b_fm, b_np, b_nm, b_own[:2], b_own[2:])
    a_fp, a_fm, a_np, a_nm, a_own = project(
        rows_a, weight, jnp.stack(mine), plan_a, [2, 2, 1, 1, 2]
    )
    add = lambda own, at: f32(own) + f32(got_y[at : at + own.shape[0]])
    a0, a1 = ring_reduce(
        pipe,
        add(a_fp, 0).astype(BF),
        add(a_fm, 2).astype(BF),
        add(a_np, 4),
        add(a_nm, 5),
        add(a_own[:1], 6),
        add(a_own[1:], 7),
    )
    away = jnp.concatenate([b0[1], b1[1]], axis=0).astype(BF)
    got_b = tensor_perm(away, (pipe,), y_other)
    sum_b = jnp.concatenate([b0[0], b1[0]], axis=0) + f32(got_b)
    sum_a = jnp.concatenate([a0[0], a1[0]], axis=0)
    return sum_a.reshape(-1, width), sum_b


def square_sum(rows, pipes):
    wide = f32(rows)
    total = jnp.sum(wide * wide, axis=-1).reshape(-1, 128)
    total = total + tensor_perm(total, pipes, y_other)
    total = total + tensor_perm(total, pipes, lambda t: t ^ 1)
    total = total + tensor_perm(total, pipes, lambda t: t ^ 2)
    return total


def gram_parts(normed, captured, z, blocks, block, total_tokens):
    micro = captured.shape[0]
    rows, width = normed.shape
    each = rows // micro
    sub = block // NZ
    count = blocks * (blocks + 1) // 2

    def kernel(cap_ref, z_ref, n_ref, *rest):
        outs, left, grams = rest[:NZ], rest[NZ], rest[NZ + 1]
        live = cap_ref[0]
        for m in range(1, micro):
            live = live + cap_ref[m]
        for m in range(micro):
            part = pl.ds(m * each, each)
            left[part] = (f32(n_ref[part]) * cap_ref[m]).astype(BF)
        scale = 1.0 / jnp.full((1, 1), live * total_tokens, F32)
        b = 0
        for i in range(blocks):
            g = lax.dot_general(
                left[:, i * block : (i + 1) * block],
                n_ref[:, i * block :],
                (((0,), (0,)), ((), ())),
                preferred_element_type=F32,
            )
            g = g * scale
            for j in range(blocks - i):
                grams[b] = g[:, j * block : (j + 1) * block]
                b += 1
        for k in range(NZ):
            at = pl.multiple_of(lax.rem(z_ref[0] + k, NZ) * sub, sub)
            outs[k][...] = grams[:, pl.ds(at, sub), :].astype(BF)

    smem = pl.BlockSpec(memory_space=pltpu.SMEM)
    vmem = pl.BlockSpec(memory_space=pltpu.VMEM)
    return pl.pallas_call(
        kernel,
        in_specs=[smem, smem, vmem],
        out_specs=[vmem] * NZ,
        out_shape=[jax.ShapeDtypeStruct((count, sub, block), BF)] * NZ,
        scratch_shapes=[
            pltpu.VMEM((rows, width), BF),
            pltpu.VMEM((count, block, block), F32),
        ],
        compiler_params=pltpu.CompilerParams(vmem_limit_bytes=VMEM),
        cost_estimate=pl.CostEstimate(
            flops=rows * width * width, bytes_accessed=2 * rows * width, transcendentals=0
        ),
    )(captured, z[None], normed)


def pick_slots(near, far, ids, capacity):
    _, sub, block = near.shape

    def kernel(ids_ref, near_ref, far_ref, *outs):
        for k in range(NZ):
            for i in range(capacity):
                at = ids_ref[k * capacity + i]
                outs[k][i] = (f32(near_ref[at]) + f32(far_ref[at])).astype(BF)

    smem = pl.BlockSpec(memory_space=pltpu.SMEM)
    vmem = pl.BlockSpec(memory_space=pltpu.VMEM)
    return pl.pallas_call(
        kernel,
        in_specs=[smem, vmem, vmem],
        out_specs=[vmem] * NZ,
        out_shape=[jax.ShapeDtypeStruct((capacity, sub, block), BF)] * NZ,
        compiler_params=pltpu.CompilerParams(vmem_limit_bytes=VMEM),
    )(ids, near, far)


def update_factor(old, live, z, parts0, parts1):
    capacity, block, _ = old.shape
    sub = block // NZ

    def kernel(live_ref, z_ref, old_ref, *rest):
        first, second, out = rest[:NZ], rest[NZ : 2 * NZ], rest[2 * NZ]
        for k in range(NZ):
            at = pl.multiple_of(lax.rem(z_ref[0] + NZ - k, NZ) * sub, sub)
            for i in range(capacity):
                got = f32(first[k][i]) + f32(second[k][i])
                new = DECAY * old_ref[i, pl.ds(at, sub), :] + (1.0 - DECAY) * got
                out[i, pl.ds(at, sub), :] = jnp.where(live_ref[i] > 0, new, 0.0)

    smem = pl.BlockSpec(memory_space=pltpu.SMEM)
    vmem = pl.BlockSpec(memory_space=pltpu.VMEM)
    return pl.pallas_call(
        kernel,
        in_specs=[smem, smem] + [vmem] * (1 + 2 * NZ),
        out_specs=vmem,
        out_shape=jax.ShapeDtypeStruct(old.shape, F32),
        compiler_params=pltpu.CompilerParams(vmem_limit_bytes=VMEM),
    )(live, z[None], old, *parts0, *parts1)


def factor_parts(pipe, rows, squares, gain, captured, slot_table, capacity, block):
    d = lax.axis_index("dp")
    z, yh = d // NYH, d % NYH
    width = rows.shape[1]
    full = width * NT
    scale = lax.rsqrt(squares / full + EPS).reshape(-1, 1)
    normed = (f32(rows) * scale * gain).astype(BF)
    tokens = rows.shape[0] // captured.shape[0] * NDP
    parts = gram_parts(normed, captured, z, width // block, block, float(tokens))
    total = f32(parts[0])
    for k in range(1, NZ):
        total = total + f32(dp_perm(parts[k], pipe, pipe, z_by(k)))
    near = total.astype(BF)
    far = dp_perm(near, pipe, pipe, lambda v: v ^ 1)
    table = jnp.maximum(slot_table, 0).reshape(NZ, NYH, capacity)
    table = lax.dynamic_index_in_dim(table, yh, 1, keepdims=False)
    ids = jnp.roll(table, -z, axis=0).reshape(-1)
    picked = pick_slots(near, far, ids, capacity)
    return [dp_perm(picked[k], pipe, 1 - pipe, z_by(k)) for k in range(NZ)]


def local(section_input, gain, weight, old_factor, slot_table, capture):
    pipe = lax.axis_index("pipe")
    t = lax.axis_index("tensor")
    d = lax.axis_index("dp")
    micro, each, width = section_input.shape
    w = weight[0]
    old = old_factor[0, 0]
    capacity, block, _ = old.shape
    x0 = section_input.reshape(micro * each, width)
    full = width * NT

    params = jnp.concatenate([gain[0], capture[0].astype(F32)])
    params = lax.ppermute(params, "pipe", [(0, 1), (1, 0)])
    gain_other, cap_other = params[:width], params[width:]

    def scaled(rows):
        return (f32(rows) * gain[0]).astype(BF)

    def finish(rows, squares, total):
        return (f32(rows) + total * lax.rsqrt(squares / full + EPS)[:, None]).astype(BF)

    squares0 = square_sum(x0, (0, 1))
    sum_a, sum_b = reduce_projection(0, scaled(x0[:ROWS_A]), scaled(x0[ROWS_A:]), w, t)
    flat0 = squares0.reshape(-1)
    x1a = finish(x0[:ROWS_A], flat0[:ROWS_A], sum_a)
    x1b = finish(x0[ROWS_A:], flat0[ROWS_A:], sum_b)
    parts0 = factor_parts(
        1, x0, squares0, gain_other, cap_other, slot_table, capacity, block
    )
    in_a, in_b = core_perm(x1a, 0), core_perm(x1b, 0)
    x1 = jnp.concatenate([x1a, x1b], axis=0)
    squares1 = square_sum(x1, (0,))
    in_squares = core_perm(squares1, 0).reshape(-1)
    sum_a, sum_b = reduce_projection(1, scaled(in_a), scaled(in_b), w, t)
    parts1 = factor_parts(
        0, x1, squares1, gain_other, cap_other, slot_table, capacity, block
    )
    x2 = jnp.concatenate(
        [
            finish(in_a, in_squares[:ROWS_A], sum_a),
            finish(in_b, in_squares[ROWS_A:], sum_b),
        ],
        axis=0,
    )
    out = jnp.where(pipe == 0, x1, x2).reshape(1, micro, each, width)
    own = lax.dynamic_slice_in_dim(slot_table, d * capacity, capacity)
    live = (own >= 0).astype(jnp.int32)
    new = update_factor(old, live, d // NYH, parts0, parts1)
    return (out, new[None, None])


def solution(mesh):
    placed = (
        P(None, "dp", "tensor"),
        P("pipe", "tensor"),
        P("pipe", "tensor", None),
        P("pipe", "tensor", "dp", None, None),
        P(),
        P("pipe", None),
    )
    return jax.shard_map(
        local,
        mesh=mesh,
        in_specs=placed,
        out_specs=(P("pipe", None, "dp", "tensor"), P("pipe", "tensor", "dp", None, None)),
        check_vma=False,
    )
```

```python
import jax
import jax.numpy as jnp
from jax import lax
from jax.experimental import pallas as pl
from jax.experimental.pallas import tpu as pltpu
from jax.sharding import PartitionSpec as P

EPS = 1e-06
DECAY = 0.9
BF = jnp.bfloat16
F32 = jnp.float32
NX, NYL, NZ, NYH = 4, 2, 8, 2
NT = NX * NYL
NDP = NZ * NYH
ROWS_A = 224
VMEM = 48 * 1024 * 1024


def f32(v):
    return v.astype(F32)


def tensor_perm(value, to):
    return lax.ppermute(value, "tensor", [(t, to(t)) for t in range(NT)])


def x_by(k):
    return lambda t: (t // NX) * NX + (t % NX + k) % NX


def y_other(t):
    return t ^ NX


def swap(value):
    return lax.ppermute(value, "pipe", [(0, 1), (1, 0)])


def dp_perm(value, to):
    return lax.ppermute(value, "dp", [(d, to(d)) for d in range(NDP)])


def z_by(k):
    return lambda d: ((d // NYH + k) % NZ) * NYH + d % NYH


def cut_weight(weight, columns):
    count = columns.shape[0]
    depth, width = weight.shape[0], weight.shape[1] // NT // 2

    def kernel(columns_ref, w_ref, out_ref):
        del columns_ref
        out_ref[0] = w_ref[...]

    return pl.pallas_call(
        kernel,
        grid_spec=pltpu.PrefetchScalarGridSpec(
            num_scalar_prefetch=1,
            grid=(count,),
            in_specs=[pl.BlockSpec((depth, width), lambda i, c: (0, c[i]))],
            out_specs=pl.BlockSpec((1, depth, width), lambda i, c: (i, 0, 0)),
        ),
        out_shape=jax.ShapeDtypeStruct((count, depth, width), weight.dtype),
        compiler_params=pltpu.CompilerParams(
            dimension_semantics=("arbitrary",), vmem_limit_bytes=VMEM
        ),
        cost_estimate=pl.CostEstimate(
            flops=0, bytes_accessed=4 * count * depth * width, transcendentals=0
        ),
    )(columns, weight)


def project(rows, weight, got, own, columns, plan, shapes):
    count, (total, depth) = len(plan), rows.shape
    width = got[0].shape[2]
    half, many = total // 2, len(got)
    own = own.astype(jnp.int32)
    table = jnp.concatenate(
        [
            own[None],
            jnp.where(own > 0, columns, columns[0]),
            jnp.where(own > 0, 0, jnp.arange(count, dtype=jnp.int32) // many),
        ]
    )

    def kernel(table_ref, x_ref, w_ref, *rest):
        got_refs, outs, y = rest[:many], rest[many:-1], rest[-1]
        step = pl.program_id(0)
        mine = table_ref[0] > 0

        @pl.when(mine)
        def _():
            y[...] = jnp.dot(x_ref[...], w_ref[...], preferred_element_type=F32).astype(BF)

        for g in range(many):

            @pl.when(jnp.logical_and(jnp.logical_not(mine), step % many == g))
            def _(g=g):
                y[...] = jnp.dot(
                    x_ref[...], got_refs[g][0], preferred_element_type=F32
                ).astype(BF)

        for i, places in enumerate(plan):

            @pl.when(step == i)
            def _(places=places):
                for h, (o, at) in enumerate(places):
                    outs[o][at] = y[h * half : (h + 1) * half]

    out_shapes = [jax.ShapeDtypeStruct((n, half, width), BF) for n in shapes]
    return pl.pallas_call(
        kernel,
        grid_spec=pltpu.PrefetchScalarGridSpec(
            num_scalar_prefetch=1,
            grid=(count,),
            in_specs=[
                pl.BlockSpec((total, depth), lambda i, t: (0, 0)),
                pl.BlockSpec((depth, width), lambda i, t: (0, t[1 + i])),
            ]
            + [
                pl.BlockSpec((1, depth, width), lambda i, t: (t[1 + count + i], 0, 0))
                for _ in got
            ],
            out_specs=[pl.BlockSpec(s.shape, lambda i, t: (0, 0, 0)) for s in out_shapes],
            scratch_shapes=[pltpu.VMEM((total, width), BF)],
        ),
        out_shape=out_shapes,
        compiler_params=pltpu.CompilerParams(
            dimension_semantics=("arbitrary",), vmem_limit_bytes=VMEM
        ),
        cost_estimate=pl.CostEstimate(
            flops=2 * total * depth * width * count,
            bytes_accessed=2 * count * width * (depth + total),
            transcendentals=0,
        ),
    )(table, rows, weight, *got)


def ring_reduce(first_p, first_m, next_p, next_m, own0, own1):
    n = first_p.shape[0] // 2
    got_p = tensor_perm(first_p, x_by(1))
    got_m = tensor_perm(first_m, x_by(-1))
    last_p = tensor_perm((f32(next_p) + f32(got_p[:n])).astype(BF), x_by(1))
    last_m = tensor_perm((f32(next_m) + f32(got_m[:n])).astype(BF), x_by(-1))
    h0 = f32(own0) + f32(got_m[n:]) + f32(last_p)
    h1 = f32(own1) + f32(got_p[n:]) + f32(last_m)
    return h0, h1


def reduce_projection(rows_a, rows_b, weight, got_other, got_mine, own, t, pipe):
    yl, x = t // NX, t % NX
    ring = jnp.stack([(x + 2) % NX, (x + 1) % NX, (x + 3) % NX, x])
    mine = 2 * (yl * NX + ring) + pipe
    other = 2 * ((1 - yl) * NX + ring) + pipe
    width = got_mine.shape[2]
    plan_a = [((0, 0), (1, 0)), ((2, 0), (0, 1)), ((1, 1), (3, 0)), ((4, 0), (4, 1))]
    flat = [0, 2, 4, 5, 6]
    plan_y = [tuple((0, flat[o] + at) for o, at in places) for places in plan_a]
    (sent_y,) = project(rows_a, weight, [got_other], own, other, plan_y, [8])
    got_y = tensor_perm(sent_y, y_other)
    plan_b = [
        tuple((o, 2 * at + which) for o, at in places)
        for places in plan_a
        for which in range(2)
    ]
    both = jnp.stack([mine, other], axis=1).reshape(-1)
    b_fp, b_fm, b_np, b_nm, b_own = project(
        rows_b, weight, [got_mine, got_other], own, both, plan_b, [4, 4, 2, 2, 4]
    )
    b0, b1 = ring_reduce(b_fp, b_fm, b_np, b_nm, b_own[:2], b_own[2:])
    a_fp, a_fm, a_np, a_nm, a_own = project(
        rows_a, weight, [got_mine], own, mine, plan_a, [2, 2, 1, 1, 2]
    )
    add = lambda part, at: f32(part) + f32(got_y[at : at + part.shape[0]])
    a0, a1 = ring_reduce(
        add(a_fp, 0).astype(BF),
        add(a_fm, 2).astype(BF),
        add(a_np, 4),
        add(a_nm, 5),
        add(a_own[:1], 6),
        add(a_own[1:], 7),
    )
    away = jnp.concatenate([b0[1], b1[1]], axis=0).astype(BF)
    got_b = tensor_perm(away, y_other)
    sum_b = jnp.concatenate([b0[0], b1[0]], axis=0) + f32(got_b)
    sum_a = jnp.concatenate([a0[0], a1[0]], axis=0)
    return sum_a.reshape(-1, width), sum_b


def square_sum(rows):
    wide = f32(rows)
    total = jnp.sum(wide * wide, axis=-1).reshape(-1, 128)
    total = total + tensor_perm(total, y_other)
    total = total + tensor_perm(total, lambda t: t ^ 1)
    total = total + tensor_perm(total, lambda t: t ^ 2)
    return total


def gram_parts(normed, captured, ids, pipe, blocks, block, total_tokens):
    micro = captured.shape[0]
    rows, width = normed.shape
    each, sub = rows // micro, block // 2
    count = blocks * (blocks + 1) // 2
    slots = ids.shape[0] // NZ

    def kernel(cap_ref, ids_ref, pipe_ref, n_ref, *rest):
        outs, left, grams = rest[:NZ], rest[NZ], rest[NZ + 1]
        live = cap_ref[0]
        for m in range(1, micro):
            live = live + cap_ref[m]
        for m in range(micro):
            part = pl.ds(m * each, each)
            left[part] = (f32(n_ref[part]) * cap_ref[m]).astype(BF)
        scale = 1.0 / jnp.full((1, 1), live * total_tokens, F32)
        b = 0
        for i in range(blocks):
            g = lax.dot_general(
                left[:, i * block : (i + 1) * block],
                n_ref[:, i * block :],
                (((0,), (0,)), ((), ())),
                preferred_element_type=F32,
            )
            g = g * scale
            for j in range(blocks - i):
                grams[b] = g[:, j * block : (j + 1) * block]
                b += 1
        at = pl.ds(pl.multiple_of(pipe_ref[0] * sub, sub), sub)
        for k in range(NZ):
            for i in range(slots):
                outs[k][i] = grams[ids_ref[k * slots + i], at, :].astype(BF)

    smem = pl.BlockSpec(memory_space=pltpu.SMEM)
    vmem = pl.BlockSpec(memory_space=pltpu.VMEM)
    return pl.pallas_call(
        kernel,
        in_specs=[smem, smem, smem, vmem],
        out_specs=[vmem] * NZ,
        out_shape=[jax.ShapeDtypeStruct((slots, sub, block), BF)] * NZ,
        scratch_shapes=[
            pltpu.VMEM((rows, width), BF),
            pltpu.VMEM((count, block, block), F32),
        ],
        compiler_params=pltpu.CompilerParams(vmem_limit_bytes=VMEM),
        cost_estimate=pl.CostEstimate(
            flops=rows * width * width, bytes_accessed=4 * rows * width, transcendentals=0
        ),
    )(captured, ids, pipe[None], normed)


def factor_rows(rows, squares, gain, captured, ids, pipe, capacity, block):
    width = rows.shape[1]
    scale = lax.rsqrt(squares / (width * NT) + EPS).reshape(-1, 1)
    normed = (f32(rows) * scale * gain).astype(BF)
    tokens = rows.shape[0] // captured.shape[0] * NDP
    parts = gram_parts(normed, captured, ids, pipe, width // block, block, float(tokens))
    total = f32(parts[0])
    for k in range(1, NZ):
        total = total + f32(dp_perm(parts[k], z_by(k)))
    far = dp_perm(total[capacity:].astype(BF), lambda v: v ^ 1)
    return total[:capacity] + f32(far)


def local(section_input, gain, weight, old_factor, slot_table, capture):
    pipe = lax.axis_index("pipe")
    t = lax.axis_index("tensor")
    d = lax.axis_index("dp")
    z, yh = d // NYH, d % NYH
    yl, x = t // NX, t % NX
    first = pipe == 0
    micro, each, width = section_input.shape
    half = width // 2
    w = weight[0]
    old = old_factor[0, 0]
    capacity, block, _ = old.shape
    x0 = section_input.reshape(micro * each, width)

    def pick(a, b):
        return jnp.where(first, a, b)

    ring = jnp.stack([(x + 2) % NX, (x + 1) % NX, (x + 3) % NX, x])
    got_other = swap(cut_weight(w, 2 * ((1 - yl) * NX + ring) + 1 - pipe))
    got_mine = swap(cut_weight(w, 2 * (yl * NX + ring) + 1 - pipe))
    params = jnp.concatenate([gain[0], capture[0].astype(F32)])
    away = swap(params)
    params = (pick(params, away), pick(away, params))
    gains = [v[:width] for v in params]
    caps = [v[width:] for v in params]
    table = jnp.maximum(slot_table, 0).reshape(NZ, NYH, capacity)
    table = jnp.where(yh == 0, table, table[:, ::-1])
    ids = jnp.roll(table, -z, axis=0).reshape(-1)

    def section(s, rows_a, rows_b):
        scaled = lambda rows: (f32(rows) * gains[s]).astype(BF)
        return reduce_projection(
            scaled(rows_a), scaled(rows_b), w, got_other, got_mine, pipe == s, t, pipe
        )

    def finish(rows, squares, total):
        part = lax.dynamic_slice_in_dim(rows, pipe * half, half, 1)
        scale = lax.rsqrt(squares / (width * NT) + EPS)[:, None]
        part = (f32(part) + total * scale).astype(BF)
        other = swap(part)
        return jnp.concatenate([pick(part, other), pick(other, part)], axis=1)

    squares0 = square_sum(x0)
    flat0 = squares0.reshape(-1)
    sum_a, sum_b = section(0, x0[:ROWS_A], x0[ROWS_A:])
    own0 = factor_rows(x0, squares0, gains[0], caps[0], ids, pipe, capacity, block)
    x1a = finish(x0[:ROWS_A], flat0[:ROWS_A], sum_a)
    x1b = finish(x0[ROWS_A:], flat0[ROWS_A:], sum_b)
    x1 = jnp.concatenate([x1a, x1b], axis=0)
    squares1 = square_sum(x1)
    flat1 = squares1.reshape(-1)
    sum_a, sum_b = section(1, x1a, x1b)
    own1 = factor_rows(x1, squares1, gains[1], caps[1], ids, pipe, capacity, block)
    x2 = finish(x1, flat1, jnp.concatenate([sum_a, sum_b], axis=0))
    out = pick(x1, x2).reshape(1, micro, each, width)
    kept = pick(own0, own1)
    got = swap(pick(own1, own0))
    blocks = jnp.concatenate([pick(kept, got), pick(got, kept)], axis=1)
    own = lax.dynamic_slice_in_dim(slot_table, d * capacity, capacity)
    new = jnp.where(
        (own >= 0)[:, None, None], DECAY * old + (1.0 - DECAY) * blocks, jnp.float32(0.0)
    )
    return (out, new[None, None])


def solution(mesh):
    placed = (
        P(None, "dp", "tensor"),
        P("pipe", "tensor"),
        P("pipe", "tensor", None),
        P("pipe", "tensor", "dp", None, None),
        P(),
        P("pipe", None),
    )
    return jax.shard_map(
        local,
        mesh=mesh,
        in_specs=placed,
        out_specs=(P("pipe", None, "dp", "tensor"), P("pipe", "tensor", "dp", None, None)),
        check_vma=False,
    )
```

```python
import jax
import jax.numpy as jnp
from jax import lax
from jax.experimental import pallas as pl
from jax.experimental.pallas import tpu as pltpu
from jax.sharding import PartitionSpec as P

EPS = 1e-06
DECAY = 0.9
BF = jnp.bfloat16
F32 = jnp.float32
NX, NYL, NZ, NYH = 4, 2, 8, 2
NT = NX * NYL
NDP = NZ * NYH
ROWS_A = 224
VMEM = 48 * 1024 * 1024


def f32(v):
    return v.astype(F32)


def tensor_perm(value, to):
    return lax.ppermute(value, "tensor", [(t, to(t)) for t in range(NT)])


def x_by(k):
    return lambda t: (t // NX) * NX + (t % NX + k) % NX


def y_other(t):
    return t ^ NX


def swap(value):
    return lax.ppermute(value, "pipe", [(0, 1), (1, 0)])


def z_perm(value, k):
    return lax.ppermute(value, "z", [(d, (d + k) % NZ) for d in range(NZ)])


def y_far(value):
    return lax.ppermute(value, "yh", [(0, 1), (1, 0)])


def y_far_swap(value):
    return lax.ppermute(value, ("yh", "pipe"), [(0, 3), (1, 2), (2, 1), (3, 0)])


def cut_weight(weight, columns):
    count = columns.shape[0]
    depth, width = weight.shape[0], weight.shape[1] // NT // 2

    def kernel(columns_ref, w_ref, out_ref, sems):
        copies = []
        for i in range(count):
            at = pl.multiple_of(columns_ref[i] * width, width)
            copies.append(
                pltpu.make_async_copy(w_ref.at[:, pl.ds(at, width)], out_ref.at[i], sems.at[i])
            )
        for copy in copies:
            copy.start()
        for copy in copies:
            copy.wait()

    return pl.pallas_call(
        kernel,
        in_specs=[pl.BlockSpec(memory_space=pltpu.SMEM), pl.BlockSpec(memory_space=pl.ANY)],
        out_specs=pl.BlockSpec(memory_space=pl.ANY),
        out_shape=jax.ShapeDtypeStruct((count, depth, width), weight.dtype),
        scratch_shapes=[pltpu.SemaphoreType.DMA((count,))],
        compiler_params=pltpu.CompilerParams(vmem_limit_bytes=VMEM),
        cost_estimate=pl.CostEstimate(
            flops=0, bytes_accessed=4 * count * depth * width, transcendentals=0
        ),
    )(columns, weight)


def project(rows, weight, got, own, columns, plan, shapes):
    count, (total, depth) = len(plan), rows.shape
    width = got[0].shape[2]
    half, many, n_out = total // 2, len(got), len(shapes)
    table = jnp.concatenate([own.astype(jnp.int32)[None], columns])

    def kernel(table_ref, x_ref, w_ref, *rest):
        got_refs, outs = rest[:many], rest[many : many + n_out]
        blocks, sems = rest[many + n_out :]
        mine = table_ref[0] > 0

        @pl.when(mine)
        def _():
            for i in range(count):
                at = pl.multiple_of(table_ref[1 + i] * width, width)
                pltpu.make_async_copy(
                    w_ref.at[:, pl.ds(at, width)], blocks.at[i], sems.at[i]
                ).start()

        @pl.when(jnp.logical_not(mine))
        def _():
            for i in range(count):
                pltpu.make_async_copy(
                    got_refs[i % many].at[i // many], blocks.at[i], sems.at[i]
                ).start()

        for i, places in enumerate(plan):
            pltpu.make_async_copy(got_refs[0].at[0], blocks.at[i], sems.at[i]).wait()
            y = jnp.dot(x_ref[...], blocks[i], preferred_element_type=F32).astype(BF)
            for h, (o, at) in enumerate(places):
                outs[o][at] = y[h * half : (h + 1) * half]

    out_shapes = [jax.ShapeDtypeStruct((n, half, width), BF) for n in shapes]
    vmem = pl.BlockSpec(memory_space=pltpu.VMEM)
    anywhere = pl.BlockSpec(memory_space=pl.ANY)
    return pl.pallas_call(
        kernel,
        in_specs=[pl.BlockSpec(memory_space=pltpu.SMEM), vmem, anywhere] + [anywhere] * many,
        out_specs=[vmem] * n_out,
        out_shape=out_shapes,
        scratch_shapes=[
            pltpu.VMEM((count, depth, width), BF),
            pltpu.SemaphoreType.DMA((count,)),
        ],
        compiler_params=pltpu.CompilerParams(vmem_limit_bytes=VMEM),
        cost_estimate=pl.CostEstimate(
            flops=2 * total * depth * width * count,
            bytes_accessed=2 * count * width * (depth + total),
            transcendentals=0,
        ),
    )(table, rows, weight, *got)


def ring_reduce(first_p, first_m, next_p, next_m, own0, own1):
    n = first_p.shape[0] // 2
    got_p = tensor_perm(first_p, x_by(1))
    got_m = tensor_perm(first_m, x_by(-1))
    last_p = tensor_perm((f32(next_p) + f32(got_p[:n])).astype(BF), x_by(1))
    last_m = tensor_perm((f32(next_m) + f32(got_m[:n])).astype(BF), x_by(-1))
    h0 = f32(own0) + f32(got_m[n:]) + f32(last_p)
    h1 = f32(own1) + f32(got_p[n:]) + f32(last_m)
    return h0, h1


def reduce_projection(rows_a, rows_b, weight, got_other, got_mine, own, t, pipe):
    yl, x = t // NX, t % NX
    ring = jnp.stack([(x + 2) % NX, (x + 1) % NX, (x + 3) % NX, x])
    mine = 2 * (yl * NX + ring) + pipe
    other = 2 * ((1 - yl) * NX + ring) + pipe
    width = got_mine.shape[2]
    plan_a = [((0, 0), (1, 0)), ((2, 0), (0, 1)), ((1, 1), (3, 0)), ((4, 0), (4, 1))]
    flat = [0, 2, 4, 5, 6]
    plan_y = [tuple((0, flat[o] + at) for o, at in places) for places in plan_a]
    (sent_y,) = project(rows_a, weight, [got_other], own, other, plan_y, [8])
    got_y = tensor_perm(sent_y, y_other)
    rows_b, sent_y = lax.optimization_barrier((rows_b, sent_y))
    plan_b = [
        tuple((o, 2 * at + which) for o, at in places)
        for places in plan_a
        for which in range(2)
    ]
    both = jnp.stack([mine, other], axis=1).reshape(-1)
    b_fp, b_fm, b_np, b_nm, b_own = project(
        rows_b, weight, [got_mine, got_other], own, both, plan_b, [4, 4, 2, 2, 4]
    )
    b0, b1 = ring_reduce(b_fp, b_fm, b_np, b_nm, b_own[:2], b_own[2:])
    a_fp, a_fm, a_np, a_nm, a_own = project(
        rows_a, weight, [got_mine], own, mine, plan_a, [2, 2, 1, 1, 2]
    )
    add = lambda part, at: f32(part) + f32(got_y[at : at + part.shape[0]])
    a0, a1 = ring_reduce(
        add(a_fp, 0).astype(BF),
        add(a_fm, 2).astype(BF),
        add(a_np, 4),
        add(a_nm, 5),
        add(a_own[:1], 6),
        add(a_own[1:], 7),
    )
    away = jnp.concatenate([b0[1], b1[1]], axis=0).astype(BF)
    got_b = tensor_perm(away, y_other)
    sum_b = jnp.concatenate([b0[0], b1[0]], axis=0) + f32(got_b)
    sum_a = jnp.concatenate([a0[0], a1[0]], axis=0)
    return sum_a.reshape(-1, width), sum_b


def square_sum(rows):
    wide = f32(rows)
    total = jnp.sum(wide * wide, axis=-1).reshape(-1, 128)
    total = total + tensor_perm(total, y_other)
    total = total + tensor_perm(total, lambda t: t ^ 1)
    total = total + tensor_perm(total, lambda t: t ^ 2)
    return total


def gram_parts(normed, captured, ids, pipe, blocks, block, total_tokens, split):
    micro = captured.shape[0]
    rows, width = normed.shape
    each, sub = rows // micro, block // 2
    count = blocks * (blocks + 1) // 2
    slots = ids.shape[0] // NZ
    n_out = NZ if split else 1

    def kernel(cap_ref, ids_ref, pipe_ref, n_ref, *rest):
        outs, left, grams = rest[:n_out], rest[n_out], rest[n_out + 1]
        live = cap_ref[0]
        for m in range(1, micro):
            live = live + cap_ref[m]
        for m in range(micro):
            part = pl.ds(m * each, each)
            left[part] = (f32(n_ref[part]) * cap_ref[m]).astype(BF)
        scale = 1.0 / jnp.full((1, 1), live * total_tokens, F32)
        b = 0
        for i in range(blocks):
            g = lax.dot_general(
                left[:, i * block : (i + 1) * block],
                n_ref[:, i * block :],
                (((0,), (0,)), ((), ())),
                preferred_element_type=F32,
            )
            g = g * scale
            for j in range(blocks - i):
                grams[b] = g[:, j * block : (j + 1) * block]
                b += 1
        at = pl.ds(pl.multiple_of(pipe_ref[0] * sub, sub), sub)
        for k in range(NZ):
            for i in range(slots):
                part = grams[ids_ref[k * slots + i], at, :].astype(BF)
                if split:
                    outs[k][i] = part
                else:
                    outs[0][k, i] = part

    smem = pl.BlockSpec(memory_space=pltpu.SMEM)
    vmem = pl.BlockSpec(memory_space=pltpu.VMEM)
    one = (slots, sub, block)
    out_shape = [jax.ShapeDtypeStruct(one if split else (NZ, *one), BF)] * n_out
    return pl.pallas_call(
        kernel,
        in_specs=[smem, smem, smem, vmem],
        out_specs=[vmem] * n_out,
        out_shape=out_shape,
        scratch_shapes=[
            pltpu.VMEM((rows, width), BF),
            pltpu.VMEM((count, block, block), F32),
        ],
        compiler_params=pltpu.CompilerParams(vmem_limit_bytes=VMEM),
        cost_estimate=pl.CostEstimate(
            flops=rows * width * width, bytes_accessed=4 * rows * width, transcendentals=0
        ),
    )(captured, ids, pipe[None], normed)


def factor_rows(rows, squares, gain, captured, table, z, pipe, block, slow):
    width = rows.shape[1]
    scale = lax.rsqrt(squares / (width * NT) + EPS).reshape(-1, 1)
    normed = (f32(rows) * scale * gain).astype(BF)
    tokens = rows.shape[0] // captured.shape[0] * NDP
    if not slow:
        table = jnp.roll(table, -z, axis=0)
    parts = gram_parts(
        normed, captured, table.reshape(-1), pipe, width // block, block, float(tokens), not slow
    )
    if slow:
        return f32(lax.psum_scatter(parts[0], "z", scatter_dimension=0, tiled=False))
    total = f32(parts[0])
    for k in range(1, NZ):
        total = total + f32(z_perm(parts[k], k))
    return total


def local(section_input, gain, weight, old_factor, slot_table, capture):
    pipe = lax.axis_index("pipe")
    t = lax.axis_index("tensor")
    z, yh = lax.axis_index("z"), lax.axis_index("yh")
    yl, x = t // NX, t % NX
    first = pipe == 0
    micro, each, width = section_input.shape
    half = width // 2
    w = weight[0]
    old = old_factor[0, 0]
    capacity, block, _ = old.shape
    x0 = section_input.reshape(micro * each, width)

    def pick(a, b):
        return jnp.where(first, a, b)

    ring = jnp.stack([(x + 2) % NX, (x + 1) % NX, (x + 3) % NX, x])
    got_other = swap(cut_weight(w, 2 * ((1 - yl) * NX + ring) + 1 - pipe))
    got_mine = swap(cut_weight(w, 2 * (yl * NX + ring) + 1 - pipe))
    params = jnp.concatenate([gain[0], capture[0].astype(F32)])
    away = swap(params)
    params = (pick(params, away), pick(away, params))
    gains = [v[:width] for v in params]
    caps = [v[width:] for v in params]
    table = jnp.maximum(slot_table, 0).reshape(NZ, NYH, capacity)
    table = jnp.where(yh == 0, table, table[:, ::-1])

    def section(s, rows_a, rows_b):
        scaled = lambda rows: (f32(rows) * gains[s]).astype(BF)
        return reduce_projection(
            scaled(rows_a), scaled(rows_b), w, got_other, got_mine, pipe == s, t, pipe
        )

    def finish(rows, squares, total):
        part = lax.dynamic_slice_in_dim(rows, pipe * half, half, 1)
        scale = lax.rsqrt(squares / (width * NT) + EPS)[:, None]
        part = (f32(part) + total * scale).astype(BF)
        other = swap(part)
        return jnp.concatenate([pick(part, other), pick(other, part)], axis=1)

    squares0 = square_sum(x0)
    flat0 = squares0.reshape(-1)
    sum_a, sum_b = section(0, x0[:ROWS_A], x0[ROWS_A:])
    tot0 = factor_rows(x0, squares0, gains[0], caps[0], table, z, pipe, block, True)
    x1a = finish(x0[:ROWS_A], flat0[:ROWS_A], sum_a)
    x1b = finish(x0[ROWS_A:], flat0[ROWS_A:], sum_b)
    x1 = jnp.concatenate([x1a, x1b], axis=0)
    squares1 = square_sum(x1)
    flat1 = squares1.reshape(-1)
    sum_a, sum_b = section(1, x1a, x1b)
    tot1 = factor_rows(x1, squares1, gains[1], caps[1], table, z, pipe, block, False)
    x2 = finish(x1, flat1, jnp.concatenate([sum_a, sum_b], axis=0))
    out = pick(x1, x2).reshape(1, micro, each, width)
    near, far = pick(tot0, tot1), pick(tot1, tot0).astype(BF)
    mine = near[:capacity] + f32(y_far(near[capacity:].astype(BF)))
    rest = f32(swap(far[:capacity])) + f32(y_far_swap(far[capacity:]))
    blocks = jnp.concatenate([pick(mine, rest), pick(rest, mine)], axis=1)
    own = lax.dynamic_slice_in_dim(slot_table, (z * NYH + yh) * capacity, capacity)
    new = jnp.where(
        (own >= 0)[:, None, None], DECAY * old + (1.0 - DECAY) * blocks, jnp.float32(0.0)
    )
    return (out, new[None, None])


def solution(mesh):
    devices = mesh.devices.reshape(NZ, NYH, 2, NT)
    fine = jax.sharding.Mesh(devices, ("z", "yh", "pipe", "tensor"))
    dp = ("z", "yh")
    placed = (
        P(None, dp, "tensor"),
        P("pipe", "tensor"),
        P("pipe", "tensor", None),
        P("pipe", "tensor", dp, None, None),
        P(),
        P("pipe", None),
    )
    return jax.shard_map(
        local,
        mesh=fine,
        in_specs=placed,
        out_specs=(P("pipe", None, dp, "tensor"), P("pipe", "tensor", dp, None, None)),
        check_vma=False,
    )
```

```python
import jax
import jax.numpy as jnp
from jax import lax
from jax.experimental import pallas as pl
from jax.experimental.pallas import tpu as pltpu
from jax.sharding import PartitionSpec as P

EPS = 1e-06
DECAY = 0.9
BF = jnp.bfloat16
F32 = jnp.float32
NX, NYL, NZ, NYH = 4, 2, 8, 2
NT = NX * NYL
NDP = NZ * NYH
ROWS_A = 224
VMEM = 48 * 1024 * 1024
SMALL = pl.CostEstimate(flops=1024, bytes_accessed=1024, transcendentals=0)


def f32(v):
    return v.astype(F32)


def tensor_perm(value, to):
    return lax.ppermute(value, "tensor", [(t, to(t)) for t in range(NT)])


def x_by(k):
    return lambda t: (t // NX) * NX + (t % NX + k) % NX


def y_other(t):
    return t ^ NX


def swap(value):
    return lax.ppermute(value, "pipe", [(0, 1), (1, 0)])


def z_perm(value, bit):
    return lax.ppermute(value, "z", [(d, d ^ bit) for d in range(NZ)])


def y_far(value):
    return lax.ppermute(value, "yh", [(0, 1), (1, 0)])


def y_far_swap(value):
    return lax.ppermute(value, ("yh", "pipe"), [(0, 3), (1, 2), (2, 1), (3, 0)])


def cut_weight(weight, columns):
    count = columns.shape[0]
    depth, width = weight.shape[0], weight.shape[1] // NT // 2

    def kernel(columns_ref, w_ref, out_ref, sems):
        copies = []
        for i in range(count):
            at = pl.multiple_of(columns_ref[i] * width, width)
            copies.append(
                pltpu.make_async_copy(w_ref.at[:, pl.ds(at, width)], out_ref.at[i], sems.at[i])
            )
        for copy in copies:
            copy.start()
        for copy in copies:
            copy.wait()

    return pl.pallas_call(
        kernel,
        in_specs=[pl.BlockSpec(memory_space=pltpu.SMEM), pl.BlockSpec(memory_space=pl.ANY)],
        out_specs=pl.BlockSpec(memory_space=pltpu.VMEM),
        out_shape=jax.ShapeDtypeStruct((count, depth, width), weight.dtype),
        scratch_shapes=[pltpu.SemaphoreType.DMA((count,))],
        compiler_params=pltpu.CompilerParams(vmem_limit_bytes=VMEM),
        cost_estimate=SMALL,
    )(columns, weight)


def project(rows, weight, got, own, columns, jobs, shapes):
    count, depth = len(jobs), rows[0].shape[1]
    width = got[0].shape[2]
    n_rows, many, n_out = len(rows), len(got), len(shapes)
    table = jnp.concatenate([own.astype(jnp.int32)[None], columns])

    def kernel(table_ref, w_ref, *rest):
        got_refs, rest = rest[:many], rest[many:]
        row_refs, outs = rest[:n_rows], rest[n_rows : n_rows + n_out]
        blocks, sems = rest[n_rows + n_out :]
        mine = table_ref[0] > 0

        @pl.when(mine)
        def _():
            for i in range(count):
                at = pl.multiple_of(table_ref[1 + i] * width, width)
                pltpu.make_async_copy(
                    w_ref.at[:, pl.ds(at, width)], blocks.at[i], sems.at[i]
                ).start()

        @pl.when(jnp.logical_not(mine))
        def _():
            for i in range(count):
                pltpu.make_async_copy(
                    got_refs[i % many].at[i // many], blocks.at[i], sems.at[i]
                ).start()

        for i, job in enumerate(jobs):
            pltpu.make_async_copy(got_refs[0].at[0], blocks.at[i], sems.at[i]).wait()
            for r, places in job:
                y = jnp.dot(row_refs[r][...], blocks[i], preferred_element_type=F32).astype(BF)
                half = y.shape[0] // 2
                for h, (o, at) in enumerate(places):
                    outs[o][at] = y[h * half : (h + 1) * half]

    out_shapes = [jax.ShapeDtypeStruct((*s, width), BF) for s in shapes]
    vmem = pl.BlockSpec(memory_space=pltpu.VMEM)
    anywhere = pl.BlockSpec(memory_space=pl.ANY)
    return pl.pallas_call(
        kernel,
        in_specs=[pl.BlockSpec(memory_space=pltpu.SMEM)]
        + [anywhere] * (1 + many)
        + [vmem] * n_rows,
        out_specs=[vmem] * n_out,
        out_shape=out_shapes,
        scratch_shapes=[
            pltpu.VMEM((count, depth, width), BF),
            pltpu.SemaphoreType.DMA((count,)),
        ],
        compiler_params=pltpu.CompilerParams(vmem_limit_bytes=VMEM),
        cost_estimate=SMALL,
    )(table, weight, *got, *rows)


def ring_first(first_p, first_m):
    return tensor_perm(first_p, x_by(1)), tensor_perm(first_m, x_by(-1))


def ring_second(got, next_p, next_m, own0, own1):
    got_p, got_m = got
    n = got_p.shape[0] // 2
    last_p = tensor_perm((f32(next_p) + f32(got_p[:n])).astype(BF), x_by(1))
    last_m = tensor_perm((f32(next_m) + f32(got_m[:n])).astype(BF), x_by(-1))
    h0 = f32(own0) + f32(got_m[n:]) + f32(last_p)
    h1 = f32(own1) + f32(got_p[n:]) + f32(last_m)
    return h0, h1


PLACES = [((0, 0), (1, 0)), ((2, 0), (0, 1)), ((1, 1), (3, 0)), ((4, 0), (4, 1))]
FLAT = [0, 2, 4, 5, 6]


def project_first(rows_a, weight, got_other, own, columns_other):
    jobs = [[(0, tuple((0, FLAT[o] + at) for o, at in places))] for places in PLACES]
    shape = (8, rows_a.shape[0] // 2)
    return project([rows_a], weight, [got_other], own, columns_other, jobs, [shape])[0]


def project_rest(rows_a, rows_b, weight, got_other, got_mine, own, columns):
    columns = jnp.stack(columns, axis=1).reshape(-1)
    jobs = []
    for places in PLACES:
        mine, other = (tuple((o, 2 * at + w) for o, at in places) for w in range(2))
        jobs.append([(0, mine), (1, tuple((5 + o, at) for o, at in places))])
        jobs.append([(0, other)])
    half_a, half_b = rows_a.shape[0] // 2, rows_b.shape[0] // 2
    shapes = [(n, half_b) for n in (4, 4, 2, 2, 4)] + [(n, half_a) for n in (2, 2, 1, 1, 2)]
    return project([rows_b, rows_a], weight, [got_mine, got_other], own, columns, jobs, shapes)


def reduce_projection(outs, got_y, got_b):
    width = got_y.shape[2]
    b_np, b_nm, b_own = outs[2:5]
    a_fp, a_fm, a_np, a_nm, a_own = outs[5:]
    got_b = tied(got_b, got_y)
    b0, b1 = ring_second(got_b, b_np, b_nm, b_own[:2], b_own[2:])
    add = lambda part, at: f32(part) + f32(got_y[at : at + part.shape[0]])
    got_a = ring_first(add(a_fp, 0).astype(BF), add(a_fm, 2).astype(BF))
    a0, a1 = ring_second(
        got_a, add(a_np, 4), add(a_nm, 5), add(a_own[:1], 6), add(a_own[1:], 7)
    )
    away = jnp.concatenate([b0[1], b1[1]], axis=0).astype(BF)
    got_b = tensor_perm(away, y_other)
    sum_b = jnp.concatenate([b0[0], b1[0]], axis=0) + f32(got_b)
    sum_a = jnp.concatenate([a0[0], a1[0]], axis=0)
    return sum_a.reshape(-1, width), sum_b


def square_sum(rows):
    wide = f32(rows)
    return jnp.sum(wide * wide, axis=-1).reshape(-1, 128)


def tied(value, after):
    return lax.optimization_barrier((value, after))[0]


def gram_parts(normed, captured, ids, pipe, blocks, block, total_tokens, n_out):
    micro = captured.shape[0]
    rows, width = normed.shape
    each, sub = rows // micro, block // 2
    count = blocks * (blocks + 1) // 2
    slots = ids.shape[0] // NZ
    many = NZ // n_out

    def kernel(cap_ref, ids_ref, pipe_ref, n_ref, *rest):
        outs, left, grams = rest[:n_out], rest[n_out], rest[n_out + 1]
        live = cap_ref[0]
        for m in range(1, micro):
            live = live + cap_ref[m]
        for m in range(micro):
            part = pl.ds(m * each, each)
            left[part] = (f32(n_ref[part]) * cap_ref[m]).astype(BF)
        scale = 1.0 / jnp.full((1, 1), live * total_tokens, F32)
        b = 0
        for i in range(blocks):
            g = lax.dot_general(
                left[:, i * block : (i + 1) * block],
                n_ref[:, i * block :],
                (((0,), (0,)), ((), ())),
                preferred_element_type=F32,
            )
            g = g * scale
            for j in range(blocks - i):
                grams[b] = g[:, j * block : (j + 1) * block]
                b += 1
        at = pl.ds(pl.multiple_of(pipe_ref[0] * sub, sub), sub)
        for k in range(NZ):
            for i in range(slots):
                part = grams[ids_ref[k * slots + i], at, :].astype(BF)
                outs[k // many][k % many, i] = part

    smem = pl.BlockSpec(memory_space=pltpu.SMEM)
    vmem = pl.BlockSpec(memory_space=pltpu.VMEM)
    out_shape = [jax.ShapeDtypeStruct((many, slots, sub, block), BF)] * n_out
    return pl.pallas_call(
        kernel,
        in_specs=[smem, smem, smem, vmem],
        out_specs=[vmem] * n_out,
        out_shape=out_shape,
        scratch_shapes=[
            pltpu.VMEM((rows, width), BF),
            pltpu.VMEM((count, block, block), F32),
        ],
        compiler_params=pltpu.CompilerParams(vmem_limit_bytes=VMEM),
        cost_estimate=SMALL,
    )(captured, ids, pipe[None], normed)


def factor_parts(rows, squares, gain, captured, table, pipe, block, n_out):
    width = rows.shape[1]
    scale = lax.rsqrt(squares / (width * NT) + EPS).reshape(-1, 1)
    normed = (f32(rows) * scale * gain).astype(BF)
    tokens = rows.shape[0] // captured.shape[0] * NDP
    return gram_parts(
        normed, captured, table.reshape(-1), pipe, width // block, block, float(tokens), n_out
    )


def halving(keep, send, after=()):
    total = f32(keep) + f32(tied(z_perm(send, 1), after))
    for bit in (2, 4):
        n = total.shape[0] // 2
        total = total[:n] + f32(z_perm(total[n:].astype(BF), bit))
    return total[0]


def local(section_input, gain, weight, old_factor, slot_table, capture):
    pipe = lax.axis_index("pipe")
    t = lax.axis_index("tensor")
    z, yh = lax.axis_index("z"), lax.axis_index("yh")
    yl, x = t // NX, t % NX
    first = pipe == 0
    micro, each, width = section_input.shape
    half = width // 2
    w = weight[0]
    old = old_factor[0, 0]
    capacity, block, _ = old.shape
    x0 = section_input.reshape(micro * each, width)

    def pick(a, b):
        return jnp.where(first, a, b)

    ring = jnp.stack([(x + 2) % NX, (x + 1) % NX, (x + 3) % NX, x])
    other, mine = 2 * ((1 - yl) * NX + ring), 2 * (yl * NX + ring)
    got_other = swap(cut_weight(w, other + 1 - pipe))
    got_mine = swap(cut_weight(w, mine + 1 - pipe))
    params = jnp.concatenate([gain[0], capture[0].astype(F32)])
    away = swap(params)
    params = (pick(params, away), pick(away, params))
    gains = [v[:width] for v in params]
    caps = [v[width:] for v in params]
    table = jnp.maximum(slot_table, 0).reshape(NZ, NYH, capacity)
    table = jnp.where(yh == 0, table, table[:, ::-1])
    near = table
    for bit in (4, 2, 1):
        parts = near.reshape(NZ // (2 * bit), 2, bit, NYH, capacity)
        near = jnp.where(z & bit > 0, parts[:, ::-1], parts).reshape(table.shape)
    near = near.reshape(2, 2, 2, NYH, capacity).transpose(2, 1, 0, 3, 4)

    def begin(s, rows_a):
        rows_a = (f32(rows_a) * gains[s]).astype(BF)
        sent = project_first(rows_a, w, got_other, pipe == s, other + pipe)
        return rows_a, sent, tensor_perm(sent, y_other)

    def rest(s, rows_a, rows_b):
        rows_b = (f32(rows_b) * gains[s]).astype(BF)
        columns = (mine + pipe, other + pipe)
        return project_rest(rows_a, rows_b, w, got_other, got_mine, pipe == s, columns)

    def finish(rows, squares, total):
        part = lax.dynamic_slice_in_dim(rows, pipe * half, half, 1)
        scale = lax.rsqrt(squares / (width * NT) + EPS)[:, None]
        part = (f32(part) + total * scale).astype(BF)
        other = swap(part)
        return jnp.concatenate([pick(part, other), pick(other, part)], axis=1)

    squares = square_sum(x0)
    squares = squares + tensor_perm(squares, y_other)
    squares = squares + tensor_perm(squares, lambda t: t ^ 1)
    rows_a, sent, got_y = begin(0, x0[:ROWS_A])
    squares = tied(squares, sent)
    squares0 = squares + tensor_perm(squares, lambda t: t ^ 2)
    flat0 = squares0.reshape(-1)
    parts = factor_parts(x0, squares0, gains[0], caps[0], near, pipe, block, 2)
    tot0 = halving(*parts)
    outs = rest(0, rows_a, tied(x0[ROWS_A:], parts[0]))
    sum_a, sum_b = reduce_projection(outs, got_y, ring_first(*outs[:2]))
    sum_a, tot0 = lax.optimization_barrier((sum_a, tot0))
    x1a = finish(x0[:ROWS_A], flat0[:ROWS_A], sum_a)
    x1b = finish(x0[ROWS_A:], flat0[ROWS_A:], sum_b)

    rows_a, sent, got_y = begin(1, x1a)
    x1 = jnp.concatenate([x1a, x1b], axis=0)
    squares = square_sum(tied(x1, sent))
    x1b = tied(x1b, squares)
    outs = rest(1, rows_a, x1b)
    squares = squares + tied(tensor_perm(squares, y_other), outs[0])
    squares = squares + tensor_perm(squares, lambda t: t ^ 1)
    squares1 = squares + tensor_perm(squares, lambda t: t ^ 2)
    flat1 = squares1.reshape(-1)
    got_b = ring_first(*outs[:2])
    sum_a, sum_b = reduce_projection(outs, got_y, got_b)
    squares1 = tied(squares1, got_y)
    parts = factor_parts(x1, squares1, gains[1], caps[1], near, pipe, block, 2)
    tot1 = halving(*parts, got_b)
    x2 = finish(x1, flat1, jnp.concatenate([sum_a, sum_b], axis=0))
    out = pick(x1, x2).reshape(1, micro, each, width)
    here, away = pick(tot0, tot1), pick(tot1, tot0).astype(BF)
    own_rows = here[:capacity] + f32(y_far(here[capacity:].astype(BF)))
    their_rows = f32(swap(away[:capacity])) + f32(y_far_swap(away[capacity:]))
    blocks = [pick(own_rows, their_rows), pick(their_rows, own_rows)]
    blocks = jnp.concatenate(blocks, axis=1)
    own = lax.dynamic_slice_in_dim(slot_table, (z * NYH + yh) * capacity, capacity)
    new = jnp.where(
        (own >= 0)[:, None, None], DECAY * old + (1.0 - DECAY) * blocks, jnp.float32(0.0)
    )
    return (out, new[None, None])


def solution(mesh):
    devices = mesh.devices.reshape(NZ, NYH, 2, NT)
    fine = jax.sharding.Mesh(devices, ("z", "yh", "pipe", "tensor"))
    dp = ("z", "yh")
    placed = (
        P(None, dp, "tensor"),
        P("pipe", "tensor"),
        P("pipe", "tensor", None),
        P("pipe", "tensor", dp, None, None),
        P(),
        P("pipe", None),
    )
    return jax.shard_map(
        local,
        mesh=fine,
        in_specs=placed,
        out_specs=(P("pipe", None, dp, "tensor"), P("pipe", "tensor", dp, None, None)),
        check_vma=False,
    )
```

```python
import jax
import jax.numpy as jnp
from jax import lax
from jax.experimental import pallas as pl
from jax.experimental.pallas import tpu as pltpu
from jax.sharding import PartitionSpec as P

EPS = 1e-06
DECAY = 0.9
BF = jnp.bfloat16
F32 = jnp.float32
NX, NYL, NZ, NYH = 4, 2, 8, 2
NT = NX * NYL
NDP = NZ * NYH
ROWS_A = 256
VMEM = 48 * 1024 * 1024
SMALL = pl.CostEstimate(flops=1024, bytes_accessed=1024, transcendentals=0)


def f32(v):
    return v.astype(F32)


def tensor_perm(value, to):
    return lax.ppermute(value, "tensor", [(t, to(t)) for t in range(NT)])


def x_by(k):
    return lambda t: (t // NX) * NX + (t % NX + k) % NX


def y_other(t):
    return t ^ NX


def swap(value):
    return lax.ppermute(value, "pipe", [(0, 1), (1, 0)])


def hand(value, source):
    return lax.ppermute(value, "pipe", [(source, 1 - source)])


def z_perm(value, bit):
    return lax.ppermute(value, "z", [(d, d ^ bit) for d in range(NZ)])


def y_far(value):
    return lax.ppermute(value, "yh", [(0, 1), (1, 0)])


def y_far_swap(value):
    return lax.ppermute(value, ("yh", "pipe"), [(0, 3), (1, 2), (2, 1), (3, 0)])


def project(rows, weight, chunks, jobs, shapes):
    count, depth = len(jobs), rows[0].shape[1]
    width = weight.shape[1] // NT
    part, n_rows, n_out = width // 2, len(rows), 2 * len(shapes)

    def kernel(chunks_ref, w_ref, *rest):
        row_refs, outs = rest[:n_rows], rest[n_rows : n_rows + n_out]
        blocks, sems = rest[n_rows + n_out :]
        copies = []
        for i in range(count):
            at = pl.multiple_of(chunks_ref[i] * width, width)
            copies.append(
                pltpu.make_async_copy(w_ref.at[:, pl.ds(at, width)], blocks.at[i], sems.at[i])
            )
        for copy in copies:
            copy.start()
        for i, job in enumerate(jobs):
            copies[i].wait()
            for r, places in job:
                y = jnp.dot(row_refs[r][...], blocks[i], preferred_element_type=F32).astype(BF)
                half = y.shape[0] // 2
                for h, (o, at) in enumerate(places):
                    for c in range(2):
                        piece = y[h * half : (h + 1) * half, c * part : (c + 1) * part]
                        outs[c * len(shapes) + o][at : at + half] = piece

    out_shapes = [jax.ShapeDtypeStruct((n, part), BF) for n in shapes] * 2
    vmem = pl.BlockSpec(memory_space=pltpu.VMEM)
    anywhere = pl.BlockSpec(memory_space=pl.ANY)
    return pl.pallas_call(
        kernel,
        in_specs=[pl.BlockSpec(memory_space=pltpu.SMEM), anywhere] + [vmem] * n_rows,
        out_specs=[vmem] * n_out,
        out_shape=out_shapes,
        scratch_shapes=[
            pltpu.VMEM((count, depth, width), BF),
            pltpu.SemaphoreType.DMA((count,)),
        ],
        compiler_params=pltpu.CompilerParams(vmem_limit_bytes=VMEM),
        cost_estimate=SMALL,
    )(chunks, weight, *rows)


def ring_first(first_p, first_m):
    return tensor_perm(first_p, x_by(1)), tensor_perm(first_m, x_by(-1))


def ring_second(got, next_p, next_m, own0, own1):
    got_p, got_m = got
    n = got_p.shape[0] // 2
    last_p = tensor_perm((f32(next_p) + f32(got_p[:n])).astype(BF), x_by(1))
    last_m = tensor_perm((f32(next_m) + f32(got_m[:n])).astype(BF), x_by(-1))
    h0 = f32(own0) + f32(got_m[n:]) + f32(last_p)
    h1 = f32(own1) + f32(got_p[n:]) + f32(last_m)
    return h0, h1


PLACES = [(0, 2), (4, 1), (3, 5), (6, 7)]


def project_first(rows_a, weight, other):
    h = rows_a.shape[0] // 2
    jobs = [[(0, tuple((0, at * h) for at in places))] for places in PLACES]
    return project([rows_a], weight, other, jobs, [8 * h])


def project_rest(rows_a, rows_b, weight, mine, other):
    columns = jnp.stack([mine, other], axis=1).reshape(-1)
    ha, hb = rows_a.shape[0] // 2, rows_b.shape[0] // 2
    jobs = []
    for places in PLACES:
        both = [tuple((at // 4, (2 * (at % 4) + w) * hb) for at in places) for w in range(2)]
        jobs.append([(0, both[0]), (1, tuple((1, 8 * hb + at * ha) for at in places))])
        jobs.append([(0, both[1])])
    return project([rows_b, rows_a], weight, columns, jobs, [8 * hb, 8 * hb + 8 * ha])


def reduce_b(got, second):
    b0, b1 = ring_second(got, second[:2], second[2:4], second[4:6], second[6:])
    here = jnp.concatenate([b0[0], b1[0]], axis=0)
    return here, jnp.concatenate([b0[1], b1[1]], axis=0).astype(BF)


def first_a(own_a, got_y):
    total = (f32(own_a[:4]) + f32(got_y[:4])).astype(BF)
    return ring_first(total[:2], total[2:])


def reduce_a(got, own_a, got_y):
    part = lambda at: f32(own_a[at : at + 1]) + f32(got_y[at : at + 1])
    a0, a1 = ring_second(got, part(4), part(5), part(6), part(7))
    return jnp.concatenate([a0[0], a1[0]], axis=0)


def square_sum(rows):
    wide = f32(rows)
    return jnp.sum(wide * wide, axis=-1).reshape(-1, 128)


def tied(value, after):
    return lax.optimization_barrier((value, after))[0]


def gram_parts(normed, captured, ids, pipe, blocks, block, total_tokens, n_out):
    micro = captured.shape[0]
    rows, width = normed.shape
    each, sub = rows // micro, block // 2
    count = blocks * (blocks + 1) // 2
    slots = ids.shape[0] // NZ
    many = NZ // n_out

    def kernel(cap_ref, ids_ref, pipe_ref, n_ref, *rest):
        outs, left, grams = rest[:n_out], rest[n_out], rest[n_out + 1]
        live = cap_ref[0]
        for m in range(1, micro):
            live = live + cap_ref[m]
        for m in range(micro):
            part = pl.ds(m * each, each)
            left[part] = (f32(n_ref[part]) * cap_ref[m]).astype(BF)
        scale = 1.0 / jnp.full((1, 1), live * total_tokens, F32)
        b = 0
        for i in range(blocks):
            g = lax.dot_general(
                left[:, i * block : (i + 1) * block],
                n_ref[:, i * block :],
                (((0,), (0,)), ((), ())),
                preferred_element_type=F32,
            )
            g = g * scale
            for j in range(blocks - i):
                grams[b] = g[:, j * block : (j + 1) * block]
                b += 1
        at = pl.ds(pl.multiple_of(pipe_ref[0] * sub, sub), sub)
        for k in range(NZ):
            for i in range(slots):
                part = grams[ids_ref[k * slots + i], at, :].astype(BF)
                outs[k // many][k % many, i] = part

    smem = pl.BlockSpec(memory_space=pltpu.SMEM)
    vmem = pl.BlockSpec(memory_space=pltpu.VMEM)
    out_shape = [jax.ShapeDtypeStruct((many, slots, sub, block), BF)] * n_out
    return pl.pallas_call(
        kernel,
        in_specs=[smem, smem, smem, vmem],
        out_specs=[vmem] * n_out,
        out_shape=out_shape,
        scratch_shapes=[
            pltpu.VMEM((rows, width), BF),
            pltpu.VMEM((count, block, block), F32),
        ],
        compiler_params=pltpu.CompilerParams(vmem_limit_bytes=VMEM),
        cost_estimate=SMALL,
    )(captured, ids, pipe[None], normed)


def factor_parts(rows, squares, gain, captured, table, pipe, block, n_out):
    width = rows.shape[1]
    scale = lax.rsqrt(squares / (width * NT) + EPS).reshape(-1, 1)
    normed = (f32(rows) * scale * gain).astype(BF)
    tokens = rows.shape[0] // captured.shape[0] * NDP
    return gram_parts(
        normed, captured, table.reshape(-1), pipe, width // block, block, float(tokens), n_out
    )


def halving(keep, send, after):
    total = f32(keep) + f32(tied(z_perm(send, 1), after[0]))
    for i, bit in enumerate((2, 4)):
        n = total.shape[0] // 2
        total = total[:n] + f32(tied(z_perm(total[n:].astype(BF), bit), after[1 + i]))
    return total[0]


def local(section_input, gain, weight, old_factor, slot_table, capture):
    pipe = lax.axis_index("pipe")
    t = lax.axis_index("tensor")
    z, yh = lax.axis_index("z"), lax.axis_index("yh")
    yl, x = t // NX, t % NX
    first = pipe == 0
    micro, each, width = section_input.shape
    half = width // 2
    w = weight[0]
    old = old_factor[0, 0]
    capacity, block, _ = old.shape
    x0 = section_input.reshape(micro * each, width)

    def pick(a, b):
        return jnp.where(first, a, b)

    ring = jnp.stack([(x + 2) % NX, (x + 1) % NX, (x + 3) % NX, x])
    other, mine = (1 - yl) * NX + ring, yl * NX + ring
    params = jnp.concatenate([gain[0], capture[0].astype(F32)])
    away = swap(params)
    params = (pick(params, away), pick(away, params))
    gains = [v[:width] for v in params]
    caps = [v[width:] for v in params]
    table = jnp.maximum(slot_table, 0).reshape(NZ, NYH, capacity)
    table = jnp.where(yh == 0, table, table[:, ::-1])
    near = table
    for bit in (4, 2, 1):
        parts = near.reshape(NZ // (2 * bit), 2, bit, NYH, capacity)
        near = jnp.where(z & bit > 0, parts[:, ::-1], parts).reshape(table.shape)
    near = near.reshape(2, 2, 2, NYH, capacity).transpose(2, 1, 0, 3, 4)

    def scaled(s, rows):
        return (f32(rows) * gains[s]).astype(BF)

    def finish(rows, squares, total):
        part = lax.dynamic_slice_in_dim(rows, pipe * half, half, 1)
        scale = lax.rsqrt(squares / (width * NT) + EPS)[:, None]
        part = (f32(part) + total * scale).astype(BF)
        other = swap(part)
        return jnp.concatenate([pick(part, other), pick(other, part)], axis=1)

    def given(s, halves):
        return pick(halves[0], swap(halves[1])) if s == 0 else pick(swap(halves[0]), halves[1])

    def first_message(s, rows):
        return given(s, project_first(rows, w, other)).reshape(8, -1, half)

    def rest_messages(s, rows_a, rows_b):
        outs = project_rest(rows_a, rows_b, w, mine, other)
        b_first, more = given(s, (outs[0], outs[2])), given(s, (outs[1], outs[3]))
        n = b_first.shape[0]
        return [v.reshape(8, -1, half) for v in (b_first, more[:n], more[n:])]

    squares = square_sum(x0)
    squares = squares + tensor_perm(squares, y_other)
    squares = squares + tensor_perm(squares, lambda t: t ^ 1)
    rows_a = scaled(0, x0[:ROWS_A])
    sent_y = first_message(0, rows_a)
    got_y = tensor_perm(sent_y, y_other)
    rows_b = scaled(0, tied(x0[ROWS_A:], sent_y))
    b_first, b_second, a_own = rest_messages(0, rows_a, rows_b)
    squares0 = squares + tensor_perm(squares, lambda t: t ^ 2)
    flat0 = squares0.reshape(-1)
    parts = factor_parts(
        x0, tied(squares0, got_y), gains[0], caps[0], near, pipe, block, 2
    )
    got_b = tied(ring_first(b_first[:4], b_first[4:]), got_y)
    got_a = first_a(a_own, got_y)
    here, away = reduce_b(got_b, b_second)
    sum_a = reduce_a(got_a, a_own, got_y)
    sum_b = here + f32(tensor_perm(away, y_other))
    tot0 = halving(*parts, (got_b, got_a, sum_a))
    x1a = finish(x0[:ROWS_A], flat0[:ROWS_A], sum_a.reshape(-1, half))
    x1b = finish(x0[ROWS_A:], flat0[ROWS_A:], sum_b)

    rows_a = scaled(1, x1a)
    sent_y = first_message(1, rows_a)
    got_y = tensor_perm(sent_y, y_other)
    x1 = jnp.concatenate([x1a, x1b], axis=0)
    squares = square_sum(tied(x1, sent_y))
    rows_b = scaled(1, tied(x1b, (squares, tot0)))
    b_first, b_second, a_own = rest_messages(1, rows_a, rows_b)
    squares = squares + tied(tensor_perm(squares, lambda t: t ^ 1), b_first)
    squares = squares + tensor_perm(squares, lambda t: t ^ 2)
    squares1 = squares + tensor_perm(tied(squares, b_first), y_other)
    flat1 = squares1.reshape(-1)
    got_b = ring_first(b_first[:4], b_first[4:])
    parts = factor_parts(
        x1, tied(squares1, got_y), gains[1], caps[1], near, pipe, block, 2
    )
    here, away = reduce_b(tied(got_b, got_y), b_second)
    got_a = first_a(a_own, got_y)
    sum_a = reduce_a(got_a, a_own, got_y)
    sum_b = here + f32(tensor_perm(away, y_other))
    tot1 = halving(*parts, (got_b, got_a, ()))
    total = jnp.concatenate([sum_a.reshape(-1, half), sum_b], axis=0)
    x2 = finish(x1, flat1, total)
    out = pick(x1, x2).reshape(1, micro, each, width)
    here, away = pick(tot0, tot1), pick(tot1, tot0).astype(BF)
    own_rows = here[:capacity] + f32(y_far(here[capacity:].astype(BF)))
    their_rows = f32(swap(away[:capacity])) + f32(y_far_swap(away[capacity:]))
    blocks = [pick(own_rows, their_rows), pick(their_rows, own_rows)]
    blocks = jnp.concatenate(blocks, axis=1)
    own = lax.dynamic_slice_in_dim(slot_table, (z * NYH + yh) * capacity, capacity)
    new = jnp.where(
        (own >= 0)[:, None, None], DECAY * old + (1.0 - DECAY) * blocks, jnp.float32(0.0)
    )
    return (out, new[None, None])


def solution(mesh):
    devices = mesh.devices.reshape(NZ, NYH, 2, NT)
    fine = jax.sharding.Mesh(devices, ("z", "yh", "pipe", "tensor"))
    dp = ("z", "yh")
    placed = (
        P(None, dp, "tensor"),
        P("pipe", "tensor"),
        P("pipe", "tensor", None),
        P("pipe", "tensor", dp, None, None),
        P(),
        P("pipe", None),
    )
    return jax.shard_map(
        local,
        mesh=fine,
        in_specs=placed,
        out_specs=(P("pipe", None, dp, "tensor"), P("pipe", "tensor", dp, None, None)),
        check_vma=False,
    )
```

```python
import jax
import jax.numpy as jnp
from jax import lax
from jax.experimental import pallas as pl
from jax.experimental.pallas import tpu as pltpu
from jax.sharding import PartitionSpec as P

EPS = 1e-06
DECAY = 0.9
BF = jnp.bfloat16
F32 = jnp.float32
NX, NYL, NZ, NYH = 4, 2, 8, 2
NT = NX * NYL
NDP = NZ * NYH
ROWS_A = 256
VMEM = 40 * 1024 * 1024
SMALL = pl.CostEstimate(flops=1024, bytes_accessed=1024, transcendentals=0)


def f32(v):
    return v.astype(F32)


def tensor_perm(value, to):
    return lax.ppermute(value, "tensor", [(t, to(t)) for t in range(NT)])


def x_by(k):
    return lambda t: (t // NX) * NX + (t % NX + k) % NX


def y_other(t):
    return t ^ NX


def swap(value):
    return lax.ppermute(value, "pipe", [(0, 1), (1, 0)])


def hand(value, source):
    return lax.ppermute(value, "pipe", [(source, 1 - source)])


def z_perm(value, bit):
    return lax.ppermute(value, "z", [(d, d ^ bit) for d in range(NZ)])


def y_far(value):
    return lax.ppermute(value, "yh", [(0, 1), (1, 0)])


def y_far_swap(value):
    return lax.ppermute(value, ("yh", "pipe"), [(0, 3), (1, 2), (2, 1), (3, 0)])


def project(rows, weight, chunks, jobs, shapes, after):
    count, depth = len(jobs), rows[0].shape[1]
    width = weight.shape[1] // NT
    part, n_rows, n_out = width // 2, len(rows), 2 * len(shapes)

    def kernel(chunks_ref, w_ref, *rest):
        rest = rest[len(after) :]
        row_refs, outs = rest[:n_rows], rest[n_rows : n_rows + n_out]
        blocks, sems = rest[n_rows + n_out :]
        copies = []
        for i in range(count):
            at = pl.multiple_of(chunks_ref[i] * width, width)
            copies.append(
                pltpu.make_async_copy(w_ref.at[:, pl.ds(at, width)], blocks.at[i], sems.at[i])
            )
        for copy in copies:
            copy.start()
        for i, job in enumerate(jobs):
            copies[i].wait()
            for r, places in job:
                y = jnp.dot(row_refs[r][...], blocks[i], preferred_element_type=F32).astype(BF)
                half = y.shape[0] // 2
                for h, (o, at) in enumerate(places):
                    for c in range(2):
                        piece = y[h * half : (h + 1) * half, c * part : (c + 1) * part]
                        outs[c * len(shapes) + o][at : at + half] = piece

    out_shapes = [jax.ShapeDtypeStruct((n, part), BF) for n in shapes] * 2
    vmem = pl.BlockSpec(memory_space=pltpu.VMEM)
    anywhere = pl.BlockSpec(memory_space=pl.ANY)
    return pl.pallas_call(
        kernel,
        in_specs=[pl.BlockSpec(memory_space=pltpu.SMEM), pl.BlockSpec(memory_space=pltpu.HBM)]
        + [anywhere] * len(after)
        + [vmem] * n_rows,
        out_specs=[vmem] * n_out,
        out_shape=out_shapes,
        scratch_shapes=[
            pltpu.VMEM((count, depth, width), BF),
            pltpu.SemaphoreType.DMA((count,)),
        ],
        compiler_params=pltpu.CompilerParams(vmem_limit_bytes=VMEM),
        cost_estimate=pl.CostEstimate(
            flops=2 * sum(r.shape[0] for r in rows) * depth * width * count,
            bytes_accessed=2 * weight.size,
            transcendentals=0,
        ),
    )(chunks, weight, *after, *rows)


def ring_send(plus, minus):
    return tensor_perm(plus, x_by(1)), tensor_perm(minus, x_by(-1))


PLACES = [(0, 2), (4, 1), (3, 5), (6, 7)]


def project_all(rows_a, rows_b, weight, mine, other, after):
    columns = jnp.stack([mine, other], axis=1).reshape(-1)
    ha, hb = rows_a.shape[0] // 2, rows_b.shape[0] // 2
    jobs = []
    for places in PLACES:
        both = [tuple((0, (2 * at + w) * hb) for at in places) for w in range(2)]
        jobs.append([(0, both[0]), (1, tuple((0, 16 * hb + (8 + at) * ha) for at in places))])
        jobs.append([(0, both[1]), (1, tuple((0, 16 * hb + at * ha) for at in places))])
    shapes = [16 * hb + 16 * ha]
    return project([rows_b, rows_a], weight, columns, jobs, shapes, after)


def onward_b(got, second):
    return [(f32(second[2 * i : 2 * i + 2]) + f32(got[i][:2])).astype(BF) for i in range(2)]


def sums_b(got, last, second):
    h0 = f32(second[4:6]) + f32(got[1][2:]) + f32(last[0])
    h1 = f32(second[6:]) + f32(got[0][2:]) + f32(last[1])
    here = jnp.concatenate([h0[0], h1[0]], axis=0)
    return here, jnp.concatenate([h0[1], h1[1]], axis=0).astype(BF)


def first_a(own_a, got_y):
    total = (f32(own_a[:4]) + f32(got_y[:4])).astype(BF)
    return total[:2], total[2:]


def onward_a(got, own_a, got_y):
    return [
        (f32(own_a[4 + i : 5 + i]) + f32(got_y[4 + i : 5 + i]) + f32(got[i][:1])).astype(BF)
        for i in range(2)
    ]


def sums_a(got, last, own_a, got_y):
    h0 = f32(own_a[6]) + f32(got_y[6]) + f32(got[1][1]) + f32(last[0][0])
    h1 = f32(own_a[7]) + f32(got_y[7]) + f32(got[0][1]) + f32(last[1][0])
    return jnp.concatenate([h0, h1], axis=0)


def square_sum(rows):
    wide = f32(rows)
    return jnp.sum(wide * wide, axis=-1).reshape(-1, 128)


class Order:
    def __init__(self):
        self.last = None

    def step(self, work, *values):
        values, tree = jax.tree.flatten(values)
        some = values if self.last is None else [*values, self.last]
        corners = [f32(v[(0,) * v.ndim]) for v in some]
        zero = sum(jnp.minimum(jnp.abs(v), 0.0) for v in corners)
        values = [(f32(v) + zero).astype(v.dtype) for v in values]
        outs = work(*jax.tree.unflatten(tree, values))
        self.last = jax.tree.leaves(outs)[0]
        return outs

    def kernel(self, work, *values):
        outs = work(*values, [] if self.last is None else [self.last])
        self.last = jax.tree.leaves(outs)[0]
        return outs


def gram_parts(normed, captured, ids, pipe, blocks, block, total_tokens, n_out, after):
    micro = captured.shape[0]
    rows, width = normed.shape
    each, sub = rows // micro, block // 2
    count = blocks * (blocks + 1) // 2
    slots = ids.shape[0] // NZ
    many = NZ // n_out

    def kernel(cap_ref, ids_ref, pipe_ref, n_ref, *rest):
        rest = rest[len(after) :]
        outs, left, grams = rest[:n_out], rest[n_out], rest[n_out + 1]
        live = cap_ref[0]
        for m in range(1, micro):
            live = live + cap_ref[m]
        for m in range(micro):
            part = pl.ds(m * each, each)
            left[part] = (f32(n_ref[part]) * cap_ref[m]).astype(BF)
        scale = 1.0 / jnp.full((1, 1), live * total_tokens, F32)
        b = 0
        for i in range(blocks):
            g = lax.dot_general(
                left[:, i * block : (i + 1) * block],
                n_ref[:, i * block :],
                (((0,), (0,)), ((), ())),
                preferred_element_type=F32,
            )
            g = g * scale
            for j in range(blocks - i):
                grams[b] = g[:, j * block : (j + 1) * block]
                b += 1
        at = pl.ds(pl.multiple_of(pipe_ref[0] * sub, sub), sub)
        for k in range(NZ):
            for i in range(slots):
                part = grams[ids_ref[k * slots + i], at, :].astype(BF)
                outs[k // many][k % many, i] = part

    smem = pl.BlockSpec(memory_space=pltpu.SMEM)
    vmem = pl.BlockSpec(memory_space=pltpu.VMEM)
    out_shape = [jax.ShapeDtypeStruct((many, slots, sub, block), BF)] * n_out
    return pl.pallas_call(
        kernel,
        in_specs=[smem, smem, smem, vmem] + [pl.BlockSpec(memory_space=pl.ANY)] * len(after),
        out_specs=[vmem] * n_out,
        out_shape=out_shape,
        scratch_shapes=[
            pltpu.VMEM((rows, width), BF),
            pltpu.VMEM((count, block, block), F32),
        ],
        compiler_params=pltpu.CompilerParams(vmem_limit_bytes=VMEM),
        cost_estimate=SMALL,
    )(captured, ids, pipe[None], normed, *after)


def factor_parts(rows, squares, gain, captured, table, pipe, block, n_out, after):
    width = rows.shape[1]
    scale = lax.rsqrt(squares / (width * NT) + EPS).reshape(-1, 1)
    normed = (f32(rows) * scale * gain).astype(BF)
    tokens = rows.shape[0] // captured.shape[0] * NDP
    ids = table.reshape(-1)
    return gram_parts(
        normed, captured, ids, pipe, width // block, block, float(tokens), n_out, after
    )


def local(section_input, gain, weight, old_factor, slot_table, capture):
    pipe = lax.axis_index("pipe")
    t = lax.axis_index("tensor")
    z, yh = lax.axis_index("z"), lax.axis_index("yh")
    yl, x = t // NX, t % NX
    first = pipe == 0
    micro, each, width = section_input.shape
    half = width // 2
    w = weight[0]
    old = old_factor[0, 0]
    capacity, block, _ = old.shape
    x0 = section_input.reshape(micro * each, width)

    def pick(a, b):
        return jnp.where(first, a, b)

    ring = jnp.stack([(x + 2) % NX, (x + 1) % NX, (x + 3) % NX, x])
    other, mine = (1 - yl) * NX + ring, yl * NX + ring
    table = jnp.maximum(slot_table, 0).reshape(NZ, NYH, capacity)
    table = jnp.where(yh == 0, table, table[:, ::-1])
    near = table
    for bit in (4, 2, 1):
        parts = near.reshape(NZ // (2 * bit), 2, bit, NYH, capacity)
        near = jnp.where(z & bit > 0, parts[:, ::-1], parts).reshape(table.shape)
    near = near.reshape(2, 2, 2, NYH, capacity).transpose(2, 1, 0, 3, 4)

    def scaled(rows):
        return (f32(rows) * gain[0]).astype(BF)

    def finish(rows, squares, total):
        part = lax.dynamic_slice_in_dim(rows, pipe * half, half, 1)
        scale = lax.rsqrt(squares / (width * NT) + EPS)[:, None]
        return (f32(part) + total * scale).astype(BF)

    def joined(part, other):
        return jnp.concatenate([pick(part, other), pick(other, part)], axis=1)

    def kept(s, halves):
        return halves if s == 0 else halves[::-1]

    def given(s, here, other):
        return pick(here, other) if s == 0 else pick(other, here)

    def projected(s):
        def work(rows_a, rows_b, after):
            outs = project_all(scaled(rows_a), scaled(rows_b), w, mine, other, after)
            return kept(s, outs)

        return work

    def messages(s):
        def work(here, got):
            both = given(s, here, got)
            ends = [8 * half_b, 16 * half_b, 16 * half_b + 8 * half_a]
            return [v.reshape(8, -1, half) for v in jnp.split(both, ends)]

        return work

    def add(a, b):
        return a + b

    def factors(s):
        def work(rows, squares, after):
            return factor_parts(rows, squares, gains[s], caps[s], near, pipe, block, 2, after)

        return work

    def total(rows):
        def work(got_a, last_a, a_own, got_y, here_b, got_away, squares):
            sum_a = sums_a(got_a, last_a, a_own, got_y)
            both = jnp.concatenate([sum_a, here_b + f32(got_away)], axis=0)
            return finish(rows, squares.reshape(-1), both)

        return work

    def fold(keep, got):
        total = f32(keep) + f32(got)
        n = total.shape[0] // 2
        return total[:n], total[n:].astype(BF)

    half_a, half_b = ROWS_A // 2, (micro * each - ROWS_A) // 2
    side, over = lambda t: t ^ 1, lambda t: t ^ 2
    go = Order()
    params = jnp.concatenate([gain[0], capture[0].astype(F32)])
    got_params = swap(params)

    def begin(s, rows, after_kernel):
        squares = go.step(square_sum, rows)
        got_squares = tensor_perm(squares, y_other)
        here, there = go.kernel(projected(s), rows[:ROWS_A], rows[ROWS_A:])
        got = swap(there)
        also = after_kernel()
        for to in (side, over):
            squares = go.step(add, squares, got_squares)
            got_squares = tensor_perm(squares, to)
        b_first, b_second, sent_y, a_own = go.step(messages(s), here, got)
        got_y = tensor_perm(sent_y, y_other)
        got_b = ring_send(b_first[:4], b_first[4:])
        squares = go.step(add, squares, got_squares)
        return squares, got_y, got_b, b_second, a_own, also

    def exchange():
        return go.step(lambda v, got: (pick(v, got), pick(got, v)), params, got_params)

    squares, got_y, got_b, b_second, a_own, params = begin(0, x0, exchange)
    gains = [v[:width] for v in params]
    caps = [v[width:] for v in params]
    keep, send = go.kernel(factors(0), x0, squares)
    got_z = z_perm(send, 1)
    last_b = ring_send(*go.step(onward_b, got_b, b_second))
    got_a = ring_send(*go.step(first_a, a_own, got_y))
    here_b, away = go.step(sums_b, got_b, last_b, b_second)
    got_away = tensor_perm(away, y_other)
    last_a = ring_send(*go.step(onward_a, got_a, a_own, got_y))
    keep, send = go.step(fold, keep, got_z)
    got_z = z_perm(send, 2)
    part = go.step(total(x0), got_a, last_a, a_own, got_y, here_b, got_away, squares)
    got_part = swap(part)
    keep0, send = go.step(fold, keep, got_z)
    got_z0 = z_perm(send, 4)
    x1 = go.step(joined, part, got_part)

    squares, got_y, got_b, b_second, a_own, _ = begin(1, x1, lambda: None)
    keep, send = go.kernel(factors(1), x1, squares)
    got_z = z_perm(send, 1)
    last_b = ring_send(*go.step(onward_b, got_b, b_second))
    got_a = ring_send(*go.step(first_a, a_own, got_y))
    keep, send = go.step(fold, keep, got_z)
    got_z = z_perm(send, 2)
    here_b, away = go.step(sums_b, got_b, last_b, b_second)
    got_away = tensor_perm(away, y_other)
    last_a = ring_send(*go.step(onward_a, got_a, a_own, got_y))
    keep, send = go.step(fold, keep, got_z)
    got_z = z_perm(send, 4)
    part = go.step(total(x1), got_a, last_a, a_own, got_y, here_b, got_away, squares)
    got_part = swap(part)

    def split(keep0, got_z0, keep, got_z):
        tot0, tot1 = keep0[0] + f32(got_z0[0]), keep[0] + f32(got_z[0])
        here, away = pick(tot0, tot1), pick(tot1, tot0).astype(BF)
        return here[:capacity], here[capacity:].astype(BF), away[:capacity], away[capacity:]

    here, here_far, away, away_far = go.step(split, keep0, got_z0, keep, got_z)
    got_far, got_away, got_away_far = y_far(here_far), swap(away), y_far_swap(away_far)
    x2 = go.step(joined, part, got_part)
    out = pick(x1, x2).reshape(1, micro, each, width)
    own_rows = here + f32(got_far)
    their_rows = f32(got_away) + f32(got_away_far)
    blocks = [pick(own_rows, their_rows), pick(their_rows, own_rows)]
    blocks = jnp.concatenate(blocks, axis=1)
    own = lax.dynamic_slice_in_dim(slot_table, (z * NYH + yh) * capacity, capacity)
    new = jnp.where(
        (own >= 0)[:, None, None], DECAY * old + (1.0 - DECAY) * blocks, jnp.float32(0.0)
    )
    return (out, new[None, None])


def solution(mesh):
    devices = mesh.devices.reshape(NZ, NYH, 2, NT)
    fine = jax.sharding.Mesh(devices, ("z", "yh", "pipe", "tensor"))
    dp = ("z", "yh")
    placed = (
        P(None, dp, "tensor"),
        P("pipe", "tensor"),
        P("pipe", "tensor", None),
        P("pipe", "tensor", dp, None, None),
        P(),
        P("pipe", None),
    )
    return jax.shard_map(
        local,
        mesh=fine,
        in_specs=placed,
        out_specs=(P("pipe", None, dp, "tensor"), P("pipe", "tensor", dp, None, None)),
        check_vma=False,
    )
```

```python
import jax
import jax.numpy as jnp
from jax import lax
from jax.experimental import pallas as pl
from jax.experimental.pallas import tpu as pltpu
from jax.sharding import PartitionSpec as P

EPS = 1e-06
DECAY = 0.9
BF = jnp.bfloat16
F32 = jnp.float32
NX, NYL, NZ, NYH = 4, 2, 8, 2
NT = NX * NYL
NDP = NZ * NYH
ROWS_A = 224
VMEM = 48 * 1024 * 1024
SMALL = pl.CostEstimate(flops=1024, bytes_accessed=1024, transcendentals=0)


def f32(v):
    return v.astype(F32)


def tensor_perm(value, to):
    return lax.ppermute(value, "tensor", [(t, to(t)) for t in range(NT)])


def x_by(k):
    return lambda t: (t // NX) * NX + (t % NX + k) % NX


def y_other(t):
    return t ^ NX


def swap(value):
    return lax.ppermute(value, "pipe", [(0, 1), (1, 0)])


def z_perm(value, bit):
    return lax.ppermute(value, "z", [(d, d ^ bit) for d in range(NZ)])


def y_far(value):
    return lax.ppermute(value, "yh", [(0, 1), (1, 0)])


def y_far_swap(value):
    return lax.ppermute(value, ("yh", "pipe"), [(0, 3), (1, 2), (2, 1), (3, 0)])


def cut_weight(weight, columns):
    count = columns.shape[0]
    depth, width = weight.shape[0], weight.shape[1] // NT // 2

    def kernel(columns_ref, w_ref, out_ref, sems):
        copies = []
        for i in range(count):
            at = pl.multiple_of(columns_ref[i] * width, width)
            copies.append(
                pltpu.make_async_copy(w_ref.at[:, pl.ds(at, width)], out_ref.at[i], sems.at[i])
            )
        for copy in copies:
            copy.start()
        for copy in copies:
            copy.wait()

    return pl.pallas_call(
        kernel,
        in_specs=[pl.BlockSpec(memory_space=pltpu.SMEM), pl.BlockSpec(memory_space=pl.ANY)],
        out_specs=pl.BlockSpec(memory_space=pltpu.VMEM),
        out_shape=jax.ShapeDtypeStruct((count, depth, width), weight.dtype),
        scratch_shapes=[pltpu.SemaphoreType.DMA((count,))],
        compiler_params=pltpu.CompilerParams(vmem_limit_bytes=VMEM),
        cost_estimate=SMALL,
    )(columns, weight)


def project(rows, weight, got, own, columns, jobs, shapes, after=()):
    count, depth = len(jobs), rows[0].shape[1]
    width = got[0].shape[2]
    n_rows, many, n_out = len(rows), len(got), len(shapes)
    table = jnp.concatenate([own.astype(jnp.int32)[None], columns])

    def kernel(table_ref, w_ref, *rest):
        rest = rest[len(after) :]
        got_refs, rest = rest[:many], rest[many:]
        row_refs, outs = rest[:n_rows], rest[n_rows : n_rows + n_out]
        blocks, sems = rest[n_rows + n_out :]
        mine = table_ref[0] > 0

        @pl.when(mine)
        def _():
            for i in range(count):
                at = pl.multiple_of(table_ref[1 + i] * width, width)
                pltpu.make_async_copy(
                    w_ref.at[:, pl.ds(at, width)], blocks.at[i], sems.at[i]
                ).start()

        @pl.when(jnp.logical_not(mine))
        def _():
            for i in range(count):
                pltpu.make_async_copy(
                    got_refs[i % many].at[i // many], blocks.at[i], sems.at[i]
                ).start()

        for i, job in enumerate(jobs):
            pltpu.make_async_copy(got_refs[0].at[0], blocks.at[i], sems.at[i]).wait()
            for r, places in job:
                y = jnp.dot(row_refs[r][...], blocks[i], preferred_element_type=F32).astype(BF)
                half = y.shape[0] // 2
                for h, (o, at) in enumerate(places):
                    outs[o][at] = y[h * half : (h + 1) * half]

    out_shapes = [jax.ShapeDtypeStruct((*s, width), BF) for s in shapes]
    vmem = pl.BlockSpec(memory_space=pltpu.VMEM)
    anywhere = pl.BlockSpec(memory_space=pl.ANY)
    return pl.pallas_call(
        kernel,
        in_specs=[pl.BlockSpec(memory_space=pltpu.SMEM)]
        + [anywhere] * (1 + len(after) + many)
        + [vmem] * n_rows,
        out_specs=[vmem] * n_out,
        out_shape=out_shapes,
        scratch_shapes=[
            pltpu.VMEM((count, depth, width), BF),
            pltpu.SemaphoreType.DMA((count,)),
        ],
        compiler_params=pltpu.CompilerParams(vmem_limit_bytes=VMEM),
        cost_estimate=SMALL,
    )(table, weight, *after, *got, *rows)


def ring_first(first_p, first_m):
    return tensor_perm(first_p, x_by(1)), tensor_perm(first_m, x_by(-1))


def ring_second(got, next_p, next_m, own0, own1):
    got_p, got_m = got
    n = got_p.shape[0] // 2
    last_p = tensor_perm((f32(next_p) + f32(got_p[:n])).astype(BF), x_by(1))
    last_m = tensor_perm((f32(next_m) + f32(got_m[:n])).astype(BF), x_by(-1))
    h0 = f32(own0) + f32(got_m[n:]) + f32(last_p)
    h1 = f32(own1) + f32(got_p[n:]) + f32(last_m)
    return h0, h1


PLACES = [((0, 0), (1, 0)), ((2, 0), (0, 1)), ((1, 1), (3, 0)), ((4, 0), (4, 1))]
FLAT = [0, 2, 4, 5, 6]


def project_first(rows_a, weight, got_other, own, columns_other):
    jobs = [[(0, tuple((0, FLAT[o] + at) for o, at in places))] for places in PLACES]
    shape = (8, rows_a.shape[0] // 2)
    return project([rows_a], weight, [got_other], own, columns_other, jobs, [shape])[0]


def project_rest(rows_a, rows_b, weight, got_other, got_mine, own, columns):
    columns = jnp.stack(columns, axis=1).reshape(-1)
    jobs = []
    for places in PLACES:
        mine, other = (tuple((o, 2 * at + w) for o, at in places) for w in range(2))
        jobs.append([(0, mine), (1, tuple((5 + o, at) for o, at in places))])
        jobs.append([(0, other)])
    half_a, half_b = rows_a.shape[0] // 2, rows_b.shape[0] // 2
    shapes = [(n, half_b) for n in (4, 4, 2, 2, 4)] + [(n, half_a) for n in (2, 2, 1, 1, 2)]
    return project([rows_b, rows_a], weight, [got_mine, got_other], own, columns, jobs, shapes)


def reduce_projection(outs, got_y, got_b):
    width = got_y.shape[2]
    b_np, b_nm, b_own = outs[2:5]
    a_fp, a_fm, a_np, a_nm, a_own = outs[5:]
    got_b = tied(got_b, got_y)
    b0, b1 = ring_second(got_b, b_np, b_nm, b_own[:2], b_own[2:])
    add = lambda part, at: f32(part) + f32(got_y[at : at + part.shape[0]])
    got_a = ring_first(add(a_fp, 0).astype(BF), add(a_fm, 2).astype(BF))
    a0, a1 = ring_second(
        got_a, add(a_np, 4), add(a_nm, 5), add(a_own[:1], 6), add(a_own[1:], 7)
    )
    away = jnp.concatenate([b0[1], b1[1]], axis=0).astype(BF)
    got_b = tensor_perm(away, y_other)
    sum_b = jnp.concatenate([b0[0], b1[0]], axis=0) + f32(got_b)
    sum_a = jnp.concatenate([a0[0], a1[0]], axis=0)
    return sum_a.reshape(-1, width), sum_b


def square_sum(rows):
    wide = f32(rows)
    return jnp.sum(wide * wide, axis=-1).reshape(-1, 128)


def tied(value, after):
    return lax.optimization_barrier((value, after))[0]


def gram_parts(normed, captured, ids, pipe, blocks, block, total_tokens, n_out, after):
    micro = captured.shape[0]
    rows, width = normed.shape
    each, sub = rows // micro, block // 2
    count = blocks * (blocks + 1) // 2
    slots = ids.shape[0] // NZ
    many = NZ // n_out

    def kernel(cap_ref, ids_ref, pipe_ref, n_ref, *rest):
        rest = rest[len(after) :]
        outs, left, grams = rest[:n_out], rest[n_out], rest[n_out + 1]
        live = cap_ref[0]
        for m in range(1, micro):
            live = live + cap_ref[m]
        for m in range(micro):
            part = pl.ds(m * each, each)
            left[part] = (f32(n_ref[part]) * cap_ref[m]).astype(BF)
        scale = 1.0 / jnp.full((1, 1), live * total_tokens, F32)
        b = 0
        for i in range(blocks):
            g = lax.dot_general(
                left[:, i * block : (i + 1) * block],
                n_ref[:, i * block :],
                (((0,), (0,)), ((), ())),
                preferred_element_type=F32,
            )
            g = g * scale
            for j in range(blocks - i):
                grams[b] = g[:, j * block : (j + 1) * block]
                b += 1
        at = pl.ds(pl.multiple_of(pipe_ref[0] * sub, sub), sub)
        for k in range(NZ):
            for i in range(slots):
                part = grams[ids_ref[k * slots + i], at, :].astype(BF)
                outs[k // many][k % many, i] = part

    smem = pl.BlockSpec(memory_space=pltpu.SMEM)
    vmem = pl.BlockSpec(memory_space=pltpu.VMEM)
    out_shape = [jax.ShapeDtypeStruct((many, slots, sub, block), BF)] * n_out
    return pl.pallas_call(
        kernel,
        in_specs=[smem, smem, smem, vmem] + [pl.BlockSpec(memory_space=pl.ANY)] * len(after),
        out_specs=[vmem] * n_out,
        out_shape=out_shape,
        scratch_shapes=[
            pltpu.VMEM((rows, width), BF),
            pltpu.VMEM((count, block, block), F32),
        ],
        compiler_params=pltpu.CompilerParams(vmem_limit_bytes=VMEM),
        cost_estimate=SMALL,
    )(captured, ids, pipe[None], normed, *after)


def factor_parts(rows, squares, gain, captured, table, pipe, block, after):
    width = rows.shape[1]
    scale = lax.rsqrt(squares / (width * NT) + EPS).reshape(-1, 1)
    normed = (f32(rows) * scale * gain).astype(BF)
    tokens = rows.shape[0] // captured.shape[0] * NDP
    ids = table.reshape(-1)
    return gram_parts(
        normed, captured, ids, pipe, width // block, block, float(tokens), 2, after
    )


def fold(keep, got, after):
    half = keep.shape[0] // 2
    shape = (half, *keep.shape[1:])

    def kernel(keep_ref, got_ref, *rest):
        left, right = rest[len(after) :]
        for i in range(half):
            left[i] = f32(keep_ref[i]) + f32(got_ref[i])
            right[i] = (f32(keep_ref[half + i]) + f32(got_ref[half + i])).astype(BF)

    vmem = pl.BlockSpec(memory_space=pltpu.VMEM)
    return pl.pallas_call(
        kernel,
        in_specs=[vmem, vmem] + [pl.BlockSpec(memory_space=pl.ANY)] * len(after),
        out_specs=[vmem, vmem],
        out_shape=[jax.ShapeDtypeStruct(shape, F32), jax.ShapeDtypeStruct(shape, BF)],
        compiler_params=pltpu.CompilerParams(vmem_limit_bytes=16 * 1024 * 1024),
        cost_estimate=SMALL,
    )(keep, got, *after)


def halving(keep, send):
    total = f32(keep) + f32(z_perm(send, 1))
    for bit in (2, 4):
        n = total.shape[0] // 2
        total = total[:n] + f32(z_perm(total[n:].astype(BF), bit))
    return total[0]


def local(section_input, gain, weight, old_factor, slot_table, capture):
    pipe = lax.axis_index("pipe")
    t = lax.axis_index("tensor")
    z, yh = lax.axis_index("z"), lax.axis_index("yh")
    yl, x = t // NX, t % NX
    first = pipe == 0
    micro, each, width = section_input.shape
    half = width // 2
    w = weight[0]
    old = old_factor[0, 0]
    capacity, block, _ = old.shape
    x0 = section_input.reshape(micro * each, width)

    def pick(a, b):
        return jnp.where(first, a, b)

    ring = jnp.stack([(x + 2) % NX, (x + 1) % NX, (x + 3) % NX, x])
    other, mine = 2 * ((1 - yl) * NX + ring), 2 * (yl * NX + ring)
    got_other = swap(cut_weight(w, other + 1 - pipe))
    got_mine = swap(cut_weight(w, mine + 1 - pipe))
    params = jnp.concatenate([gain[0], capture[0].astype(F32)])
    away = swap(params)
    params = (pick(params, away), pick(away, params))
    gains = [v[:width] for v in params]
    caps = [v[width:] for v in params]
    table = jnp.maximum(slot_table, 0).reshape(NZ, NYH, capacity)
    table = jnp.where(yh == 0, table, table[:, ::-1])
    near = table
    for bit in (4, 2, 1):
        parts = near.reshape(NZ // (2 * bit), 2, bit, NYH, capacity)
        near = jnp.where(z & bit > 0, parts[:, ::-1], parts).reshape(table.shape)
    near = near.reshape(2, 2, 2, NYH, capacity).transpose(2, 1, 0, 3, 4)

    def begin(s, rows_a):
        rows_a = (f32(rows_a) * gains[s]).astype(BF)
        sent = project_first(rows_a, w, got_other, pipe == s, other + pipe)
        return rows_a, sent, tensor_perm(sent, y_other)

    def rest(s, rows_a, rows_b):
        rows_b = (f32(rows_b) * gains[s]).astype(BF)
        columns = (mine + pipe, other + pipe)
        return project_rest(rows_a, rows_b, w, got_other, got_mine, pipe == s, columns)

    def finish(rows, squares, total):
        part = lax.dynamic_slice_in_dim(rows, pipe * half, half, 1)
        scale = lax.rsqrt(squares / (width * NT) + EPS)[:, None]
        part = (f32(part) + total * scale).astype(BF)
        other = swap(part)
        return jnp.concatenate([pick(part, other), pick(other, part)], axis=1)

    squares = square_sum(x0)
    squares = squares + tensor_perm(squares, y_other)
    squares = squares + tensor_perm(squares, lambda t: t ^ 1)
    rows_a, sent, got_y = begin(0, x0[:ROWS_A])
    squares = tied(squares, sent)
    squares0 = squares + tensor_perm(squares, lambda t: t ^ 2)
    flat0 = squares0.reshape(-1)
    outs = rest(0, rows_a, x0[ROWS_A:])
    keep, send = factor_parts(x0, squares0, gains[0], caps[0], near, pipe, block, outs[:1])
    got_z = z_perm(send, 1)
    sum_a, sum_b = reduce_projection(outs, got_y, ring_first(*outs[:2]))
    x1a = finish(x0[:ROWS_A], flat0[:ROWS_A], sum_a)
    x1b = finish(x0[ROWS_A:], flat0[ROWS_A:], sum_b)
    keep, send = fold(keep, got_z, [x1a])
    got_z = z_perm(send, 2)

    rows_a, sent, got_y = begin(1, x1a)
    x1 = jnp.concatenate([x1a, x1b], axis=0)
    squares = square_sum(tied(x1, sent))
    x1b = tied(x1b, squares)
    outs = rest(1, rows_a, x1b)
    keep, send = fold(keep, got_z, outs[:1])
    tot0 = keep[0] + f32(z_perm(send, 4)[0])
    squares = squares + tensor_perm(squares, lambda t: t ^ 1)
    squares = squares + tensor_perm(squares, lambda t: t ^ 2)
    squares1 = squares + tensor_perm(squares, y_other)
    flat1 = squares1.reshape(-1)
    got_b = ring_first(*outs[:2])
    sum_a, sum_b = reduce_projection(outs, got_y, got_b)
    parts = factor_parts(x1, squares1, gains[1], caps[1], near, pipe, block, got_b)
    tot1 = halving(*parts)
    x2 = finish(x1, flat1, jnp.concatenate([sum_a, sum_b], axis=0))
    out = pick(x1, x2).reshape(1, micro, each, width)
    here, away = pick(tot0, tot1), pick(tot1, tot0).astype(BF)
    own_rows = here[:capacity] + f32(y_far(here[capacity:].astype(BF)))
    their_rows = f32(swap(away[:capacity])) + f32(y_far_swap(away[capacity:]))
    blocks = [pick(own_rows, their_rows), pick(their_rows, own_rows)]
    blocks = jnp.concatenate(blocks, axis=1)
    own = lax.dynamic_slice_in_dim(slot_table, (z * NYH + yh) * capacity, capacity)
    new = jnp.where(
        (own >= 0)[:, None, None], DECAY * old + (1.0 - DECAY) * blocks, jnp.float32(0.0)
    )
    return (out, new[None, None])


def solution(mesh):
    devices = mesh.devices.reshape(NZ, NYH, 2, NT)
    fine = jax.sharding.Mesh(devices, ("z", "yh", "pipe", "tensor"))
    dp = ("z", "yh")
    placed = (
        P(None, dp, "tensor"),
        P("pipe", "tensor"),
        P("pipe", "tensor", None),
        P("pipe", "tensor", dp, None, None),
        P(),
        P("pipe", None),
    )
    return jax.shard_map(
        local,
        mesh=fine,
        in_specs=placed,
        out_specs=(P("pipe", None, dp, "tensor"), P("pipe", "tensor", dp, None, None)),
        check_vma=False,
    )
```

```python
import jax
import jax.numpy as jnp
from jax import lax
from jax.experimental import pallas as pl
from jax.experimental.pallas import tpu as pltpu
from jax.sharding import PartitionSpec as P

EPS = 1e-06
DECAY = 0.9
BF = jnp.bfloat16
F32 = jnp.float32
NX, NYL, NZ, NYH = 4, 2, 8, 2
NT = NX * NYL
NDP = NZ * NYH
ROWS_A = (192, 256)
VMEM = 48 * 1024 * 1024
SMALL = pl.CostEstimate(flops=1024, bytes_accessed=1024, transcendentals=0)


def f32(v):
    return v.astype(F32)


def tensor_perm(value, to):
    return lax.ppermute(value, "tensor", [(t, to(t)) for t in range(NT)])


def x_by(k):
    return lambda t: (t // NX) * NX + (t % NX + k) % NX


def y_other(t):
    return t ^ NX


def swap(value):
    return lax.ppermute(value, "pipe", [(0, 1), (1, 0)])


def z_perm(value, bit):
    return lax.ppermute(value, "z", [(d, d ^ bit) for d in range(NZ)])


def y_far(value):
    return lax.ppermute(value, "yh", [(0, 1), (1, 0)])


def z_y_far(value):
    return lax.ppermute(value, ("z", "yh"), [(i, i ^ (4 * NYH + 1)) for i in range(NDP)])


def cut_weight(weight, columns):
    count = columns.shape[0]
    depth, width = weight.shape[0], weight.shape[1] // NT // 2

    def kernel(columns_ref, w_ref, out_ref, sems):
        copies = []
        for i in range(count):
            at = pl.multiple_of(columns_ref[i] * width, width)
            copies.append(
                pltpu.make_async_copy(w_ref.at[:, pl.ds(at, width)], out_ref.at[i], sems.at[i])
            )
        for copy in copies:
            copy.start()
        for copy in copies:
            copy.wait()

    return pl.pallas_call(
        kernel,
        in_specs=[pl.BlockSpec(memory_space=pltpu.SMEM), pl.BlockSpec(memory_space=pl.ANY)],
        out_specs=pl.BlockSpec(memory_space=pltpu.VMEM),
        out_shape=jax.ShapeDtypeStruct((count, depth, width), weight.dtype),
        scratch_shapes=[pltpu.SemaphoreType.DMA((count,))],
        compiler_params=pltpu.CompilerParams(vmem_limit_bytes=VMEM),
        cost_estimate=SMALL,
    )(columns, weight)


def project(rows, weight, got, own, columns, jobs, shapes, after=()):
    count, depth = len(jobs), rows[0].shape[1]
    width = got[0].shape[2]
    n_rows, many, n_out = len(rows), len(got), len(shapes)
    table = jnp.concatenate([own.astype(jnp.int32)[None], columns])

    def kernel(table_ref, w_ref, *rest):
        rest = rest[len(after) :]
        got_refs, rest = rest[:many], rest[many:]
        row_refs, outs = rest[:n_rows], rest[n_rows : n_rows + n_out]
        blocks, sems = rest[n_rows + n_out :]
        mine = table_ref[0] > 0

        @pl.when(mine)
        def _():
            for i in range(count):
                at = pl.multiple_of(table_ref[1 + i] * width, width)
                pltpu.make_async_copy(
                    w_ref.at[:, pl.ds(at, width)], blocks.at[i], sems.at[i]
                ).start()

        @pl.when(jnp.logical_not(mine))
        def _():
            for i in range(count):
                pltpu.make_async_copy(
                    got_refs[i % many].at[i // many], blocks.at[i], sems.at[i]
                ).start()

        for i, job in enumerate(jobs):
            pltpu.make_async_copy(got_refs[0].at[0], blocks.at[i], sems.at[i]).wait()
            for r, places in job:
                y = jnp.dot(row_refs[r][...], blocks[i], preferred_element_type=F32).astype(BF)
                half = y.shape[0] // 2
                for h, (o, at) in enumerate(places):
                    outs[o][at] = y[h * half : (h + 1) * half]

    out_shapes = [jax.ShapeDtypeStruct((*s, width), BF) for s in shapes]
    vmem = pl.BlockSpec(memory_space=pltpu.VMEM)
    anywhere = pl.BlockSpec(memory_space=pl.ANY)
    return pl.pallas_call(
        kernel,
        in_specs=[pl.BlockSpec(memory_space=pltpu.SMEM)]
        + [anywhere] * (1 + len(after) + many)
        + [vmem] * n_rows,
        out_specs=[vmem] * n_out,
        out_shape=out_shapes,
        scratch_shapes=[
            pltpu.VMEM((count, depth, width), BF),
            pltpu.SemaphoreType.DMA((count,)),
        ],
        compiler_params=pltpu.CompilerParams(vmem_limit_bytes=VMEM),
        cost_estimate=SMALL,
    )(table, weight, *after, *got, *rows)


def ring_first(first_p, first_m):
    return tensor_perm(first_p, x_by(1)), tensor_perm(first_m, x_by(-1))


def ring_second(got, next_p, next_m, own0, own1):
    got_p, got_m = got
    n = got_p.shape[0] // 2
    last_p = tensor_perm((f32(next_p) + f32(got_p[:n])).astype(BF), x_by(1))
    last_m = tensor_perm((f32(next_m) + f32(got_m[:n])).astype(BF), x_by(-1))
    h0 = f32(own0) + f32(got_m[n:]) + f32(last_p)
    h1 = f32(own1) + f32(got_p[n:]) + f32(last_m)
    return h0, h1


PLACES = [((0, 0), (1, 0)), ((2, 0), (0, 1)), ((1, 1), (3, 0)), ((4, 0), (4, 1))]
FLAT = [0, 2, 4, 5, 6]


def project_first(rows_a, weight, got_other, own, columns_other, after):
    jobs = [[(0, tuple((0, FLAT[o] + at) for o, at in places))] for places in PLACES]
    shape = (8, rows_a.shape[0] // 2)
    jobs = (jobs, [shape], after)
    return project([rows_a], weight, [got_other], own, columns_other, *jobs)[0]


def project_rest(rows_a, rows_b, weight, got_other, got_mine, own, columns, after):
    columns = jnp.stack(columns, axis=1).reshape(-1)
    jobs = []
    for places in PLACES:
        mine, other = (tuple((o, 2 * at + w) for o, at in places) for w in range(2))
        jobs.append([(0, mine), (1, tuple((5 + o, at) for o, at in places))])
        jobs.append([(0, other)])
    half_a, half_b = rows_a.shape[0] // 2, rows_b.shape[0] // 2
    shapes = [(n, half_b) for n in (4, 4, 2, 2, 4)] + [(n, half_a) for n in (2, 2, 1, 1, 2)]
    jobs = (jobs, shapes, after)
    return project([rows_b, rows_a], weight, [got_mine, got_other], own, columns, *jobs)


def reduce_projection(outs, got_y, got_b):
    width = got_y.shape[2]
    b_np, b_nm, b_own = outs[2:5]
    a_fp, a_fm, a_np, a_nm, a_own = outs[5:]
    got_b = tied(got_b, got_y)
    b0, b1 = ring_second(got_b, b_np, b_nm, b_own[:2], b_own[2:])
    add = lambda part, at: f32(part) + f32(got_y[at : at + part.shape[0]])
    got_a = ring_first(add(a_fp, 0).astype(BF), add(a_fm, 2).astype(BF))
    a0, a1 = ring_second(
        got_a, add(a_np, 4), add(a_nm, 5), add(a_own[:1], 6), add(a_own[1:], 7)
    )
    away = jnp.concatenate([b0[1], b1[1]], axis=0).astype(BF)
    got_b = tensor_perm(away, y_other)
    sum_b = jnp.concatenate([b0[0], b1[0]], axis=0) + f32(got_b)
    sum_a = jnp.concatenate([a0[0], a1[0]], axis=0)
    return sum_a.reshape(-1, width), sum_b


def square_sum(rows):
    wide = f32(rows)
    return jnp.sum(wide * wide, axis=-1).reshape(-1, 128)


def tied(value, after):
    return lax.optimization_barrier((value, after))[0]


def gram_parts(normed, captured, ids, pipe, blocks, block, total_tokens, n_out, after):
    micro = captured.shape[0]
    rows, width = normed.shape
    each, sub = rows // micro, block // 2
    count = blocks * (blocks + 1) // 2
    slots = ids.shape[0] // NZ
    many = NZ // n_out

    def kernel(cap_ref, ids_ref, pipe_ref, n_ref, *rest):
        rest = rest[len(after) :]
        outs, left, grams = rest[:n_out], rest[n_out], rest[n_out + 1]
        live = cap_ref[0]
        for m in range(1, micro):
            live = live + cap_ref[m]
        for m in range(micro):
            part = pl.ds(m * each, each)
            left[part] = (f32(n_ref[part]) * cap_ref[m]).astype(BF)
        scale = 1.0 / jnp.full((1, 1), live * total_tokens, F32)
        b = 0
        for i in range(blocks):
            g = lax.dot_general(
                left[:, i * block : (i + 1) * block],
                n_ref[:, i * block :],
                (((0,), (0,)), ((), ())),
                preferred_element_type=F32,
            )
            g = g * scale
            for j in range(blocks - i):
                grams[b] = g[:, j * block : (j + 1) * block]
                b += 1
        at = pl.ds(pl.multiple_of(pipe_ref[0] * sub, sub), sub)
        for k in range(NZ):
            for i in range(slots):
                part = grams[ids_ref[k * slots + i], at, :].astype(BF)
                outs[k // many][k % many, i] = part

    smem = pl.BlockSpec(memory_space=pltpu.SMEM)
    vmem = pl.BlockSpec(memory_space=pltpu.VMEM)
    out_shape = [jax.ShapeDtypeStruct((many, slots, sub, block), BF)] * n_out
    return pl.pallas_call(
        kernel,
        in_specs=[smem, smem, smem, vmem] + [pl.BlockSpec(memory_space=pl.ANY)] * len(after),
        out_specs=[vmem] * n_out,
        out_shape=out_shape,
        scratch_shapes=[
            pltpu.VMEM((rows, width), BF),
            pltpu.VMEM((count, block, block), F32),
        ],
        compiler_params=pltpu.CompilerParams(vmem_limit_bytes=VMEM),
        cost_estimate=SMALL,
    )(captured, ids, pipe[None], normed, *after)


def factor_parts(rows, squares, gain, captured, table, pipe, block, after):
    width = rows.shape[1]
    scale = lax.rsqrt(squares / (width * NT) + EPS).reshape(-1, 1)
    normed = (f32(rows) * scale * gain).astype(BF)
    tokens = rows.shape[0] // captured.shape[0] * NDP
    ids = table.reshape(-1)
    return gram_parts(
        normed, captured, ids, pipe, width // block, block, float(tokens), 2, after
    )


def fold(keep, got, after):
    half = keep.shape[0] // 2
    shape = (half, *keep.shape[1:])

    def kernel(keep_ref, got_ref, *rest):
        left, right = rest[len(after) :]
        for i in range(half):
            left[i] = f32(keep_ref[i]) + f32(got_ref[i])
            right[i] = (f32(keep_ref[half + i]) + f32(got_ref[half + i])).astype(BF)

    vmem = pl.BlockSpec(memory_space=pltpu.VMEM)
    return pl.pallas_call(
        kernel,
        in_specs=[vmem, vmem] + [pl.BlockSpec(memory_space=pl.ANY)] * len(after),
        out_specs=[vmem, vmem],
        out_shape=[jax.ShapeDtypeStruct(shape, F32), jax.ShapeDtypeStruct(shape, BF)],
        compiler_params=pltpu.CompilerParams(vmem_limit_bytes=16 * 1024 * 1024),
        cost_estimate=SMALL,
    )(keep, got, *after)


def spread(keep, got, after):
    slots, sub, block = keep.shape[1:]
    near = slots // 2

    def kernel(keep_ref, got_ref, *rest):
        outs = rest[len(after) :]
        for i in range(2):
            total = f32(keep_ref[i]) + f32(got_ref[i])
            outs[2 * i][...] = total[:near].astype(outs[2 * i].dtype)
            outs[2 * i + 1][...] = total[near:].astype(BF)

    vmem = pl.BlockSpec(memory_space=pltpu.VMEM)
    out_shape = [jax.ShapeDtypeStruct((near, sub, block), t) for t in (F32, BF, BF, BF)]
    own, own_far, other, other_far = pl.pallas_call(
        kernel,
        in_specs=[vmem, vmem] + [pl.BlockSpec(memory_space=pl.ANY)] * len(after),
        out_specs=[vmem] * 4,
        out_shape=out_shape,
        compiler_params=pltpu.CompilerParams(vmem_limit_bytes=16 * 1024 * 1024),
        cost_estimate=SMALL,
    )(keep, got, *after)
    return own + f32(z_perm(other, 4)) + f32(y_far(own_far)) + f32(z_y_far(other_far))


def plus(a, b, after):
    def kernel(a_ref, b_ref, *rest):
        rest[-1][...] = a_ref[...] + b_ref[...]

    vmem = pl.BlockSpec(memory_space=pltpu.VMEM)
    return pl.pallas_call(
        kernel,
        in_specs=[vmem, vmem] + [pl.BlockSpec(memory_space=pl.ANY)] * len(after),
        out_specs=vmem,
        out_shape=jax.ShapeDtypeStruct(a.shape, F32),
        compiler_params=pltpu.CompilerParams(vmem_limit_bytes=16 * 1024 * 1024),
        cost_estimate=SMALL,
    )(a, b, *after)


def local(section_input, gain, weight, old_factor, slot_table, capture):
    pipe = lax.axis_index("pipe")
    t = lax.axis_index("tensor")
    z, yh = lax.axis_index("z"), lax.axis_index("yh")
    yl, x = t // NX, t % NX
    first = pipe == 0
    micro, each, width = section_input.shape
    half = width // 2
    w = weight[0]
    old = old_factor[0, 0]
    capacity, block, _ = old.shape
    x0 = section_input.reshape(micro * each, width)

    def pick(a, b):
        return jnp.where(first, a, b)

    ring = jnp.stack([(x + 2) % NX, (x + 1) % NX, (x + 3) % NX, x])
    other, mine = 2 * ((1 - yl) * NX + ring), 2 * (yl * NX + ring)
    got_other = swap(cut_weight(w, other + 1 - pipe))
    got_mine = swap(cut_weight(w, mine + 1 - pipe))
    params = jnp.concatenate([gain[0], capture[0].astype(F32)])
    away = swap(params)
    params = (pick(params, away), pick(away, params))
    gains = [v[:width] for v in params]
    caps = [v[width:] for v in params]
    table = jnp.maximum(slot_table, 0).reshape(NZ, NYH, capacity)
    table = jnp.where(yh == 0, table, table[:, ::-1])
    near = table
    for bit in (4, 2, 1):
        parts = near.reshape(NZ // (2 * bit), 2, bit, NYH, capacity)
        near = jnp.where(z & bit > 0, parts[:, ::-1], parts).reshape(table.shape)
    near = near.reshape(2, 2, 2, NYH, capacity).transpose(2, 1, 0, 3, 4)

    def begin(s, rows_a, after):
        rows_a = (f32(rows_a) * gains[s]).astype(BF)
        sent = project_first(rows_a, w, got_other, pipe == s, other + pipe, after)
        return rows_a, sent, tensor_perm(sent, y_other)

    def rest(s, rows_a, rows_b, after):
        rows_b = (f32(rows_b) * gains[s]).astype(BF)
        columns = (mine + pipe, other + pipe)
        return project_rest(rows_a, rows_b, w, got_other, got_mine, pipe == s, columns, after)

    def finish(rows, squares, total):
        part = lax.dynamic_slice_in_dim(rows, pipe * half, half, 1)
        scale = lax.rsqrt(squares / (width * NT) + EPS)[:, None]
        part = (f32(part) + total * scale).astype(BF)
        other = swap(part)
        return jnp.concatenate([pick(part, other), pick(other, part)], axis=1)

    side, over = lambda t: t ^ 1, lambda t: t ^ 2
    side, over = lambda t: t ^ 1, lambda t: t ^ 2
    squares = square_sum(x0)
    got_squares = tensor_perm(squares, y_other)
    rows_a, sent, got_y = begin(0, x0[: ROWS_A[0]], [squares])
    squares = plus(squares, got_squares, [sent])
    got_squares = tensor_perm(squares, side)
    outs = rest(0, rows_a, x0[ROWS_A[0] :], [squares])
    squares = plus(squares, got_squares, outs[:1])
    squares0 = squares + tensor_perm(squares, over)
    flat0 = squares0.reshape(-1)
    keep, send = factor_parts(x0, squares0, gains[0], caps[0], near, pipe, block, [got_y])
    got_z = z_perm(send, 1)
    sum_a, sum_b = reduce_projection(outs, got_y, ring_first(*outs[:2]))
    x1 = finish(x0, flat0, jnp.concatenate([sum_a, sum_b], axis=0))

    squares = square_sum(x1)
    got_squares = tensor_perm(squares, side)
    rows_a, sent, got_y = begin(1, x1[: ROWS_A[1]], [squares])
    squares = plus(squares, got_squares, [sent])
    got_squares = tensor_perm(squares, over)
    outs = rest(1, rows_a, x1[ROWS_A[1] :], [squares])
    squares = plus(squares, got_squares, outs[:1])
    got_squares = tensor_perm(squares, y_other)
    squares1 = squares + got_squares
    flat1 = squares1.reshape(-1)
    got_b = ring_first(*outs[:2])
    sum_a, sum_b = reduce_projection(outs, got_y, got_b)
    keep0, send0 = fold(keep, got_z, [got_squares])
    got_z0 = z_perm(send0, 2)
    keep, send = factor_parts(x1, squares1, gains[1], caps[1], near, pipe, block, got_b)
    keep, send = fold(keep, z_perm(send, 1), [])
    own0 = spread(keep0, got_z0, [keep])
    own1 = spread(keep, z_perm(send, 2), [sum_a])
    x2 = finish(x1, flat1, jnp.concatenate([sum_a, sum_b], axis=0))
    out = pick(x1, x2).reshape(1, micro, each, width)
    kept, got = pick(own0, own1), f32(swap(pick(own1, own0).astype(BF)))
    blocks = [pick(kept, got), pick(got, kept)]
    blocks = jnp.concatenate(blocks, axis=1)
    own = lax.dynamic_slice_in_dim(slot_table, (z * NYH + yh) * capacity, capacity)
    new = jnp.where(
        (own >= 0)[:, None, None], DECAY * old + (1.0 - DECAY) * blocks, jnp.float32(0.0)
    )
    return (out, new[None, None])


def solution(mesh):
    devices = mesh.devices.reshape(NZ, NYH, 2, NT)
    fine = jax.sharding.Mesh(devices, ("z", "yh", "pipe", "tensor"))
    dp = ("z", "yh")
    placed = (
        P(None, dp, "tensor"),
        P("pipe", "tensor"),
        P("pipe", "tensor", None),
        P("pipe", "tensor", dp, None, None),
        P(),
        P("pipe", None),
    )
    return jax.shard_map(
        local,
        mesh=fine,
        in_specs=placed,
        out_specs=(P("pipe", None, dp, "tensor"), P("pipe", "tensor", dp, None, None)),
        check_vma=False,
    )
```

```python
import jax
import jax.numpy as jnp
from jax import lax
from jax.experimental import pallas as pl
from jax.experimental.pallas import tpu as pltpu
from jax.sharding import PartitionSpec as P

EPS = 1e-06
DECAY = 0.9
BF = jnp.bfloat16
F32 = jnp.float32
NX, NYL, NZ, NYH = 4, 2, 8, 2
NT = NX * NYL
NDP = NZ * NYH
ROWS_A = 224
VMEM = 48 * 1024 * 1024
SMALL = pl.CostEstimate(flops=1024, bytes_accessed=1024, transcendentals=0)


def f32(v):
    return v.astype(F32)


def tensor_perm(value, to):
    return lax.ppermute(value, "tensor", [(t, to(t)) for t in range(NT)])


def x_by(k):
    return lambda t: (t // NX) * NX + (t % NX + k) % NX


def y_other(t):
    return t ^ NX


def swap(value):
    return lax.ppermute(value, "pipe", [(0, 1), (1, 0)])


def z_perm(value, bit):
    return lax.ppermute(value, "z", [(d, d ^ bit) for d in range(NZ)])


def y_far(value):
    return lax.ppermute(value, "yh", [(0, 1), (1, 0)])


def y_far_swap(value):
    return lax.ppermute(value, ("yh", "pipe"), [(0, 3), (1, 2), (2, 1), (3, 0)])


def cut_weight(weight, columns):
    count = columns.shape[0]
    depth, width = weight.shape[0], weight.shape[1] // NT // 2

    def kernel(columns_ref, w_ref, out_ref, sems):
        copies = []
        for i in range(count):
            at = pl.multiple_of(columns_ref[i] * width, width)
            copies.append(
                pltpu.make_async_copy(w_ref.at[:, pl.ds(at, width)], out_ref.at[i], sems.at[i])
            )
        for copy in copies:
            copy.start()
        for copy in copies:
            copy.wait()

    return pl.pallas_call(
        kernel,
        in_specs=[pl.BlockSpec(memory_space=pltpu.SMEM), pl.BlockSpec(memory_space=pl.ANY)],
        out_specs=pl.BlockSpec(memory_space=pltpu.VMEM),
        out_shape=jax.ShapeDtypeStruct((count, depth, width), weight.dtype),
        scratch_shapes=[pltpu.SemaphoreType.DMA((count,))],
        compiler_params=pltpu.CompilerParams(vmem_limit_bytes=VMEM),
        cost_estimate=SMALL,
    )(columns, weight)


def project(rows, weight, got, own, columns, jobs, shapes, after=()):
    count, depth = len(jobs), rows[0].shape[1]
    width = got[0].shape[2]
    n_rows, many, n_out = len(rows), len(got), len(shapes)
    table = jnp.concatenate([own.astype(jnp.int32)[None], columns])

    def kernel(table_ref, w_ref, *rest):
        rest = rest[len(after) :]
        got_refs, rest = rest[:many], rest[many:]
        row_refs, outs = rest[:n_rows], rest[n_rows : n_rows + n_out]
        blocks, sems = rest[n_rows + n_out :]
        mine = table_ref[0] > 0

        @pl.when(mine)
        def _():
            for i in range(count):
                at = pl.multiple_of(table_ref[1 + i] * width, width)
                pltpu.make_async_copy(
                    w_ref.at[:, pl.ds(at, width)], blocks.at[i], sems.at[i]
                ).start()

        @pl.when(jnp.logical_not(mine))
        def _():
            for i in range(count):
                pltpu.make_async_copy(
                    got_refs[i % many].at[i // many], blocks.at[i], sems.at[i]
                ).start()

        for i, job in enumerate(jobs):
            pltpu.make_async_copy(got_refs[0].at[0], blocks.at[i], sems.at[i]).wait()
            for r, places in job:
                y = jnp.dot(row_refs[r][...], blocks[i], preferred_element_type=F32).astype(BF)
                half = y.shape[0] // 2
                for h, (o, at) in enumerate(places):
                    outs[o][at] = y[h * half : (h + 1) * half]

    out_shapes = [jax.ShapeDtypeStruct((*s, width), BF) for s in shapes]
    vmem = pl.BlockSpec(memory_space=pltpu.VMEM)
    anywhere = pl.BlockSpec(memory_space=pl.ANY)
    return pl.pallas_call(
        kernel,
        in_specs=[pl.BlockSpec(memory_space=pltpu.SMEM)]
        + [anywhere] * (1 + len(after) + many)
        + [vmem] * n_rows,
        out_specs=[vmem] * n_out,
        out_shape=out_shapes,
        scratch_shapes=[
            pltpu.VMEM((count, depth, width), BF),
            pltpu.SemaphoreType.DMA((count,)),
        ],
        compiler_params=pltpu.CompilerParams(vmem_limit_bytes=VMEM),
        cost_estimate=SMALL,
    )(table, weight, *after, *got, *rows)


def ring_first(first_p, first_m):
    return tensor_perm(first_p, x_by(1)), tensor_perm(first_m, x_by(-1))


def ring_second(got, next_p, next_m, own0, own1):
    got_p, got_m = got
    n = got_p.shape[0] // 2
    last_p = tensor_perm((f32(next_p) + f32(got_p[:n])).astype(BF), x_by(1))
    last_m = tensor_perm((f32(next_m) + f32(got_m[:n])).astype(BF), x_by(-1))
    h0 = f32(own0) + f32(got_m[n:]) + f32(last_p)
    h1 = f32(own1) + f32(got_p[n:]) + f32(last_m)
    return h0, h1


PLACES = [((0, 0), (1, 0)), ((2, 0), (0, 1)), ((1, 1), (3, 0)), ((4, 0), (4, 1))]
FLAT = [0, 2, 4, 5, 6]


def project_first(rows_a, weight, got_other, own, columns_other, after):
    jobs = [[(0, tuple((0, FLAT[o] + at) for o, at in places))] for places in PLACES]
    shape = (8, rows_a.shape[0] // 2)
    jobs = (jobs, [shape], after)
    return project([rows_a], weight, [got_other], own, columns_other, *jobs)[0]


def project_rest(rows_a, rows_b, weight, got_other, got_mine, own, columns, after):
    columns = jnp.stack(columns, axis=1).reshape(-1)
    jobs = []
    for places in PLACES:
        mine, other = (tuple((o, 2 * at + w) for o, at in places) for w in range(2))
        jobs.append([(0, mine), (1, tuple((5 + o, at) for o, at in places))])
        jobs.append([(0, other)])
    half_a, half_b = rows_a.shape[0] // 2, rows_b.shape[0] // 2
    shapes = [(n, half_b) for n in (4, 4, 2, 2, 4)] + [(n, half_a) for n in (2, 2, 1, 1, 2)]
    jobs = (jobs, shapes, after)
    return project([rows_b, rows_a], weight, [got_mine, got_other], own, columns, *jobs)


def reduce_projection(outs, got_y, got_b, after):
    width = got_y.shape[2]
    b_np, b_nm, b_own = outs[2:5]
    a_fp, a_fm, a_np, a_nm, a_own = outs[5:]
    got_b = tied(got_b, got_y)
    b0, b1 = ring_second(got_b, b_np, b_nm, b_own[:2], b_own[2:])
    add = lambda part, at: f32(part) + f32(got_y[at : at + part.shape[0]])
    got_p, got_m = ring_first(add(a_fp, 0).astype(BF), add(a_fm, 2).astype(BF))
    sent = onward((a_np, a_nm), (got_y[4:5], got_y[5:6]), (got_p, got_m), after)
    last_p, last_m = tensor_perm(sent[0], x_by(1)), tensor_perm(sent[1], x_by(-1))
    a0 = add(a_own[:1], 6) + f32(got_m[1:]) + f32(last_p)
    a1 = add(a_own[1:], 7) + f32(got_p[1:]) + f32(last_m)
    away = jnp.concatenate([b0[1], b1[1]], axis=0).astype(BF)
    got_b = tensor_perm(away, y_other)
    sum_b = jnp.concatenate([b0[0], b1[0]], axis=0) + f32(got_b)
    sum_a = jnp.concatenate([a0[0], a1[0]], axis=0)
    return sum_a.reshape(-1, width), sum_b


def square_sum(rows):
    wide = f32(rows)
    return jnp.sum(wide * wide, axis=-1).reshape(-1, 128)


def tied(value, after):
    return lax.optimization_barrier((value, after))[0]


def gram_parts(normed, captured, ids, pipe, blocks, block, total_tokens, n_out, after):
    micro = captured.shape[0]
    rows, width = normed.shape
    each, sub = rows // micro, block // 2
    count = blocks * (blocks + 1) // 2
    slots = ids.shape[0] // NZ
    many = NZ // n_out

    def kernel(cap_ref, ids_ref, pipe_ref, n_ref, *rest):
        rest = rest[len(after) :]
        outs, left, grams = rest[:n_out], rest[n_out], rest[n_out + 1]
        live = cap_ref[0]
        for m in range(1, micro):
            live = live + cap_ref[m]
        for m in range(micro):
            part = pl.ds(m * each, each)
            left[part] = (f32(n_ref[part]) * cap_ref[m]).astype(BF)
        scale = 1.0 / jnp.full((1, 1), live * total_tokens, F32)
        b = 0
        for i in range(blocks):
            g = lax.dot_general(
                left[:, i * block : (i + 1) * block],
                n_ref[:, i * block :],
                (((0,), (0,)), ((), ())),
                preferred_element_type=F32,
            )
            g = g * scale
            for j in range(blocks - i):
                grams[b] = g[:, j * block : (j + 1) * block]
                b += 1
        at = pl.ds(pl.multiple_of(pipe_ref[0] * sub, sub), sub)
        for k in range(NZ):
            for i in range(slots):
                part = grams[ids_ref[k * slots + i], at, :].astype(BF)
                outs[k // many][k % many, i] = part

    smem = pl.BlockSpec(memory_space=pltpu.SMEM)
    vmem = pl.BlockSpec(memory_space=pltpu.VMEM)
    out_shape = [jax.ShapeDtypeStruct((many, slots, sub, block), BF)] * n_out
    return pl.pallas_call(
        kernel,
        in_specs=[smem, smem, smem, vmem] + [pl.BlockSpec(memory_space=pl.ANY)] * len(after),
        out_specs=[vmem] * n_out,
        out_shape=out_shape,
        scratch_shapes=[
            pltpu.VMEM((rows, width), BF),
            pltpu.VMEM((count, block, block), F32),
        ],
        compiler_params=pltpu.CompilerParams(vmem_limit_bytes=VMEM),
        cost_estimate=SMALL,
    )(captured, ids, pipe[None], normed, *after)


def factor_parts(rows, squares, gain, captured, table, pipe, block, after):
    width = rows.shape[1]
    scale = lax.rsqrt(squares / (width * NT) + EPS).reshape(-1, 1)
    normed = (f32(rows) * scale * gain).astype(BF)
    tokens = rows.shape[0] // captured.shape[0] * NDP
    ids = table.reshape(-1)
    return gram_parts(
        normed, captured, ids, pipe, width // block, block, float(tokens), 2, after
    )


def fold(keep, got, after):
    half = keep.shape[0] // 2
    shape = (half, *keep.shape[1:])

    def kernel(keep_ref, got_ref, *rest):
        left, right = rest[len(after) :]
        for i in range(half):
            left[i] = f32(keep_ref[i]) + f32(got_ref[i])
            right[i] = (f32(keep_ref[half + i]) + f32(got_ref[half + i])).astype(BF)

    vmem = pl.BlockSpec(memory_space=pltpu.VMEM)
    return pl.pallas_call(
        kernel,
        in_specs=[vmem, vmem] + [pl.BlockSpec(memory_space=pl.ANY)] * len(after),
        out_specs=[vmem, vmem],
        out_shape=[jax.ShapeDtypeStruct(shape, F32), jax.ShapeDtypeStruct(shape, BF)],
        compiler_params=pltpu.CompilerParams(vmem_limit_bytes=16 * 1024 * 1024),
        cost_estimate=SMALL,
    )(keep, got, *after)


def plus(a, b, after):
    def kernel(a_ref, b_ref, *rest):
        rest[-1][...] = a_ref[...] + b_ref[...]

    vmem = pl.BlockSpec(memory_space=pltpu.VMEM)
    return pl.pallas_call(
        kernel,
        in_specs=[vmem, vmem] + [pl.BlockSpec(memory_space=pl.ANY)] * len(after),
        out_specs=vmem,
        out_shape=jax.ShapeDtypeStruct(a.shape, F32),
        compiler_params=pltpu.CompilerParams(vmem_limit_bytes=16 * 1024 * 1024),
        cost_estimate=SMALL,
    )(a, b, *after)


def onward(own, got_y, got, after):
    def kernel(*refs):
        ins, outs = refs[:6], refs[-2:]
        for i in range(2):
            o, y, g = ins[3 * i : 3 * i + 3]
            outs[i][...] = (f32(o[...]) + f32(y[...]) + f32(g[:1])).astype(BF)

    vmem = pl.BlockSpec(memory_space=pltpu.VMEM)
    ins = [v for i in range(2) for v in (own[i], got_y[i], got[i])]
    return pl.pallas_call(
        kernel,
        in_specs=[vmem] * 6 + [pl.BlockSpec(memory_space=pl.ANY)] * len(after),
        out_specs=[vmem] * 2,
        out_shape=[jax.ShapeDtypeStruct(own[0].shape, BF)] * 2,
        compiler_params=pltpu.CompilerParams(vmem_limit_bytes=16 * 1024 * 1024),
        cost_estimate=SMALL,
    )(*ins, *after)


def local(section_input, gain, weight, old_factor, slot_table, capture):
    pipe = lax.axis_index("pipe")
    t = lax.axis_index("tensor")
    z, yh = lax.axis_index("z"), lax.axis_index("yh")
    yl, x = t // NX, t % NX
    first = pipe == 0
    micro, each, width = section_input.shape
    half = width // 2
    w = weight[0]
    old = old_factor[0, 0]
    capacity, block, _ = old.shape
    x0 = section_input.reshape(micro * each, width)

    def pick(a, b):
        return jnp.where(first, a, b)

    ring = jnp.stack([(x + 2) % NX, (x + 1) % NX, (x + 3) % NX, x])
    other, mine = 2 * ((1 - yl) * NX + ring), 2 * (yl * NX + ring)
    got_other = swap(cut_weight(w, other + 1 - pipe))
    got_mine = swap(cut_weight(w, mine + 1 - pipe))
    params = jnp.concatenate([gain[0], capture[0].astype(F32)])
    away = swap(params)
    params = (pick(params, away), pick(away, params))
    gains = [v[:width] for v in params]
    caps = [v[width:] for v in params]
    table = jnp.maximum(slot_table, 0).reshape(NZ, NYH, capacity)
    table = jnp.where(yh == 0, table, table[:, ::-1])
    near = table
    for bit in (4, 2, 1):
        parts = near.reshape(NZ // (2 * bit), 2, bit, NYH, capacity)
        near = jnp.where(z & bit > 0, parts[:, ::-1], parts).reshape(table.shape)
    near = near.reshape(2, 2, 2, NYH, capacity).transpose(2, 1, 0, 3, 4)

    def begin(s, rows_a, after=()):
        rows_a = (f32(rows_a) * gains[s]).astype(BF)
        sent = project_first(rows_a, w, got_other, pipe == s, other + pipe, after)
        return rows_a, sent, tensor_perm(sent, y_other)

    def rest(s, rows_a, rows_b, after=()):
        rows_b = (f32(rows_b) * gains[s]).astype(BF)
        columns = (mine + pipe, other + pipe)
        return project_rest(rows_a, rows_b, w, got_other, got_mine, pipe == s, columns, after)

    def finish(rows, squares, total):
        part = lax.dynamic_slice_in_dim(rows, pipe * half, half, 1)
        scale = lax.rsqrt(squares / (width * NT) + EPS)[:, None]
        part = (f32(part) + total * scale).astype(BF)
        other = swap(part)
        return jnp.concatenate([pick(part, other), pick(other, part)], axis=1)

    side, over = lambda t: t ^ 1, lambda t: t ^ 2
    squares = square_sum(x0)
    got_squares = tensor_perm(squares, y_other)
    rows_a, sent, got_y = begin(0, x0[:ROWS_A], [squares])
    squares = plus(squares, got_squares, [sent])
    got_squares = tensor_perm(squares, side)
    outs = rest(0, rows_a, x0[ROWS_A:])
    squares = plus(squares, got_squares, outs[:1])
    squares0 = squares + tensor_perm(squares, over)
    flat0 = squares0.reshape(-1)
    keep, send = factor_parts(x0, squares0, gains[0], caps[0], near, pipe, block, outs[:1])
    got_z = z_perm(send, 1)
    sum_a, sum_b = reduce_projection(outs, got_y, ring_first(*outs[:2]), [])
    x1a = finish(x0[:ROWS_A], flat0[:ROWS_A], sum_a)
    x1b = finish(x0[ROWS_A:], flat0[ROWS_A:], sum_b)
    keep0, send0 = fold(keep, got_z, [x1a])
    got_z0 = z_perm(send0, 2)

    rows_a, sent, got_y = begin(1, x1a)
    x1 = jnp.concatenate([x1a, x1b], axis=0)
    squares = square_sum(x1)
    got_squares = tensor_perm(squares, side)
    squares = plus(squares, got_squares, [sent])
    got_squares = tensor_perm(squares, over)
    outs = rest(1, rows_a, x1b, [squares, send0])
    keep0, send0 = fold(keep0, got_z0, [])
    squares = plus(squares, got_squares, outs[:1])
    squares1 = squares + tensor_perm(squares, y_other)
    flat1 = squares1.reshape(-1)
    got_b = ring_first(*outs[:2])
    waits = [*got_b, send0]
    keep, send = factor_parts(x1, squares1, gains[1], caps[1], near, pipe, block, waits)
    keep, send = fold(keep, z_perm(send, 1), [])
    got_z = z_perm(send, 2)
    sum_a, sum_b = reduce_projection(outs, got_y, got_b, [keep])
    keep, send = fold(keep, got_z, [])
    got_z = z_perm(jnp.concatenate([send0, send], axis=0), 4)
    tot0, tot1 = keep0[0] + f32(got_z[0]), keep[0] + f32(got_z[1])
    x2 = finish(x1, flat1, jnp.concatenate([sum_a, sum_b], axis=0))
    out = pick(x1, x2).reshape(1, micro, each, width)
    here, away = pick(tot0, tot1), pick(tot1, tot0).astype(BF)
    own_rows = here[:capacity] + f32(y_far(here[capacity:].astype(BF)))
    their_rows = f32(swap(away[:capacity])) + f32(y_far_swap(away[capacity:]))
    blocks = [pick(own_rows, their_rows), pick(their_rows, own_rows)]
    blocks = jnp.concatenate(blocks, axis=1)
    own = lax.dynamic_slice_in_dim(slot_table, (z * NYH + yh) * capacity, capacity)
    new = jnp.where(
        (own >= 0)[:, None, None], DECAY * old + (1.0 - DECAY) * blocks, jnp.float32(0.0)
    )
    return (out, new[None, None])


def solution(mesh):
    devices = mesh.devices.reshape(NZ, NYH, 2, NT)
    fine = jax.sharding.Mesh(devices, ("z", "yh", "pipe", "tensor"))
    dp = ("z", "yh")
    placed = (
        P(None, dp, "tensor"),
        P("pipe", "tensor"),
        P("pipe", "tensor", None),
        P("pipe", "tensor", dp, None, None),
        P(),
        P("pipe", None),
    )
    return jax.shard_map(
        local,
        mesh=fine,
        in_specs=placed,
        out_specs=(P("pipe", None, dp, "tensor"), P("pipe", "tensor", dp, None, None)),
        check_vma=False,
    )
```

```python
import jax
import jax.numpy as jnp
from jax import lax
from jax.experimental import pallas as pl
from jax.experimental.pallas import tpu as pltpu
from jax.sharding import PartitionSpec as P

EPS = 1e-06
DECAY = 0.9
BF = jnp.bfloat16
F32 = jnp.float32
NX, NYL, NZ, NYH = 4, 2, 8, 2
NT = NX * NYL
NDP = NZ * NYH
ROWS_A = 224
VMEM = 48 * 1024 * 1024
SMALL = pl.CostEstimate(flops=1024, bytes_accessed=1024, transcendentals=0)


def f32(v):
    return v.astype(F32)


def tensor_perm(value, to):
    return lax.ppermute(value, "tensor", [(t, to(t)) for t in range(NT)])


def x_by(k):
    return lambda t: (t // NX) * NX + (t % NX + k) % NX


def y_other(t):
    return t ^ NX


def swap(value):
    return lax.ppermute(value, "pipe", [(0, 1), (1, 0)])


def z_perm(value, bit):
    return lax.ppermute(value, "z", [(d, d ^ bit) for d in range(NZ)])


def y_far(value):
    return lax.ppermute(value, "yh", [(0, 1), (1, 0)])


def y_far_swap(value):
    return lax.ppermute(value, ("yh", "pipe"), [(0, 3), (1, 2), (2, 1), (3, 0)])


def cut_weight(weight, columns):
    count = columns.shape[0]
    depth, width = weight.shape[0], weight.shape[1] // NT // 2

    def kernel(columns_ref, w_ref, out_ref, sems):
        copies = []
        for i in range(count):
            at = pl.multiple_of(columns_ref[i] * width, width)
            copies.append(
                pltpu.make_async_copy(w_ref.at[:, pl.ds(at, width)], out_ref.at[i], sems.at[i])
            )
        for copy in copies:
            copy.start()
        for copy in copies:
            copy.wait()

    return pl.pallas_call(
        kernel,
        in_specs=[pl.BlockSpec(memory_space=pltpu.SMEM), pl.BlockSpec(memory_space=pl.ANY)],
        out_specs=pl.BlockSpec(memory_space=pltpu.VMEM),
        out_shape=jax.ShapeDtypeStruct((count, depth, width), weight.dtype),
        scratch_shapes=[pltpu.SemaphoreType.DMA((count,))],
        compiler_params=pltpu.CompilerParams(vmem_limit_bytes=VMEM),
        cost_estimate=SMALL,
    )(columns, weight)


def project(rows, weight, got, own, columns, jobs, shapes, after=()):
    count, depth = len(jobs), rows[0].shape[1]
    width = got[0].shape[2]
    n_rows, many, n_out = len(rows), len(got), len(shapes)
    table = jnp.concatenate([own.astype(jnp.int32)[None], columns])

    def kernel(table_ref, w_ref, *rest):
        rest = rest[len(after) :]
        got_refs, rest = rest[:many], rest[many:]
        row_refs, outs = rest[:n_rows], rest[n_rows : n_rows + n_out]
        blocks, sems = rest[n_rows + n_out :]
        mine = table_ref[0] > 0

        @pl.when(mine)
        def _():
            for i in range(count):
                at = pl.multiple_of(table_ref[1 + i] * width, width)
                pltpu.make_async_copy(
                    w_ref.at[:, pl.ds(at, width)], blocks.at[i], sems.at[i]
                ).start()

        @pl.when(jnp.logical_not(mine))
        def _():
            for i in range(count):
                pltpu.make_async_copy(
                    got_refs[i % many].at[i // many], blocks.at[i], sems.at[i]
                ).start()

        for i, job in enumerate(jobs):
            pltpu.make_async_copy(got_refs[0].at[0], blocks.at[i], sems.at[i]).wait()
            for r, places in job:
                y = jnp.dot(row_refs[r][...], blocks[i], preferred_element_type=F32).astype(BF)
                half = y.shape[0] // 2
                for h, (o, at) in enumerate(places):
                    outs[o][at] = y[h * half : (h + 1) * half]

    out_shapes = [jax.ShapeDtypeStruct((*s, width), BF) for s in shapes]
    vmem = pl.BlockSpec(memory_space=pltpu.VMEM)
    anywhere = pl.BlockSpec(memory_space=pl.ANY)
    return pl.pallas_call(
        kernel,
        in_specs=[pl.BlockSpec(memory_space=pltpu.SMEM)]
        + [anywhere] * (1 + len(after) + many)
        + [vmem] * n_rows,
        out_specs=[vmem] * n_out,
        out_shape=out_shapes,
        scratch_shapes=[
            pltpu.VMEM((count, depth, width), BF),
            pltpu.SemaphoreType.DMA((count,)),
        ],
        compiler_params=pltpu.CompilerParams(vmem_limit_bytes=VMEM),
        cost_estimate=SMALL,
    )(table, weight, *after, *got, *rows)


def ring_first(first_p, first_m):
    return tensor_perm(first_p, x_by(1)), tensor_perm(first_m, x_by(-1))


def ring_second(got, next_p, next_m, own0, own1):
    got_p, got_m = got
    n = got_p.shape[0] // 2
    last_p = tensor_perm((f32(next_p) + f32(got_p[:n])).astype(BF), x_by(1))
    last_m = tensor_perm((f32(next_m) + f32(got_m[:n])).astype(BF), x_by(-1))
    h0 = f32(own0) + f32(got_m[n:]) + f32(last_p)
    h1 = f32(own1) + f32(got_p[n:]) + f32(last_m)
    return (last_p, last_m), h0, h1


PLACES = [((0, 0), (1, 0)), ((2, 0), (0, 1)), ((1, 1), (3, 0)), ((4, 0), (4, 1))]
FLAT = [0, 2, 4, 5, 6]


def project_first(rows_a, weight, got_other, own, columns_other, after):
    jobs = [[(0, tuple((0, FLAT[o] + at) for o, at in places))] for places in PLACES]
    shape = (8, rows_a.shape[0] // 2)
    jobs = (jobs, [shape], after)
    return project([rows_a], weight, [got_other], own, columns_other, *jobs)[0]


def project_rest(rows_a, rows_b, weight, got_other, got_mine, own, columns, after):
    columns = jnp.stack(columns, axis=1).reshape(-1)
    jobs = []
    for places in PLACES:
        mine, other = (tuple((o, 2 * at + w) for o, at in places) for w in range(2))
        jobs.append([(0, mine), (1, tuple((5 + o, at) for o, at in places))])
        jobs.append([(0, other)])
    half_a, half_b = rows_a.shape[0] // 2, rows_b.shape[0] // 2
    shapes = [(n, half_b) for n in (4, 4, 2, 2, 4)] + [(n, half_a) for n in (2, 2, 1, 1, 2)]
    jobs = (jobs, shapes, after)
    return project([rows_b, rows_a], weight, [got_mine, got_other], own, columns, *jobs)


def combine_away(own, got_p, got_m, last_p, last_m, after):
    rows, width = own.shape[1:]

    def kernel(own_ref, gp, gm, lp, lm, *rest):
        out = rest[-1]
        out[:rows] = (f32(own_ref[1]) + f32(gm[3]) + f32(lp[1])).astype(BF)
        out[rows:] = (f32(own_ref[3]) + f32(gp[3]) + f32(lm[1])).astype(BF)

    vmem = pl.BlockSpec(memory_space=pltpu.VMEM)
    return pl.pallas_call(
        kernel,
        in_specs=[vmem] * 5 + [pl.BlockSpec(memory_space=pl.ANY)] * len(after),
        out_specs=vmem,
        out_shape=jax.ShapeDtypeStruct((2 * rows, width), BF),
        compiler_params=pltpu.CompilerParams(vmem_limit_bytes=16 * 1024 * 1024),
        cost_estimate=SMALL,
    )(own, got_p, got_m, last_p, last_m, *after)


def reduce_projection(outs, got_y, got_b, after=()):
    width = got_y.shape[2]
    b_np, b_nm, b_own = outs[2:5]
    a_fp, a_fm, a_np, a_nm, a_own = outs[5:]
    got_b = tied(got_b, got_y)
    last_b, b0, b1 = ring_second(got_b, b_np, b_nm, b_own[:2], b_own[2:])
    add = lambda part, at: f32(part) + f32(got_y[at : at + part.shape[0]])
    got_a = ring_first(add(a_fp, 0).astype(BF), add(a_fm, 2).astype(BF))
    if after:
        sent = onward((a_np, a_nm), (got_y[4:5], got_y[5:6]), got_a, after)
        last_p, last_m = tensor_perm(sent[0], x_by(1)), tensor_perm(sent[1], x_by(-1))
        a0 = add(a_own[:1], 6) + f32(got_a[1][1:]) + f32(last_p)
        a1 = add(a_own[1:], 7) + f32(got_a[0][1:]) + f32(last_m)
        away = combine_away(b_own, *got_b, *last_b, after)
    else:
        _, a0, a1 = ring_second(
            got_a, add(a_np, 4), add(a_nm, 5), add(a_own[:1], 6), add(a_own[1:], 7)
        )
        away = jnp.concatenate([b0[1], b1[1]], axis=0).astype(BF)
    got_b = tensor_perm(away, y_other)
    sum_b = jnp.concatenate([b0[0], b1[0]], axis=0) + f32(got_b)
    sum_a = jnp.concatenate([a0[0], a1[0]], axis=0)
    return sum_a.reshape(-1, width), sum_b


def square_sum(rows):
    wide = f32(rows)
    return jnp.sum(wide * wide, axis=-1).reshape(-1, 128)


def tied(value, after):
    return lax.optimization_barrier((value, after))[0]


def gram_parts(normed, captured, ids, pipe, blocks, block, total_tokens, n_out, after):
    micro = captured.shape[0]
    rows, width = normed.shape
    each, sub = rows // micro, block // 2
    count = blocks * (blocks + 1) // 2
    slots = ids.shape[0] // NZ
    many = NZ // n_out

    def kernel(cap_ref, ids_ref, pipe_ref, n_ref, *rest):
        rest = rest[len(after) :]
        outs, left, grams = rest[:n_out], rest[n_out], rest[n_out + 1]
        live = cap_ref[0]
        for m in range(1, micro):
            live = live + cap_ref[m]
        for m in range(micro):
            part = pl.ds(m * each, each)
            left[part] = (f32(n_ref[part]) * cap_ref[m]).astype(BF)
        scale = 1.0 / jnp.full((1, 1), live * total_tokens, F32)
        b = 0
        for i in range(blocks):
            g = lax.dot_general(
                left[:, i * block : (i + 1) * block],
                n_ref[:, i * block :],
                (((0,), (0,)), ((), ())),
                preferred_element_type=F32,
            )
            g = g * scale
            for j in range(blocks - i):
                grams[b] = g[:, j * block : (j + 1) * block]
                b += 1
        at = pl.ds(pl.multiple_of(pipe_ref[0] * sub, sub), sub)
        for k in range(NZ):
            for i in range(slots):
                part = grams[ids_ref[k * slots + i], at, :].astype(BF)
                outs[k // many][k % many, i] = part

    smem = pl.BlockSpec(memory_space=pltpu.SMEM)
    vmem = pl.BlockSpec(memory_space=pltpu.VMEM)
    out_shape = [jax.ShapeDtypeStruct((many, slots, sub, block), BF)] * n_out
    return pl.pallas_call(
        kernel,
        in_specs=[smem, smem, smem, vmem] + [pl.BlockSpec(memory_space=pl.ANY)] * len(after),
        out_specs=[vmem] * n_out,
        out_shape=out_shape,
        scratch_shapes=[
            pltpu.VMEM((rows, width), BF),
            pltpu.VMEM((count, block, block), F32),
        ],
        compiler_params=pltpu.CompilerParams(vmem_limit_bytes=VMEM),
        cost_estimate=SMALL,
    )(captured, ids, pipe[None], normed, *after)


def factor_parts(rows, squares, gain, captured, table, pipe, block, after):
    width = rows.shape[1]
    scale = lax.rsqrt(squares / (width * NT) + EPS).reshape(-1, 1)
    normed = (f32(rows) * scale * gain).astype(BF)
    tokens = rows.shape[0] // captured.shape[0] * NDP
    ids = table.reshape(-1)
    return gram_parts(
        normed, captured, ids, pipe, width // block, block, float(tokens), 2, after
    )


def fold(keep, got, after):
    half = keep.shape[0] // 2
    shape = (half, *keep.shape[1:])

    def kernel(keep_ref, got_ref, *rest):
        left, right = rest[len(after) :]
        for i in range(half):
            left[i] = f32(keep_ref[i]) + f32(got_ref[i])
            right[i] = (f32(keep_ref[half + i]) + f32(got_ref[half + i])).astype(BF)

    vmem = pl.BlockSpec(memory_space=pltpu.VMEM)
    return pl.pallas_call(
        kernel,
        in_specs=[vmem, vmem] + [pl.BlockSpec(memory_space=pl.ANY)] * len(after),
        out_specs=[vmem, vmem],
        out_shape=[jax.ShapeDtypeStruct(shape, F32), jax.ShapeDtypeStruct(shape, BF)],
        compiler_params=pltpu.CompilerParams(vmem_limit_bytes=16 * 1024 * 1024),
        cost_estimate=SMALL,
    )(keep, got, *after)


def plus(a, b, after):
    def kernel(a_ref, b_ref, *rest):
        rest[-1][...] = a_ref[...] + b_ref[...]

    vmem = pl.BlockSpec(memory_space=pltpu.VMEM)
    return pl.pallas_call(
        kernel,
        in_specs=[vmem, vmem] + [pl.BlockSpec(memory_space=pl.ANY)] * len(after),
        out_specs=vmem,
        out_shape=jax.ShapeDtypeStruct(a.shape, F32),
        compiler_params=pltpu.CompilerParams(vmem_limit_bytes=16 * 1024 * 1024),
        cost_estimate=SMALL,
    )(a, b, *after)


def onward(own, got_y, got, after):
    def kernel(*refs):
        ins, outs = refs[:6], refs[-2:]
        for i in range(2):
            o, y, g = ins[3 * i : 3 * i + 3]
            outs[i][...] = (f32(o[...]) + f32(y[...]) + f32(g[:1])).astype(BF)

    vmem = pl.BlockSpec(memory_space=pltpu.VMEM)
    ins = [v for i in range(2) for v in (own[i], got_y[i], got[i])]
    return pl.pallas_call(
        kernel,
        in_specs=[vmem] * 6 + [pl.BlockSpec(memory_space=pl.ANY)] * len(after),
        out_specs=[vmem] * 2,
        out_shape=[jax.ShapeDtypeStruct(own[0].shape, BF)] * 2,
        compiler_params=pltpu.CompilerParams(vmem_limit_bytes=16 * 1024 * 1024),
        cost_estimate=SMALL,
    )(*ins, *after)


def local(section_input, gain, weight, old_factor, slot_table, capture):
    pipe = lax.axis_index("pipe")
    t = lax.axis_index("tensor")
    z, yh = lax.axis_index("z"), lax.axis_index("yh")
    yl, x = t // NX, t % NX
    first = pipe == 0
    micro, each, width = section_input.shape
    half = width // 2
    w = weight[0]
    old = old_factor[0, 0]
    capacity, block, _ = old.shape
    x0 = section_input.reshape(micro * each, width)

    def pick(a, b):
        return jnp.where(first, a, b)

    ring = jnp.stack([(x + 2) % NX, (x + 1) % NX, (x + 3) % NX, x])
    other, mine = 2 * ((1 - yl) * NX + ring), 2 * (yl * NX + ring)
    got_other = swap(cut_weight(w, other + 1 - pipe))
    got_mine = swap(cut_weight(w, mine + 1 - pipe))
    params = jnp.concatenate([gain[0], capture[0].astype(F32)])
    away = swap(params)
    params = (pick(params, away), pick(away, params))
    gains = [v[:width] for v in params]
    caps = [v[width:] for v in params]
    table = jnp.maximum(slot_table, 0).reshape(NZ, NYH, capacity)
    table = jnp.where(yh == 0, table, table[:, ::-1])
    near = table
    for bit in (4, 2, 1):
        parts = near.reshape(NZ // (2 * bit), 2, bit, NYH, capacity)
        near = jnp.where(z & bit > 0, parts[:, ::-1], parts).reshape(table.shape)
    near = near.reshape(2, 2, 2, NYH, capacity).transpose(2, 1, 0, 3, 4)

    def begin(s, rows_a, after=()):
        rows_a = (f32(rows_a) * gains[s]).astype(BF)
        sent = project_first(rows_a, w, got_other, pipe == s, other + pipe, after)
        return rows_a, sent, tensor_perm(sent, y_other)

    def rest(s, rows_a, rows_b, after=()):
        rows_b = (f32(rows_b) * gains[s]).astype(BF)
        columns = (mine + pipe, other + pipe)
        return project_rest(rows_a, rows_b, w, got_other, got_mine, pipe == s, columns, after)

    def finish(rows, squares, total):
        part = lax.dynamic_slice_in_dim(rows, pipe * half, half, 1)
        scale = lax.rsqrt(squares / (width * NT) + EPS)[:, None]
        part = (f32(part) + total * scale).astype(BF)
        other = swap(part)
        return jnp.concatenate([pick(part, other), pick(other, part)], axis=1)

    side, over = lambda t: t ^ 1, lambda t: t ^ 2
    squares = square_sum(x0)
    squares = squares + tensor_perm(squares, y_other)
    squares = squares + tensor_perm(squares, side)
    rows_a, sent, got_y = begin(0, x0[:ROWS_A])
    squares = tied(squares, sent)
    squares0 = squares + tensor_perm(squares, over)
    flat0 = squares0.reshape(-1)
    outs = rest(0, rows_a, x0[ROWS_A:])
    keep, send = factor_parts(x0, squares0, gains[0], caps[0], near, pipe, block, outs[:1])
    got_z = z_perm(send, 1)
    sum_a, sum_b = reduce_projection(outs, got_y, ring_first(*outs[:2]))
    x1a = finish(x0[:ROWS_A], flat0[:ROWS_A], sum_a)
    x1b = finish(x0[ROWS_A:], flat0[ROWS_A:], sum_b)
    keep0, send0 = fold(keep, got_z, [x1a])
    got_z0 = z_perm(send0, 2)

    rows_a, sent, got_y = begin(1, x1a)
    x1 = jnp.concatenate([x1a, x1b], axis=0)
    squares = square_sum(x1)
    got_squares = tensor_perm(squares, side)
    squares = plus(squares, got_squares, [sent])
    got_squares = tensor_perm(squares, over)
    outs = rest(1, rows_a, x1b, [squares, send0])
    keep0, send0 = fold(keep0, got_z0, outs[:1])
    squares = plus(squares, got_squares, outs[:1])
    squares1 = squares + tensor_perm(squares, y_other)
    flat1 = squares1.reshape(-1)
    got_b = ring_first(*outs[:2])
    got_z0 = z_perm(send0, 4)
    tot0 = keep0[0] + f32(got_z0[0])
    waits = [*got_b, got_z0]
    keep, send = factor_parts(x1, squares1, gains[1], caps[1], near, pipe, block, waits)
    keep, send = fold(keep, z_perm(send, 1), [])
    got_z = z_perm(send, 2)
    sum_a, sum_b = reduce_projection(outs, got_y, got_b, [keep])
    keep, send = fold(keep, got_z, [])
    tot1 = keep[0] + f32(z_perm(send, 4)[0])
    x2 = finish(x1, flat1, jnp.concatenate([sum_a, sum_b], axis=0))
    out = pick(x1, x2).reshape(1, micro, each, width)
    here, away = pick(tot0, tot1), pick(tot1, tot0).astype(BF)
    own_rows = here[:capacity] + f32(y_far(here[capacity:].astype(BF)))
    their_rows = f32(swap(away[:capacity])) + f32(y_far_swap(away[capacity:]))
    blocks = [pick(own_rows, their_rows), pick(their_rows, own_rows)]
    blocks = jnp.concatenate(blocks, axis=1)
    own = lax.dynamic_slice_in_dim(slot_table, (z * NYH + yh) * capacity, capacity)
    new = jnp.where(
        (own >= 0)[:, None, None], DECAY * old + (1.0 - DECAY) * blocks, jnp.float32(0.0)
    )
    return (out, new[None, None])


def solution(mesh):
    devices = mesh.devices.reshape(NZ, NYH, 2, NT)
    fine = jax.sharding.Mesh(devices, ("z", "yh", "pipe", "tensor"))
    dp = ("z", "yh")
    placed = (
        P(None, dp, "tensor"),
        P("pipe", "tensor"),
        P("pipe", "tensor", None),
        P("pipe", "tensor", dp, None, None),
        P(),
        P("pipe", None),
    )
    return jax.shard_map(
        local,
        mesh=fine,
        in_specs=placed,
        out_specs=(P("pipe", None, dp, "tensor"), P("pipe", "tensor", dp, None, None)),
        check_vma=False,
    )
```

```python
import jax
import jax.numpy as jnp
from jax import lax
from jax.experimental import pallas as pl
from jax.experimental.pallas import tpu as pltpu
from jax.sharding import PartitionSpec as P

EPS = 1e-06
DECAY = 0.9
BF = jnp.bfloat16
F32 = jnp.float32
NX, NYL, NZ, NYH = 4, 2, 8, 2
NT = NX * NYL
NDP = NZ * NYH
ROWS_A = 224
VMEM = 48 * 1024 * 1024
SMALL = pl.CostEstimate(flops=1024, bytes_accessed=1024, transcendentals=0)


def f32(v):
    return v.astype(F32)


def tensor_perm(value, to):
    return lax.ppermute(value, "tensor", [(t, to(t)) for t in range(NT)])


def x_by(k):
    return lambda t: (t // NX) * NX + (t % NX + k) % NX


def y_other(t):
    return t ^ NX


def swap(value):
    return lax.ppermute(value, "pipe", [(0, 1), (1, 0)])


def z_perm(value, bit):
    return lax.ppermute(value, "z", [(d, d ^ bit) for d in range(NZ)])


def y_far(value):
    return lax.ppermute(value, "yh", [(0, 1), (1, 0)])


def cut_weight(weight, columns):
    count = columns.shape[0]
    depth, width = weight.shape[0], weight.shape[1] // NT // 2

    def kernel(columns_ref, w_ref, out_ref, sems):
        copies = []
        for i in range(count):
            at = pl.multiple_of(columns_ref[i] * width, width)
            copies.append(
                pltpu.make_async_copy(w_ref.at[:, pl.ds(at, width)], out_ref.at[i], sems.at[i])
            )
        for copy in copies:
            copy.start()
        for copy in copies:
            copy.wait()

    return pl.pallas_call(
        kernel,
        in_specs=[pl.BlockSpec(memory_space=pltpu.SMEM), pl.BlockSpec(memory_space=pl.ANY)],
        out_specs=pl.BlockSpec(memory_space=pltpu.VMEM),
        out_shape=jax.ShapeDtypeStruct((count, depth, width), weight.dtype),
        scratch_shapes=[pltpu.SemaphoreType.DMA((count,))],
        compiler_params=pltpu.CompilerParams(vmem_limit_bytes=VMEM),
        cost_estimate=SMALL,
    )(columns, weight)


def project(rows, weight, got, own, columns, jobs, shapes, after=()):
    count, depth = len(jobs), rows[0].shape[1]
    width = got[0].shape[2]
    n_rows, many, n_out = len(rows), len(got), len(shapes)
    table = jnp.concatenate([own.astype(jnp.int32)[None], columns])

    def kernel(table_ref, w_ref, *rest):
        rest = rest[len(after) :]
        got_refs, rest = rest[:many], rest[many:]
        row_refs, outs = rest[:n_rows], rest[n_rows : n_rows + n_out]
        blocks, sems = rest[n_rows + n_out :]
        mine = table_ref[0] > 0

        @pl.when(mine)
        def _():
            for i in range(count):
                at = pl.multiple_of(table_ref[1 + i] * width, width)
                pltpu.make_async_copy(
                    w_ref.at[:, pl.ds(at, width)], blocks.at[i], sems.at[i]
                ).start()

        @pl.when(jnp.logical_not(mine))
        def _():
            for i in range(count):
                pltpu.make_async_copy(
                    got_refs[i % many].at[i // many], blocks.at[i], sems.at[i]
                ).start()

        for i, job in enumerate(jobs):
            pltpu.make_async_copy(got_refs[0].at[0], blocks.at[i], sems.at[i]).wait()
            for r, places in job:
                y = jnp.dot(row_refs[r][...], blocks[i], preferred_element_type=F32).astype(BF)
                half = y.shape[0] // 2
                for h, (o, at) in enumerate(places):
                    outs[o][at] = y[h * half : (h + 1) * half]

    out_shapes = [jax.ShapeDtypeStruct((*s, width), BF) for s in shapes]
    vmem = pl.BlockSpec(memory_space=pltpu.VMEM)
    anywhere = pl.BlockSpec(memory_space=pl.ANY)
    return pl.pallas_call(
        kernel,
        in_specs=[pl.BlockSpec(memory_space=pltpu.SMEM)]
        + [anywhere] * (1 + len(after) + many)
        + [vmem] * n_rows,
        out_specs=[vmem] * n_out,
        out_shape=out_shapes,
        scratch_shapes=[
            pltpu.VMEM((count, depth, width), BF),
            pltpu.SemaphoreType.DMA((count,)),
        ],
        compiler_params=pltpu.CompilerParams(vmem_limit_bytes=VMEM),
        cost_estimate=SMALL,
    )(table, weight, *after, *got, *rows)


def ring_first(first_p, first_m):
    return tensor_perm(first_p, x_by(1)), tensor_perm(first_m, x_by(-1))


def ring_second(got, next_p, next_m, own0, own1):
    got_p, got_m = got
    n = got_p.shape[0] // 2
    last_p = tensor_perm((f32(next_p) + f32(got_p[:n])).astype(BF), x_by(1))
    last_m = tensor_perm((f32(next_m) + f32(got_m[:n])).astype(BF), x_by(-1))
    h0 = f32(own0) + f32(got_m[n:]) + f32(last_p)
    h1 = f32(own1) + f32(got_p[n:]) + f32(last_m)
    return (last_p, last_m), h0, h1


PLACES = [((0, 0), (1, 0)), ((2, 0), (0, 1)), ((1, 1), (3, 0)), ((4, 0), (4, 1))]
FLAT = [0, 2, 4, 5, 6]


def project_first(rows_a, weight, got_other, own, columns_other, after):
    jobs = [[(0, tuple((0, FLAT[o] + at) for o, at in places))] for places in PLACES]
    shape = (8, rows_a.shape[0] // 2)
    jobs = (jobs, [shape], after)
    return project([rows_a], weight, [got_other], own, columns_other, *jobs)[0]


def project_rest(rows_a, rows_b, weight, got_other, got_mine, own, columns, after):
    columns = jnp.stack(columns, axis=1).reshape(-1)
    jobs = []
    for places in PLACES:
        mine, other = (tuple((o, 2 * at + w) for o, at in places) for w in range(2))
        jobs.append([(0, mine), (1, tuple((5 + o, at) for o, at in places))])
        jobs.append([(0, other)])
    half_a, half_b = rows_a.shape[0] // 2, rows_b.shape[0] // 2
    shapes = [(n, half_b) for n in (4, 4, 2, 2, 4)] + [(n, half_a) for n in (2, 2, 1, 1, 2)]
    jobs = (jobs, shapes, after)
    return project([rows_b, rows_a], weight, [got_mine, got_other], own, columns, *jobs)


def combine_away(own, got_p, got_m, last_p, last_m, after):
    rows, width = own.shape[1:]

    def kernel(own_ref, gp, gm, lp, lm, *rest):
        out = rest[-1]
        out[:rows] = (f32(own_ref[1]) + f32(gm[3]) + f32(lp[1])).astype(BF)
        out[rows:] = (f32(own_ref[3]) + f32(gp[3]) + f32(lm[1])).astype(BF)

    vmem = pl.BlockSpec(memory_space=pltpu.VMEM)
    return pl.pallas_call(
        kernel,
        in_specs=[vmem] * 5 + [pl.BlockSpec(memory_space=pl.ANY)] * len(after),
        out_specs=vmem,
        out_shape=jax.ShapeDtypeStruct((2 * rows, width), BF),
        compiler_params=pltpu.CompilerParams(vmem_limit_bytes=16 * 1024 * 1024),
        cost_estimate=SMALL,
    )(own, got_p, got_m, last_p, last_m, *after)


def reduce_projection(outs, got_y, got_b, after=(), later=()):
    width = got_y.shape[2]
    b_np, b_nm, b_own = outs[2:5]
    a_fp, a_fm, a_np, a_nm, a_own = outs[5:]
    got_b = tied(got_b, got_y)
    last_b, b0, b1 = ring_second(got_b, b_np, b_nm, b_own[:2], b_own[2:])
    add = lambda part, at: f32(part) + f32(got_y[at : at + part.shape[0]])
    got_a = ring_first(add(a_fp, 0).astype(BF), add(a_fm, 2).astype(BF))
    if after:
        sent = onward((a_np, a_nm), (got_y[4:5], got_y[5:6]), got_a, after)
        last_p, last_m = tensor_perm(sent[0], x_by(1)), tensor_perm(sent[1], x_by(-1))
        a0 = add(a_own[:1], 6) + f32(got_a[1][1:]) + f32(last_p)
        a1 = add(a_own[1:], 7) + f32(got_a[0][1:]) + f32(last_m)
        away = combine_away(b_own, *got_b, *last_b, later)
    else:
        _, a0, a1 = ring_second(
            got_a, add(a_np, 4), add(a_nm, 5), add(a_own[:1], 6), add(a_own[1:], 7)
        )
        away = jnp.concatenate([b0[1], b1[1]], axis=0).astype(BF)
    got_b = tensor_perm(away, y_other)
    sum_b = jnp.concatenate([b0[0], b1[0]], axis=0) + f32(got_b)
    sum_a = jnp.concatenate([a0[0], a1[0]], axis=0)
    return sum_a.reshape(-1, width), sum_b


def square_sum(rows):
    wide = f32(rows)
    return jnp.sum(wide * wide, axis=-1).reshape(-1, 128)


def tied(value, after):
    return lax.optimization_barrier((value, after))[0]


def gram_parts(normed, captured, ids, pipe, blocks, block, total_tokens, n_out, after):
    micro = captured.shape[0]
    rows, width = normed.shape
    each, sub = rows // micro, block // 2
    count = blocks * (blocks + 1) // 2
    slots = ids.shape[0] // NZ
    many = NZ // n_out

    def kernel(cap_ref, ids_ref, pipe_ref, n_ref, *rest):
        rest = rest[len(after) :]
        outs, left, grams = rest[:n_out], rest[n_out], rest[n_out + 1]
        live = cap_ref[0]
        for m in range(1, micro):
            live = live + cap_ref[m]
        for m in range(micro):
            part = pl.ds(m * each, each)
            left[part] = (f32(n_ref[part]) * cap_ref[m]).astype(BF)
        scale = 1.0 / jnp.full((1, 1), live * total_tokens, F32)
        b = 0
        for i in range(blocks):
            g = lax.dot_general(
                left[:, i * block : (i + 1) * block],
                n_ref[:, i * block :],
                (((0,), (0,)), ((), ())),
                preferred_element_type=F32,
            )
            g = g * scale
            for j in range(blocks - i):
                grams[b] = g[:, j * block : (j + 1) * block]
                b += 1
        at = pl.ds(pl.multiple_of(pipe_ref[0] * sub, sub), sub)
        for k in range(NZ):
            for i in range(slots):
                part = grams[ids_ref[k * slots + i], at, :].astype(BF)
                outs[k // many][k % many, i] = part

    smem = pl.BlockSpec(memory_space=pltpu.SMEM)
    vmem = pl.BlockSpec(memory_space=pltpu.VMEM)
    out_shape = [jax.ShapeDtypeStruct((many, slots, sub, block), BF)] * n_out
    return pl.pallas_call(
        kernel,
        in_specs=[smem, smem, smem, vmem] + [pl.BlockSpec(memory_space=pl.ANY)] * len(after),
        out_specs=[vmem] * n_out,
        out_shape=out_shape,
        scratch_shapes=[
            pltpu.VMEM((rows, width), BF),
            pltpu.VMEM((count, block, block), F32),
        ],
        compiler_params=pltpu.CompilerParams(vmem_limit_bytes=VMEM),
        cost_estimate=SMALL,
    )(captured, ids, pipe[None], normed, *after)


def factor_parts(rows, squares, gain, captured, table, pipe, block, after):
    width = rows.shape[1]
    scale = lax.rsqrt(squares / (width * NT) + EPS).reshape(-1, 1)
    normed = (f32(rows) * scale * gain).astype(BF)
    tokens = rows.shape[0] // captured.shape[0] * NDP
    ids = table.reshape(-1)
    return gram_parts(
        normed, captured, ids, pipe, width // block, block, float(tokens), 2, after
    )


def fold(keep, got, after):
    half = keep.shape[0] // 2
    shape = (half, *keep.shape[1:])

    def kernel(keep_ref, got_ref, *rest):
        left, right = rest[len(after) :]
        for i in range(half):
            left[i] = f32(keep_ref[i]) + f32(got_ref[i])
            right[i] = (f32(keep_ref[half + i]) + f32(got_ref[half + i])).astype(BF)

    vmem = pl.BlockSpec(memory_space=pltpu.VMEM)
    return pl.pallas_call(
        kernel,
        in_specs=[vmem, vmem] + [pl.BlockSpec(memory_space=pl.ANY)] * len(after),
        out_specs=[vmem, vmem],
        out_shape=[jax.ShapeDtypeStruct(shape, F32), jax.ShapeDtypeStruct(shape, BF)],
        compiler_params=pltpu.CompilerParams(vmem_limit_bytes=16 * 1024 * 1024),
        cost_estimate=SMALL,
    )(keep, got, *after)


def plus(a, b, after):
    def kernel(a_ref, b_ref, *rest):
        rest[-1][...] = a_ref[...] + b_ref[...]

    vmem = pl.BlockSpec(memory_space=pltpu.VMEM)
    return pl.pallas_call(
        kernel,
        in_specs=[vmem, vmem] + [pl.BlockSpec(memory_space=pl.ANY)] * len(after),
        out_specs=vmem,
        out_shape=jax.ShapeDtypeStruct(a.shape, F32),
        compiler_params=pltpu.CompilerParams(vmem_limit_bytes=16 * 1024 * 1024),
        cost_estimate=SMALL,
    )(a, b, *after)


def onward(own, got_y, got, after):
    def kernel(*refs):
        ins, outs = refs[:6], refs[-2:]
        for i in range(2):
            o, y, g = ins[3 * i : 3 * i + 3]
            outs[i][...] = (f32(o[...]) + f32(y[...]) + f32(g[:1])).astype(BF)

    vmem = pl.BlockSpec(memory_space=pltpu.VMEM)
    ins = [v for i in range(2) for v in (own[i], got_y[i], got[i])]
    return pl.pallas_call(
        kernel,
        in_specs=[vmem] * 6 + [pl.BlockSpec(memory_space=pl.ANY)] * len(after),
        out_specs=[vmem] * 2,
        out_shape=[jax.ShapeDtypeStruct(own[0].shape, BF)] * 2,
        compiler_params=pltpu.CompilerParams(vmem_limit_bytes=16 * 1024 * 1024),
        cost_estimate=SMALL,
    )(*ins, *after)


def local(section_input, gain, weight, old_factor, slot_table, capture):
    pipe = lax.axis_index("pipe")
    t = lax.axis_index("tensor")
    z, yh = lax.axis_index("z"), lax.axis_index("yh")
    yl, x = t // NX, t % NX
    first = pipe == 0
    micro, each, width = section_input.shape
    half = width // 2
    w = weight[0]
    old = old_factor[0, 0]
    capacity, block, _ = old.shape
    x0 = section_input.reshape(micro * each, width)

    def pick(a, b):
        return jnp.where(first, a, b)

    ring = jnp.stack([(x + 2) % NX, (x + 1) % NX, (x + 3) % NX, x])
    other, mine = 2 * ((1 - yl) * NX + ring), 2 * (yl * NX + ring)
    got_other = swap(cut_weight(w, other + 1 - pipe))
    got_mine = swap(cut_weight(w, mine + 1 - pipe))
    params = jnp.concatenate([gain[0], capture[0].astype(F32)])
    away = swap(params)
    params = (pick(params, away), pick(away, params))
    gains = [v[:width] for v in params]
    caps = [v[width:] for v in params]
    table = jnp.maximum(slot_table, 0).reshape(NZ, NYH, capacity)
    table = jnp.where(yh == 0, table, table[:, ::-1])
    near = table
    for bit in (4, 2, 1):
        parts = near.reshape(NZ // (2 * bit), 2, bit, NYH, capacity)
        near = jnp.where(z & bit > 0, parts[:, ::-1], parts).reshape(table.shape)
    near = near.reshape(2, 2, 2, NYH, capacity).transpose(2, 1, 0, 3, 4)

    def begin(s, rows_a, after=()):
        rows_a = (f32(rows_a) * gains[s]).astype(BF)
        sent = project_first(rows_a, w, got_other, pipe == s, other + pipe, after)
        return rows_a, sent, tensor_perm(sent, y_other)

    def rest(s, rows_a, rows_b, after=()):
        rows_b = (f32(rows_b) * gains[s]).astype(BF)
        columns = (mine + pipe, other + pipe)
        return project_rest(rows_a, rows_b, w, got_other, got_mine, pipe == s, columns, after)

    def finish(rows, squares, total):
        part = lax.dynamic_slice_in_dim(rows, pipe * half, half, 1)
        scale = lax.rsqrt(squares / (width * NT) + EPS)[:, None]
        part = (f32(part) + total * scale).astype(BF)
        other = swap(part)
        return jnp.concatenate([pick(part, other), pick(other, part)], axis=1)

    side, over = lambda t: t ^ 1, lambda t: t ^ 2
    squares = square_sum(x0)
    squares = squares + tensor_perm(squares, y_other)
    squares = squares + tensor_perm(squares, side)
    rows_a, sent, got_y = begin(0, x0[:ROWS_A])
    squares = tied(squares, sent)
    squares0 = squares + tensor_perm(squares, over)
    flat0 = squares0.reshape(-1)
    outs = rest(0, rows_a, x0[ROWS_A:])
    keep, send = factor_parts(x0, squares0, gains[0], caps[0], near, pipe, block, outs[:1])
    got_z = z_perm(send, 1)
    sum_a, sum_b = reduce_projection(outs, got_y, ring_first(*outs[:2]))
    x1a = finish(x0[:ROWS_A], flat0[:ROWS_A], sum_a)
    x1b = finish(x0[ROWS_A:], flat0[ROWS_A:], sum_b)
    keep0, send0 = fold(keep, got_z, [x1a])
    got_z0 = z_perm(send0, 2)

    rows_a, sent, got_y = begin(1, x1a)
    x1 = jnp.concatenate([x1a, x1b], axis=0)
    squares = square_sum(x1)
    got_squares = tensor_perm(squares, side)
    squares = plus(squares, got_squares, [sent])
    got_squares = tensor_perm(squares, over)
    outs = rest(1, rows_a, x1b, [squares, send0])
    keep0, send0 = fold(keep0, got_z0, outs[:1])
    squares = plus(squares, got_squares, outs[:1])
    squares1 = squares + tensor_perm(squares, y_other)
    flat1 = squares1.reshape(-1)
    got_b = ring_first(*outs[:2])
    got_z0 = z_perm(send0, 4)
    tot0 = keep0[0] + f32(got_z0[0])
    waits = [*got_b, got_z0]
    keep, send = factor_parts(x1, squares1, gains[1], caps[1], near, pipe, block, waits)
    keep, send = fold(keep, z_perm(send, 1), [])
    got_z = z_perm(send, 2)
    early = [keep]
    keep, send = fold(keep, got_z, [])
    sum_a, sum_b = reduce_projection(outs, got_y, got_b, [keep], [])
    tot1 = keep[0] + f32(z_perm(send, 4)[0])
    x2 = finish(x1, flat1, jnp.concatenate([sum_a, sum_b], axis=0))
    out = pick(x1, x2).reshape(1, micro, each, width)
    totals = jnp.stack([tot0, tot1])
    totals = totals[:, :capacity] + f32(y_far(totals[:, capacity:].astype(BF)))
    kept, got = pick(totals[0], totals[1]), pick(totals[1], totals[0])
    got = f32(swap(got.astype(BF)))
    blocks = [pick(kept, got), pick(got, kept)]
    blocks = jnp.concatenate(blocks, axis=1)
    own = lax.dynamic_slice_in_dim(slot_table, (z * NYH + yh) * capacity, capacity)
    new = jnp.where(
        (own >= 0)[:, None, None], DECAY * old + (1.0 - DECAY) * blocks, jnp.float32(0.0)
    )
    return (out, new[None, None])


def solution(mesh):
    devices = mesh.devices.reshape(NZ, NYH, 2, NT)
    fine = jax.sharding.Mesh(devices, ("z", "yh", "pipe", "tensor"))
    dp = ("z", "yh")
    placed = (
        P(None, dp, "tensor"),
        P("pipe", "tensor"),
        P("pipe", "tensor", None),
        P("pipe", "tensor", dp, None, None),
        P(),
        P("pipe", None),
    )
    return jax.shard_map(
        local,
        mesh=fine,
        in_specs=placed,
        out_specs=(P("pipe", None, dp, "tensor"), P("pipe", "tensor", dp, None, None)),
        check_vma=False,
    )
```

```python
import jax
import jax.numpy as jnp
from jax import lax
from jax.experimental import pallas as pl
from jax.experimental.pallas import tpu as pltpu
from jax.sharding import PartitionSpec as P

EPS = 1e-06
DECAY = 0.9
BF = jnp.bfloat16
F32 = jnp.float32
NX, NYL, NZ, NYH = 4, 2, 8, 2
NT = NX * NYL
NDP = NZ * NYH
ROWS_A = 224
VMEM = 48 * 1024 * 1024
SMALL = pl.CostEstimate(flops=1024, bytes_accessed=1024, transcendentals=0)


def f32(v):
    return v.astype(F32)


def tensor_perm(value, to):
    return lax.ppermute(value, "tensor", [(t, to(t)) for t in range(NT)])


def x_by(k):
    return lambda t: (t // NX) * NX + (t % NX + k) % NX


def y_other(t):
    return t ^ NX


def swap(value):
    return lax.ppermute(value, "pipe", [(0, 1), (1, 0)])


def z_perm(value, bit):
    return lax.ppermute(value, "z", [(d, d ^ bit) for d in range(NZ)])


def y_far(value):
    return lax.ppermute(value, "yh", [(0, 1), (1, 0)])


def cut_weight(weight, columns):
    count = columns.shape[0]
    depth, width = weight.shape[0], weight.shape[1] // NT // 2

    def kernel(columns_ref, w_ref, out_ref, sems):
        copies = []
        for i in range(count):
            at = pl.multiple_of(columns_ref[i] * width, width)
            copies.append(
                pltpu.make_async_copy(w_ref.at[:, pl.ds(at, width)], out_ref.at[i], sems.at[i])
            )
        for copy in copies:
            copy.start()
        for copy in copies:
            copy.wait()

    return pl.pallas_call(
        kernel,
        in_specs=[pl.BlockSpec(memory_space=pltpu.SMEM), pl.BlockSpec(memory_space=pl.ANY)],
        out_specs=pl.BlockSpec(memory_space=pltpu.VMEM),
        out_shape=jax.ShapeDtypeStruct((count, depth, width), weight.dtype),
        scratch_shapes=[pltpu.SemaphoreType.DMA((count,))],
        compiler_params=pltpu.CompilerParams(vmem_limit_bytes=VMEM),
        cost_estimate=SMALL,
    )(columns, weight)


def project(rows, weight, got, own, columns, jobs, shapes, after=()):
    count, depth = len(jobs), rows[0].shape[1]
    width = got[0].shape[2]
    n_rows, many, n_out = len(rows), len(got), len(shapes)
    table = jnp.concatenate([own.astype(jnp.int32)[None], columns])

    def kernel(table_ref, w_ref, *rest):
        rest = rest[len(after) :]
        got_refs, rest = rest[:many], rest[many:]
        row_refs, outs = rest[:n_rows], rest[n_rows : n_rows + n_out]
        blocks, sems = rest[n_rows + n_out :]
        mine = table_ref[0] > 0

        @pl.when(mine)
        def _():
            for i in range(count):
                at = pl.multiple_of(table_ref[1 + i] * width, width)
                pltpu.make_async_copy(
                    w_ref.at[:, pl.ds(at, width)], blocks.at[i], sems.at[i]
                ).start()

        @pl.when(jnp.logical_not(mine))
        def _():
            for i in range(count):
                pltpu.make_async_copy(
                    got_refs[i % many].at[i // many], blocks.at[i], sems.at[i]
                ).start()

        for i, job in enumerate(jobs):
            pltpu.make_async_copy(got_refs[0].at[0], blocks.at[i], sems.at[i]).wait()
            for r, places in job:
                y = jnp.dot(row_refs[r][...], blocks[i], preferred_element_type=F32).astype(BF)
                half = y.shape[0] // 2
                for h, (o, at) in enumerate(places):
                    outs[o][at] = y[h * half : (h + 1) * half]

    out_shapes = [jax.ShapeDtypeStruct((*s, width), BF) for s in shapes]
    vmem = pl.BlockSpec(memory_space=pltpu.VMEM)
    anywhere = pl.BlockSpec(memory_space=pl.ANY)
    return pl.pallas_call(
        kernel,
        in_specs=[pl.BlockSpec(memory_space=pltpu.SMEM)]
        + [anywhere] * (1 + len(after) + many)
        + [vmem] * n_rows,
        out_specs=[vmem] * n_out,
        out_shape=out_shapes,
        scratch_shapes=[
            pltpu.VMEM((count, depth, width), BF),
            pltpu.SemaphoreType.DMA((count,)),
        ],
        compiler_params=pltpu.CompilerParams(vmem_limit_bytes=VMEM),
        cost_estimate=SMALL,
    )(table, weight, *after, *got, *rows)


def ring_first(first_p, first_m):
    return tensor_perm(first_p, x_by(1)), tensor_perm(first_m, x_by(-1))


def ring_second(got, next_p, next_m, own0, own1):
    got_p, got_m = got
    n = got_p.shape[0] // 2
    last_p = tensor_perm((f32(next_p) + f32(got_p[:n])).astype(BF), x_by(1))
    last_m = tensor_perm((f32(next_m) + f32(got_m[:n])).astype(BF), x_by(-1))
    h0 = f32(own0) + f32(got_m[n:]) + f32(last_p)
    h1 = f32(own1) + f32(got_p[n:]) + f32(last_m)
    return (last_p, last_m), h0, h1


PLACES = [((0, 0), (1, 0)), ((2, 0), (0, 1)), ((1, 1), (3, 0)), ((4, 0), (4, 1))]
FLAT = [0, 2, 4, 5, 6]


def project_first(rows_a, weight, got_other, own, columns_other, after):
    jobs = [[(0, tuple((0, FLAT[o] + at) for o, at in places))] for places in PLACES]
    shape = (8, rows_a.shape[0] // 2)
    jobs = (jobs, [shape], after)
    return project([rows_a], weight, [got_other], own, columns_other, *jobs)[0]


def project_rest(rows_a, rows_b, weight, got_other, got_mine, own, columns, after):
    columns = jnp.stack(columns, axis=1).reshape(-1)
    jobs = []
    for places in PLACES:
        mine, other = (tuple((o, 2 * at + w) for o, at in places) for w in range(2))
        jobs.append([(0, mine), (1, tuple((5 + o, at) for o, at in places))])
        jobs.append([(0, other)])
    half_a, half_b = rows_a.shape[0] // 2, rows_b.shape[0] // 2
    shapes = [(n, half_b) for n in (4, 4, 2, 2, 4)] + [(n, half_a) for n in (2, 2, 1, 1, 2)]
    jobs = (jobs, shapes, after)
    return project([rows_b, rows_a], weight, [got_mine, got_other], own, columns, *jobs)


def combine_away(own, got_p, got_m, last_p, last_m, after):
    rows, width = own.shape[1:]

    def kernel(own_ref, gp, gm, lp, lm, *rest):
        out = rest[-1]
        out[:rows] = (f32(own_ref[1]) + f32(gm[3]) + f32(lp[1])).astype(BF)
        out[rows:] = (f32(own_ref[3]) + f32(gp[3]) + f32(lm[1])).astype(BF)

    vmem = pl.BlockSpec(memory_space=pltpu.VMEM)
    return pl.pallas_call(
        kernel,
        in_specs=[vmem] * 5 + [pl.BlockSpec(memory_space=pl.ANY)] * len(after),
        out_specs=vmem,
        out_shape=jax.ShapeDtypeStruct((2 * rows, width), BF),
        compiler_params=pltpu.CompilerParams(vmem_limit_bytes=16 * 1024 * 1024),
        cost_estimate=SMALL,
    )(own, got_p, got_m, last_p, last_m, *after)


def reduce_projection(outs, got_y, got_b, after=(), later=()):
    width = got_y.shape[2]
    b_np, b_nm, b_own = outs[2:5]
    a_fp, a_fm, a_np, a_nm, a_own = outs[5:]
    got_b = tied(got_b, got_y)
    last_b, b0, b1 = ring_second(got_b, b_np, b_nm, b_own[:2], b_own[2:])
    add = lambda part, at: f32(part) + f32(got_y[at : at + part.shape[0]])
    got_a = ring_first(add(a_fp, 0).astype(BF), add(a_fm, 2).astype(BF))
    if after:
        sent = onward((a_np, a_nm), (got_y[4:5], got_y[5:6]), got_a, after)
        last_p, last_m = tensor_perm(sent[0], x_by(1)), tensor_perm(sent[1], x_by(-1))
        a0 = add(a_own[:1], 6) + f32(got_a[1][1:]) + f32(last_p)
        a1 = add(a_own[1:], 7) + f32(got_a[0][1:]) + f32(last_m)
        away = combine_away(b_own, *got_b, *last_b, later)
    else:
        _, a0, a1 = ring_second(
            got_a, add(a_np, 4), add(a_nm, 5), add(a_own[:1], 6), add(a_own[1:], 7)
        )
        away = jnp.concatenate([b0[1], b1[1]], axis=0).astype(BF)
    got_b = tensor_perm(away, y_other)
    sum_b = jnp.concatenate([b0[0], b1[0]], axis=0) + f32(got_b)
    sum_a = jnp.concatenate([a0[0], a1[0]], axis=0)
    return sum_a.reshape(-1, width), sum_b


def square_sum(rows):
    wide = f32(rows)
    return jnp.sum(wide * wide, axis=-1).reshape(-1, 128)


def tied(value, after):
    return lax.optimization_barrier((value, after))[0]


def gram_parts(normed, captured, ids, pipe, blocks, block, total_tokens, n_out, after):
    micro = captured.shape[0]
    rows, width = normed.shape
    each, sub = rows // micro, block // 2
    count = blocks * (blocks + 1) // 2
    slots = ids.shape[0] // NZ
    many = NZ // n_out

    def kernel(cap_ref, ids_ref, pipe_ref, n_ref, *rest):
        rest = rest[len(after) :]
        outs, left, grams = rest[:n_out], rest[n_out], rest[n_out + 1]
        live = cap_ref[0]
        for m in range(1, micro):
            live = live + cap_ref[m]
        for m in range(micro):
            part = pl.ds(m * each, each)
            left[part] = (f32(n_ref[part]) * cap_ref[m]).astype(BF)
        scale = 1.0 / jnp.full((1, 1), live * total_tokens, F32)
        b = 0
        for i in range(blocks):
            g = lax.dot_general(
                left[:, i * block : (i + 1) * block],
                n_ref[:, i * block :],
                (((0,), (0,)), ((), ())),
                preferred_element_type=F32,
            )
            g = g * scale
            for j in range(blocks - i):
                grams[b] = g[:, j * block : (j + 1) * block]
                b += 1
        at = pl.ds(pl.multiple_of(pipe_ref[0] * sub, sub), sub)
        for k in range(NZ):
            for i in range(slots):
                part = grams[ids_ref[k * slots + i], at, :].astype(BF)
                outs[k // many][k % many, i] = part

    smem = pl.BlockSpec(memory_space=pltpu.SMEM)
    vmem = pl.BlockSpec(memory_space=pltpu.VMEM)
    out_shape = [jax.ShapeDtypeStruct((many, slots, sub, block), BF)] * n_out
    return pl.pallas_call(
        kernel,
        in_specs=[smem, smem, smem, vmem] + [pl.BlockSpec(memory_space=pl.ANY)] * len(after),
        out_specs=[vmem] * n_out,
        out_shape=out_shape,
        scratch_shapes=[
            pltpu.VMEM((rows, width), BF),
            pltpu.VMEM((count, block, block), F32),
        ],
        compiler_params=pltpu.CompilerParams(vmem_limit_bytes=VMEM),
        cost_estimate=SMALL,
    )(captured, ids, pipe[None], normed, *after)


def factor_parts(rows, squares, gain, captured, table, pipe, block, after):
    width = rows.shape[1]
    scale = lax.rsqrt(squares / (width * NT) + EPS).reshape(-1, 1)
    normed = (f32(rows) * scale * gain).astype(BF)
    tokens = rows.shape[0] // captured.shape[0] * NDP
    ids = table.reshape(-1)
    return gram_parts(
        normed, captured, ids, pipe, width // block, block, float(tokens), 2, after
    )


def fold(keep, got, after):
    half = keep.shape[0] // 2
    shape = (half, *keep.shape[1:])

    def kernel(keep_ref, got_ref, *rest):
        left, right = rest[len(after) :]
        for i in range(half):
            left[i] = f32(keep_ref[i]) + f32(got_ref[i])
            right[i] = (f32(keep_ref[half + i]) + f32(got_ref[half + i])).astype(BF)

    vmem = pl.BlockSpec(memory_space=pltpu.VMEM)
    return pl.pallas_call(
        kernel,
        in_specs=[vmem, vmem] + [pl.BlockSpec(memory_space=pl.ANY)] * len(after),
        out_specs=[vmem, vmem],
        out_shape=[jax.ShapeDtypeStruct(shape, F32), jax.ShapeDtypeStruct(shape, BF)],
        compiler_params=pltpu.CompilerParams(vmem_limit_bytes=16 * 1024 * 1024),
        cost_estimate=SMALL,
    )(keep, got, *after)


def plus(a, b, after):
    def kernel(a_ref, b_ref, *rest):
        rest[-1][...] = a_ref[...] + b_ref[...]

    vmem = pl.BlockSpec(memory_space=pltpu.VMEM)
    return pl.pallas_call(
        kernel,
        in_specs=[vmem, vmem] + [pl.BlockSpec(memory_space=pl.ANY)] * len(after),
        out_specs=vmem,
        out_shape=jax.ShapeDtypeStruct(a.shape, F32),
        compiler_params=pltpu.CompilerParams(vmem_limit_bytes=16 * 1024 * 1024),
        cost_estimate=SMALL,
    )(a, b, *after)


def onward(own, got_y, got, after):
    def kernel(*refs):
        ins, outs = refs[:6], refs[-2:]
        for i in range(2):
            o, y, g = ins[3 * i : 3 * i + 3]
            outs[i][...] = (f32(o[...]) + f32(y[...]) + f32(g[:1])).astype(BF)

    vmem = pl.BlockSpec(memory_space=pltpu.VMEM)
    ins = [v for i in range(2) for v in (own[i], got_y[i], got[i])]
    return pl.pallas_call(
        kernel,
        in_specs=[vmem] * 6 + [pl.BlockSpec(memory_space=pl.ANY)] * len(after),
        out_specs=[vmem] * 2,
        out_shape=[jax.ShapeDtypeStruct(own[0].shape, BF)] * 2,
        compiler_params=pltpu.CompilerParams(vmem_limit_bytes=16 * 1024 * 1024),
        cost_estimate=SMALL,
    )(*ins, *after)


def local(section_input, gain, weight, old_factor, slot_table, capture):
    pipe = lax.axis_index("pipe")
    t = lax.axis_index("tensor")
    z, yh = lax.axis_index("z"), lax.axis_index("yh")
    yl, x = t // NX, t % NX
    first = pipe == 0
    micro, each, width = section_input.shape
    half = width // 2
    w = weight[0]
    old = old_factor[0, 0]
    capacity, block, _ = old.shape
    x0 = section_input.reshape(micro * each, width)

    def pick(a, b):
        return jnp.where(first, a, b)

    ring = jnp.stack([(x + 2) % NX, (x + 1) % NX, (x + 3) % NX, x])
    other, mine = 2 * ((1 - yl) * NX + ring), 2 * (yl * NX + ring)
    got_other = swap(cut_weight(w, other + 1 - pipe))
    got_mine = swap(cut_weight(w, mine + 1 - pipe))
    params = jnp.concatenate([gain[0], capture[0].astype(F32)])
    away = swap(params)
    params = (pick(params, away), pick(away, params))
    gains = [v[:width] for v in params]
    caps = [v[width:] for v in params]
    table = jnp.maximum(slot_table, 0).reshape(NZ, NYH, capacity)
    table = jnp.where(yh == 0, table, table[:, ::-1])
    near = table
    for bit in (4, 2, 1):
        parts = near.reshape(NZ // (2 * bit), 2, bit, NYH, capacity)
        near = jnp.where(z & bit > 0, parts[:, ::-1], parts).reshape(table.shape)
    near = near.reshape(2, 2, 2, NYH, capacity).transpose(2, 1, 0, 3, 4)

    def begin(s, rows_a, after=()):
        rows_a = (f32(rows_a) * gains[s]).astype(BF)
        sent = project_first(rows_a, w, got_other, pipe == s, other + pipe, after)
        return rows_a, sent, tensor_perm(sent, y_other)

    def rest(s, rows_a, rows_b, after=()):
        rows_b = (f32(rows_b) * gains[s]).astype(BF)
        columns = (mine + pipe, other + pipe)
        return project_rest(rows_a, rows_b, w, got_other, got_mine, pipe == s, columns, after)

    def finish(rows, squares, total):
        part = lax.dynamic_slice_in_dim(rows, pipe * half, half, 1)
        scale = lax.rsqrt(squares / (width * NT) + EPS)[:, None]
        part = (f32(part) + total * scale).astype(BF)
        other = swap(part)
        return jnp.concatenate([pick(part, other), pick(other, part)], axis=1)

    side, over = lambda t: t ^ 1, lambda t: t ^ 2
    squares = square_sum(x0)
    squares = squares + tensor_perm(squares, y_other)
    got_squares = tensor_perm(squares, side)
    rows_a, sent, got_y = begin(0, x0[:ROWS_A])
    squares = plus(squares, got_squares, [sent])
    squares0 = squares + tensor_perm(squares, over)
    flat0 = squares0.reshape(-1)
    outs = rest(0, rows_a, x0[ROWS_A:])
    keep, send = factor_parts(x0, squares0, gains[0], caps[0], near, pipe, block, outs[:1])
    got_z = z_perm(send, 1)
    sum_a, sum_b = reduce_projection(outs, got_y, ring_first(*outs[:2]))
    x1a = finish(x0[:ROWS_A], flat0[:ROWS_A], sum_a)
    x1b = finish(x0[ROWS_A:], flat0[ROWS_A:], sum_b)
    keep0, send0 = fold(keep, got_z, [x1a])
    got_z0 = z_perm(send0, 2)

    rows_a, sent, got_y = begin(1, x1a)
    x1 = jnp.concatenate([x1a, x1b], axis=0)
    squares = square_sum(x1)
    got_squares = tensor_perm(squares, side)
    squares = plus(squares, got_squares, [sent])
    got_squares = tensor_perm(squares, over)
    outs = rest(1, rows_a, x1b, [squares, send0])
    keep0, send0 = fold(keep0, got_z0, outs[:1])
    squares = plus(squares, got_squares, outs[:1])
    squares1 = squares + tensor_perm(squares, y_other)
    flat1 = squares1.reshape(-1)
    got_b = ring_first(*outs[:2])
    got_z0 = z_perm(send0, 4)
    tot0 = keep0[0] + f32(got_z0[0])
    waits = [got_z0]
    keep, send = factor_parts(x1, squares1, gains[1], caps[1], near, pipe, block, waits)
    keep, send = fold(keep, z_perm(send, 1), [])
    got_z = z_perm(send, 2)
    early = [keep]
    keep, send = fold(keep, got_z, [])
    sum_a, sum_b = reduce_projection(outs, got_y, got_b, [keep], [])
    tot1 = keep[0] + f32(z_perm(send, 4)[0])
    x2 = finish(x1, flat1, jnp.concatenate([sum_a, sum_b], axis=0))
    out = pick(x1, x2).reshape(1, micro, each, width)
    totals = jnp.stack([tot0, tot1])
    totals = totals[:, :capacity] + f32(y_far(totals[:, capacity:].astype(BF)))
    kept, got = pick(totals[0], totals[1]), pick(totals[1], totals[0])
    got = f32(swap(got.astype(BF)))
    blocks = [pick(kept, got), pick(got, kept)]
    blocks = jnp.concatenate(blocks, axis=1)
    own = lax.dynamic_slice_in_dim(slot_table, (z * NYH + yh) * capacity, capacity)
    new = jnp.where(
        (own >= 0)[:, None, None], DECAY * old + (1.0 - DECAY) * blocks, jnp.float32(0.0)
    )
    return (out, new[None, None])


def solution(mesh):
    devices = mesh.devices.reshape(NZ, NYH, 2, NT)
    fine = jax.sharding.Mesh(devices, ("z", "yh", "pipe", "tensor"))
    dp = ("z", "yh")
    placed = (
        P(None, dp, "tensor"),
        P("pipe", "tensor"),
        P("pipe", "tensor", None),
        P("pipe", "tensor", dp, None, None),
        P(),
        P("pipe", None),
    )
    return jax.shard_map(
        local,
        mesh=fine,
        in_specs=placed,
        out_specs=(P("pipe", None, dp, "tensor"), P("pipe", "tensor", dp, None, None)),
        check_vma=False,
    )
```

```python
import jax
import jax.numpy as jnp
from jax import lax
from jax.experimental import pallas as pl
from jax.experimental.pallas import tpu as pltpu
from jax.sharding import PartitionSpec as P

EPS = 1e-06
DECAY = 0.9
BF = jnp.bfloat16
F32 = jnp.float32
NX, NYL, NZ, NYH = 4, 2, 8, 2
NT = NX * NYL
NDP = NZ * NYH
ROWS_A = 224
VMEM = 48 * 1024 * 1024
SMALL = pl.CostEstimate(flops=1024, bytes_accessed=1024, transcendentals=0)


def f32(v):
    return v.astype(F32)


def tensor_perm(value, to):
    return lax.ppermute(value, "tensor", [(t, to(t)) for t in range(NT)])


def x_by(k):
    return lambda t: (t // NX) * NX + (t % NX + k) % NX


def y_other(t):
    return t ^ NX


def swap(value):
    return lax.ppermute(value, "pipe", [(0, 1), (1, 0)])


def z_perm(value, bit):
    return lax.ppermute(value, "z", [(d, d ^ bit) for d in range(NZ)])


def y_far(value):
    return lax.ppermute(value, "yh", [(0, 1), (1, 0)])


def cut_weight(weight, columns):
    count = columns.shape[0]
    depth, width = weight.shape[0], weight.shape[1] // NT // 2

    def kernel(columns_ref, w_ref, out_ref, sems):
        copies = []
        for i in range(count):
            at = pl.multiple_of(columns_ref[i] * width, width)
            copies.append(
                pltpu.make_async_copy(w_ref.at[:, pl.ds(at, width)], out_ref.at[i], sems.at[i])
            )
        for copy in copies:
            copy.start()
        for copy in copies:
            copy.wait()

    return pl.pallas_call(
        kernel,
        in_specs=[pl.BlockSpec(memory_space=pltpu.SMEM), pl.BlockSpec(memory_space=pl.ANY)],
        out_specs=pl.BlockSpec(memory_space=pltpu.VMEM),
        out_shape=jax.ShapeDtypeStruct((count, depth, width), weight.dtype),
        scratch_shapes=[pltpu.SemaphoreType.DMA((count,))],
        compiler_params=pltpu.CompilerParams(vmem_limit_bytes=VMEM),
        cost_estimate=SMALL,
    )(columns, weight)


def project(rows, weight, got, own, columns, sources, jobs, shapes, after=()):
    count, depth = len(jobs), rows[0].shape[1]
    width = got[0].shape[2]
    n_rows, many, n_out = len(rows), len(got), len(shapes)
    table = jnp.concatenate([own.astype(jnp.int32)[None], columns])

    def kernel(table_ref, w_ref, *rest):
        rest = rest[len(after) :]
        got_refs, rest = rest[:many], rest[many:]
        row_refs, outs = rest[:n_rows], rest[n_rows : n_rows + n_out]
        blocks, sems = rest[n_rows + n_out :]
        mine = table_ref[0] > 0

        @pl.when(mine)
        def _():
            for i in range(count):
                at = pl.multiple_of(table_ref[1 + i] * width, width)
                pltpu.make_async_copy(
                    w_ref.at[:, pl.ds(at, width)], blocks.at[i], sems.at[i]
                ).start()

        @pl.when(jnp.logical_not(mine))
        def _():
            for i in range(count):
                pltpu.make_async_copy(
                    got_refs[sources[i][0]].at[sources[i][1]], blocks.at[i], sems.at[i]
                ).start()

        for i, job in enumerate(jobs):
            pltpu.make_async_copy(got_refs[0].at[0], blocks.at[i], sems.at[i]).wait()
            for r, places in job:
                y = jnp.dot(row_refs[r][...], blocks[i], preferred_element_type=F32).astype(BF)
                half = y.shape[0] // 2
                for h, (o, at) in enumerate(places):
                    outs[o][at] = y[h * half : (h + 1) * half]

    out_shapes = [jax.ShapeDtypeStruct((*s, width), BF) for s in shapes]
    vmem = pl.BlockSpec(memory_space=pltpu.VMEM)
    anywhere = pl.BlockSpec(memory_space=pl.ANY)
    return pl.pallas_call(
        kernel,
        in_specs=[pl.BlockSpec(memory_space=pltpu.SMEM)]
        + [anywhere] * (1 + len(after) + many)
        + [vmem] * n_rows,
        out_specs=[vmem] * n_out,
        out_shape=out_shapes,
        scratch_shapes=[
            pltpu.VMEM((count, depth, width), BF),
            pltpu.SemaphoreType.DMA((count,)),
        ],
        compiler_params=pltpu.CompilerParams(vmem_limit_bytes=VMEM),
        cost_estimate=SMALL,
    )(table, weight, *after, *got, *rows)


def ring_first(first_p, first_m):
    return tensor_perm(first_p, x_by(1)), tensor_perm(first_m, x_by(-1))


def ring_second(got, next_p, next_m, own0, own1):
    got_p, got_m = got
    n = got_p.shape[0] // 2
    last_p = tensor_perm((f32(next_p) + f32(got_p[:n])).astype(BF), x_by(1))
    last_m = tensor_perm((f32(next_m) + f32(got_m[:n])).astype(BF), x_by(-1))
    h0 = f32(own0) + f32(got_m[n:]) + f32(last_p)
    h1 = f32(own1) + f32(got_p[n:]) + f32(last_m)
    return (last_p, last_m), h0, h1


PLACES = [((0, 0), (1, 0)), ((2, 0), (0, 1)), ((1, 1), (3, 0)), ((4, 0), (4, 1))]
FLAT = [0, 2, 4, 5, 6]


def project_first(rows_a, weight, got_other, own, columns_other, after):
    jobs = [[(0, tuple((0, FLAT[o] + at) for o, at in places))] for places in PLACES]
    shape = (8, rows_a.shape[0] // 2)
    sources = [(0, r) for r in range(len(jobs))]
    columns = (columns_other, sources, jobs, [shape], after)
    return project([rows_a], weight, [got_other], own, *columns)[0]


def project_rest(rows_a, rows_b, weight, got_other, got_mine, own, columns, after, split):
    got = [got_mine, got_other]
    half_a, half_b = rows_a.shape[0] // 2, rows_b.shape[0] // 2
    if not split:
        sources, jobs = [(w, r) for r in range(4) for w in range(2)], []
        for w, r in sources:
            job = [(0, tuple((o, 2 * at + w) for o, at in PLACES[r]))]
            if w == 0:
                job.append((1, tuple((5 + o, at) for o, at in PLACES[r])))
            jobs.append(job)
        ids = jnp.stack([columns[w][r] for w, r in sources])
        shapes = [(n, half_b) for n in (4, 4, 2, 2, 4)] + [(n, half_a) for n in (2, 2, 1, 1, 2)]
        return project([rows_b, rows_a], weight, got, own, ids, sources, jobs, shapes, after)
    sources = [(w, r) for r in range(3) for w in range(2)]
    jobs = [[(0, tuple((o, 2 * at + w) for o, at in PLACES[r]))] for w, r in sources]
    ids = jnp.stack([columns[w][r] for w, r in sources])
    shapes = [(n, half_b) for n in (4, 4, 2, 2)]
    first = project([rows_b], weight, got, own, ids, sources, jobs, shapes, after)
    sources = [(1, 3), (0, 3), (0, 0), (0, 1), (0, 2)]
    jobs = []
    for w, r in sources:
        job = [(0, tuple((0, 2 * at + w) for _, at in PLACES[r]))] if r == 3 else []
        if w == 0:
            job.append((1, tuple((1 + o, at) for o, at in PLACES[r])))
        jobs.append(job)
    ids = jnp.stack([columns[w][r] for w, r in sources])
    shapes = [(4, half_b)] + [(n, half_a) for n in (2, 2, 1, 1, 2)]
    second = project([rows_b, rows_a], weight, got, own, ids, sources, jobs, shapes, ())
    return [*first, *second]


def combine_away(own, got_p, got_m, last_p, last_m, after):
    rows, width = own.shape[1:]

    def kernel(own_ref, gp, gm, lp, lm, *rest):
        out = rest[-1]
        out[:rows] = (f32(own_ref[1]) + f32(gm[3]) + f32(lp[1])).astype(BF)
        out[rows:] = (f32(own_ref[3]) + f32(gp[3]) + f32(lm[1])).astype(BF)

    vmem = pl.BlockSpec(memory_space=pltpu.VMEM)
    return pl.pallas_call(
        kernel,
        in_specs=[vmem] * 5 + [pl.BlockSpec(memory_space=pl.ANY)] * len(after),
        out_specs=vmem,
        out_shape=jax.ShapeDtypeStruct((2 * rows, width), BF),
        compiler_params=pltpu.CompilerParams(vmem_limit_bytes=16 * 1024 * 1024),
        cost_estimate=SMALL,
    )(own, got_p, got_m, last_p, last_m, *after)


def reduce_projection(outs, got_y, got_b, after=(), later=()):
    width = got_y.shape[2]
    b_np, b_nm, b_own = outs[2:5]
    a_fp, a_fm, a_np, a_nm, a_own = outs[5:]
    got_b = tied(got_b, got_y)
    last_b, b0, b1 = ring_second(got_b, b_np, b_nm, b_own[:2], b_own[2:])
    add = lambda part, at: f32(part) + f32(got_y[at : at + part.shape[0]])
    got_a = ring_first(add(a_fp, 0).astype(BF), add(a_fm, 2).astype(BF))
    if after:
        sent = onward((a_np, a_nm), (got_y[4:5], got_y[5:6]), got_a, after)
        last_p, last_m = tensor_perm(sent[0], x_by(1)), tensor_perm(sent[1], x_by(-1))
        a0 = add(a_own[:1], 6) + f32(got_a[1][1:]) + f32(last_p)
        a1 = add(a_own[1:], 7) + f32(got_a[0][1:]) + f32(last_m)
        away = combine_away(b_own, *got_b, *last_b, later)
    else:
        _, a0, a1 = ring_second(
            got_a, add(a_np, 4), add(a_nm, 5), add(a_own[:1], 6), add(a_own[1:], 7)
        )
        away = jnp.concatenate([b0[1], b1[1]], axis=0).astype(BF)
    got_b = tensor_perm(away, y_other)
    sum_b = jnp.concatenate([b0[0], b1[0]], axis=0) + f32(got_b)
    sum_a = jnp.concatenate([a0[0], a1[0]], axis=0)
    return sum_a.reshape(-1, width), sum_b


def square_sum(rows):
    wide = f32(rows)
    return jnp.sum(wide * wide, axis=-1).reshape(-1, 128)


def tied(value, after):
    return lax.optimization_barrier((value, after))[0]


def gram_parts(normed, captured, ids, pipe, blocks, block, total_tokens, n_out, after):
    micro = captured.shape[0]
    rows, width = normed.shape
    each, sub = rows // micro, block // 2
    count = blocks * (blocks + 1) // 2
    slots = ids.shape[0] // NZ
    many = NZ // n_out

    def kernel(cap_ref, ids_ref, pipe_ref, n_ref, *rest):
        rest = rest[len(after) :]
        outs, left, grams = rest[:n_out], rest[n_out], rest[n_out + 1]
        live = cap_ref[0]
        for m in range(1, micro):
            live = live + cap_ref[m]
        for m in range(micro):
            part = pl.ds(m * each, each)
            left[part] = (f32(n_ref[part]) * cap_ref[m]).astype(BF)
        scale = 1.0 / jnp.full((1, 1), live * total_tokens, F32)
        b = 0
        for i in range(blocks):
            g = lax.dot_general(
                left[:, i * block : (i + 1) * block],
                n_ref[:, i * block :],
                (((0,), (0,)), ((), ())),
                preferred_element_type=F32,
            )
            g = g * scale
            for j in range(blocks - i):
                grams[b] = g[:, j * block : (j + 1) * block]
                b += 1
        at = pl.ds(pl.multiple_of(pipe_ref[0] * sub, sub), sub)
        for k in range(NZ):
            for i in range(slots):
                part = grams[ids_ref[k * slots + i], at, :].astype(BF)
                outs[k // many][k % many, i] = part

    smem = pl.BlockSpec(memory_space=pltpu.SMEM)
    vmem = pl.BlockSpec(memory_space=pltpu.VMEM)
    out_shape = [jax.ShapeDtypeStruct((many, slots, sub, block), BF)] * n_out
    return pl.pallas_call(
        kernel,
        in_specs=[smem, smem, smem, vmem] + [pl.BlockSpec(memory_space=pl.ANY)] * len(after),
        out_specs=[vmem] * n_out,
        out_shape=out_shape,
        scratch_shapes=[
            pltpu.VMEM((rows, width), BF),
            pltpu.VMEM((count, block, block), F32),
        ],
        compiler_params=pltpu.CompilerParams(vmem_limit_bytes=VMEM),
        cost_estimate=SMALL,
    )(captured, ids, pipe[None], normed, *after)


def factor_parts(rows, squares, gain, captured, table, pipe, block, after):
    width = rows.shape[1]
    scale = lax.rsqrt(squares / (width * NT) + EPS).reshape(-1, 1)
    normed = (f32(rows) * scale * gain).astype(BF)
    tokens = rows.shape[0] // captured.shape[0] * NDP
    ids = table.reshape(-1)
    return gram_parts(
        normed, captured, ids, pipe, width // block, block, float(tokens), 2, after
    )


def fold(keep, got, after):
    half = keep.shape[0] // 2
    shape = (half, *keep.shape[1:])

    def kernel(keep_ref, got_ref, *rest):
        left, right = rest[len(after) :]
        for i in range(half):
            left[i] = f32(keep_ref[i]) + f32(got_ref[i])
            right[i] = (f32(keep_ref[half + i]) + f32(got_ref[half + i])).astype(BF)

    vmem = pl.BlockSpec(memory_space=pltpu.VMEM)
    return pl.pallas_call(
        kernel,
        in_specs=[vmem, vmem] + [pl.BlockSpec(memory_space=pl.ANY)] * len(after),
        out_specs=[vmem, vmem],
        out_shape=[jax.ShapeDtypeStruct(shape, F32), jax.ShapeDtypeStruct(shape, BF)],
        compiler_params=pltpu.CompilerParams(vmem_limit_bytes=16 * 1024 * 1024),
        cost_estimate=SMALL,
    )(keep, got, *after)


def plus(a, b, after):
    def kernel(a_ref, b_ref, *rest):
        rest[-1][...] = a_ref[...] + b_ref[...]

    vmem = pl.BlockSpec(memory_space=pltpu.VMEM)
    return pl.pallas_call(
        kernel,
        in_specs=[vmem, vmem] + [pl.BlockSpec(memory_space=pl.ANY)] * len(after),
        out_specs=vmem,
        out_shape=jax.ShapeDtypeStruct(a.shape, F32),
        compiler_params=pltpu.CompilerParams(vmem_limit_bytes=16 * 1024 * 1024),
        cost_estimate=SMALL,
    )(a, b, *after)


def onward(own, got_y, got, after):
    def kernel(*refs):
        ins, outs = refs[:6], refs[-2:]
        for i in range(2):
            o, y, g = ins[3 * i : 3 * i + 3]
            outs[i][...] = (f32(o[...]) + f32(y[...]) + f32(g[:1])).astype(BF)

    vmem = pl.BlockSpec(memory_space=pltpu.VMEM)
    ins = [v for i in range(2) for v in (own[i], got_y[i], got[i])]
    return pl.pallas_call(
        kernel,
        in_specs=[vmem] * 6 + [pl.BlockSpec(memory_space=pl.ANY)] * len(after),
        out_specs=[vmem] * 2,
        out_shape=[jax.ShapeDtypeStruct(own[0].shape, BF)] * 2,
        compiler_params=pltpu.CompilerParams(vmem_limit_bytes=16 * 1024 * 1024),
        cost_estimate=SMALL,
    )(*ins, *after)


def local(section_input, gain, weight, old_factor, slot_table, capture):
    pipe = lax.axis_index("pipe")
    t = lax.axis_index("tensor")
    z, yh = lax.axis_index("z"), lax.axis_index("yh")
    yl, x = t // NX, t % NX
    first = pipe == 0
    micro, each, width = section_input.shape
    half = width // 2
    w = weight[0]
    old = old_factor[0, 0]
    capacity, block, _ = old.shape
    x0 = section_input.reshape(micro * each, width)

    def pick(a, b):
        return jnp.where(first, a, b)

    ring = jnp.stack([(x + 2) % NX, (x + 1) % NX, (x + 3) % NX, x])
    other, mine = 2 * ((1 - yl) * NX + ring), 2 * (yl * NX + ring)
    got_other = swap(cut_weight(w, other + 1 - pipe))
    got_mine = swap(cut_weight(w, mine + 1 - pipe))
    params = jnp.concatenate([gain[0], capture[0].astype(F32)])
    away = swap(params)
    params = (pick(params, away), pick(away, params))
    gains = [v[:width] for v in params]
    caps = [v[width:] for v in params]
    table = jnp.maximum(slot_table, 0).reshape(NZ, NYH, capacity)
    table = jnp.where(yh == 0, table, table[:, ::-1])
    near = table
    for bit in (4, 2, 1):
        parts = near.reshape(NZ // (2 * bit), 2, bit, NYH, capacity)
        near = jnp.where(z & bit > 0, parts[:, ::-1], parts).reshape(table.shape)
    near = near.reshape(2, 2, 2, NYH, capacity).transpose(2, 1, 0, 3, 4)

    def begin(s, rows_a, after=()):
        rows_a = (f32(rows_a) * gains[s]).astype(BF)
        sent = project_first(rows_a, w, got_other, pipe == s, other + pipe, after)
        return rows_a, sent, tensor_perm(sent, y_other)

    def rest(s, rows_a, rows_b, after=()):
        rows_b = (f32(rows_b) * gains[s]).astype(BF)
        columns = (mine + pipe, other + pipe)
        return project_rest(rows_a, rows_b, w, got_other, got_mine, pipe == s, columns, after, s == 0)

    def finish(rows, squares, total):
        part = lax.dynamic_slice_in_dim(rows, pipe * half, half, 1)
        scale = lax.rsqrt(squares / (width * NT) + EPS)[:, None]
        part = (f32(part) + total * scale).astype(BF)
        other = swap(part)
        return jnp.concatenate([pick(part, other), pick(other, part)], axis=1)

    side, over = lambda t: t ^ 1, lambda t: t ^ 2
    squares = square_sum(x0)
    squares = squares + tensor_perm(squares, y_other)
    got_squares = tensor_perm(squares, side)
    rows_a, sent, got_y = begin(0, x0[:ROWS_A])
    squares = plus(squares, got_squares, [sent])
    squares0 = squares + tensor_perm(squares, over)
    flat0 = squares0.reshape(-1)
    outs = rest(0, rows_a, x0[ROWS_A:])
    keep, send = factor_parts(x0, squares0, gains[0], caps[0], near, pipe, block, outs[4:5])
    got_z = z_perm(send, 1)
    sum_a, sum_b = reduce_projection(outs, got_y, ring_first(*outs[:2]))
    x1a = finish(x0[:ROWS_A], flat0[:ROWS_A], sum_a)
    x1b = finish(x0[ROWS_A:], flat0[ROWS_A:], sum_b)
    keep0, send0 = fold(keep, got_z, [x1a])
    got_z0 = z_perm(send0, 2)

    rows_a, sent, got_y = begin(1, x1a)
    x1 = jnp.concatenate([x1a, x1b], axis=0)
    squares = square_sum(x1)
    got_squares = tensor_perm(squares, side)
    squares = plus(squares, got_squares, [sent])
    got_squares = tensor_perm(squares, over)
    outs = rest(1, rows_a, x1b, [squares, send0])
    keep0, send0 = fold(keep0, got_z0, outs[:1])
    squares = plus(squares, got_squares, outs[:1])
    squares1 = squares + tensor_perm(squares, y_other)
    flat1 = squares1.reshape(-1)
    got_b = ring_first(*outs[:2])
    got_z0 = z_perm(send0, 4)
    tot0 = keep0[0] + f32(got_z0[0])
    waits = [got_z0]
    keep, send = factor_parts(x1, squares1, gains[1], caps[1], near, pipe, block, waits)
    keep, send = fold(keep, z_perm(send, 1), [])
    got_z = z_perm(send, 2)
    early = [keep]
    keep, send = fold(keep, got_z, [])
    sum_a, sum_b = reduce_projection(outs, got_y, got_b, [keep], [])
    tot1 = keep[0] + f32(z_perm(send, 4)[0])
    x2 = finish(x1, flat1, jnp.concatenate([sum_a, sum_b], axis=0))
    out = pick(x1, x2).reshape(1, micro, each, width)
    totals = jnp.stack([tot0, tot1])
    totals = totals[:, :capacity] + f32(y_far(totals[:, capacity:].astype(BF)))
    kept, got = pick(totals[0], totals[1]), pick(totals[1], totals[0])
    got = f32(swap(got.astype(BF)))
    blocks = [pick(kept, got), pick(got, kept)]
    blocks = jnp.concatenate(blocks, axis=1)
    own = lax.dynamic_slice_in_dim(slot_table, (z * NYH + yh) * capacity, capacity)
    new = jnp.where(
        (own >= 0)[:, None, None], DECAY * old + (1.0 - DECAY) * blocks, jnp.float32(0.0)
    )
    return (out, new[None, None])


def solution(mesh):
    devices = mesh.devices.reshape(NZ, NYH, 2, NT)
    fine = jax.sharding.Mesh(devices, ("z", "yh", "pipe", "tensor"))
    dp = ("z", "yh")
    placed = (
        P(None, dp, "tensor"),
        P("pipe", "tensor"),
        P("pipe", "tensor", None),
        P("pipe", "tensor", dp, None, None),
        P(),
        P("pipe", None),
    )
    return jax.shard_map(
        local,
        mesh=fine,
        in_specs=placed,
        out_specs=(P("pipe", None, dp, "tensor"), P("pipe", "tensor", dp, None, None)),
        check_vma=False,
    )
```

```python
import jax
import jax.numpy as jnp
from jax import lax
from jax.experimental import pallas as pl
from jax.experimental.pallas import tpu as pltpu
from jax.sharding import PartitionSpec as P

EPS = 1e-06
DECAY = 0.9
BF = jnp.bfloat16
F32 = jnp.float32
NX, NYL, NZ, NYH = 4, 2, 8, 2
NT = NX * NYL
NDP = NZ * NYH
ROWS_A = 224
VMEM = 48 * 1024 * 1024
SMALL = pl.CostEstimate(flops=1024, bytes_accessed=1024, transcendentals=0)


def f32(v):
    return v.astype(F32)


def tensor_perm(value, to):
    return lax.ppermute(value, "tensor", [(t, to(t)) for t in range(NT)])


def x_by(k):
    return lambda t: (t // NX) * NX + (t % NX + k) % NX


def y_other(t):
    return t ^ NX


def swap(value):
    return lax.ppermute(value, "pipe", [(0, 1), (1, 0)])


def z_perm(value, bit):
    return lax.ppermute(value, "z", [(d, d ^ bit) for d in range(NZ)])


def y_far(value):
    return lax.ppermute(value, "yh", [(0, 1), (1, 0)])


def cut_weight(weight, columns):
    count = columns.shape[0]
    depth, width = weight.shape[0], weight.shape[1] // NT // 2

    def kernel(columns_ref, w_ref, out_ref, sems):
        copies = []
        for i in range(count):
            at = pl.multiple_of(columns_ref[i] * width, width)
            copies.append(
                pltpu.make_async_copy(w_ref.at[:, pl.ds(at, width)], out_ref.at[i], sems.at[i])
            )
        for copy in copies:
            copy.start()
        for copy in copies:
            copy.wait()

    return pl.pallas_call(
        kernel,
        in_specs=[pl.BlockSpec(memory_space=pltpu.SMEM), pl.BlockSpec(memory_space=pl.ANY)],
        out_specs=pl.BlockSpec(memory_space=pltpu.VMEM),
        out_shape=jax.ShapeDtypeStruct((count, depth, width), weight.dtype),
        scratch_shapes=[pltpu.SemaphoreType.DMA((count,))],
        compiler_params=pltpu.CompilerParams(vmem_limit_bytes=VMEM),
        cost_estimate=SMALL,
    )(columns, weight)


def project(rows, weight, got, own, columns, sources, jobs, shapes, after=()):
    count, depth = len(jobs), rows[0].shape[1]
    width = got[0].shape[2]
    n_rows, many, n_out = len(rows), len(got), len(shapes)
    table = jnp.concatenate([own.astype(jnp.int32)[None], columns])

    def kernel(table_ref, w_ref, *rest):
        rest = rest[len(after) :]
        got_refs, rest = rest[:many], rest[many:]
        row_refs, outs = rest[:n_rows], rest[n_rows : n_rows + n_out]
        blocks, sems = rest[n_rows + n_out :]
        mine = table_ref[0] > 0

        @pl.when(mine)
        def _():
            for i in range(count):
                at = pl.multiple_of(table_ref[1 + i] * width, width)
                pltpu.make_async_copy(
                    w_ref.at[:, pl.ds(at, width)], blocks.at[i], sems.at[i]
                ).start()

        @pl.when(jnp.logical_not(mine))
        def _():
            for i in range(count):
                pltpu.make_async_copy(
                    got_refs[sources[i][0]].at[sources[i][1]], blocks.at[i], sems.at[i]
                ).start()

        for i, job in enumerate(jobs):
            pltpu.make_async_copy(got_refs[0].at[0], blocks.at[i], sems.at[i]).wait()
            for r, places in job:
                y = jnp.dot(row_refs[r][...], blocks[i], preferred_element_type=F32).astype(BF)
                half = y.shape[0] // 2
                for h, (o, at) in enumerate(places):
                    outs[o][at] = y[h * half : (h + 1) * half]

    out_shapes = [jax.ShapeDtypeStruct((*s, width), BF) for s in shapes]
    vmem = pl.BlockSpec(memory_space=pltpu.VMEM)
    anywhere = pl.BlockSpec(memory_space=pl.ANY)
    return pl.pallas_call(
        kernel,
        in_specs=[pl.BlockSpec(memory_space=pltpu.SMEM)]
        + [anywhere] * (1 + len(after) + many)
        + [vmem] * n_rows,
        out_specs=[vmem] * n_out,
        out_shape=out_shapes,
        scratch_shapes=[
            pltpu.VMEM((count, depth, width), BF),
            pltpu.SemaphoreType.DMA((count,)),
        ],
        compiler_params=pltpu.CompilerParams(vmem_limit_bytes=VMEM),
        cost_estimate=SMALL,
    )(table, weight, *after, *got, *rows)


def ring_first(first_p, first_m):
    return tensor_perm(first_p, x_by(1)), tensor_perm(first_m, x_by(-1))


def ring_second(got, next_p, next_m, own0, own1):
    got_p, got_m = got
    n = got_p.shape[0] // 2
    last_p = tensor_perm((f32(next_p) + f32(got_p[:n])).astype(BF), x_by(1))
    last_m = tensor_perm((f32(next_m) + f32(got_m[:n])).astype(BF), x_by(-1))
    h0 = f32(own0) + f32(got_m[n:]) + f32(last_p)
    h1 = f32(own1) + f32(got_p[n:]) + f32(last_m)
    return (last_p, last_m), h0, h1


PLACES = [((0, 0), (1, 0)), ((2, 0), (0, 1)), ((1, 1), (3, 0)), ((4, 0), (4, 1))]
FLAT = [0, 2, 4, 5, 6]


def project_first(rows_a, weight, got_other, own, columns_other, after):
    jobs = [[(0, tuple((0, FLAT[o] + at) for o, at in places))] for places in PLACES]
    shape = (8, rows_a.shape[0] // 2)
    sources = [(0, r) for r in range(len(jobs))]
    columns = (columns_other, sources, jobs, [shape], after)
    return project([rows_a], weight, [got_other], own, *columns)[0]


def project_rest(rows_a, rows_b, weight, got_other, got_mine, own, columns, after, split):
    got = [got_mine, got_other]
    both = jnp.stack(columns, axis=1).reshape(-1)
    half_a, half_b = rows_a.shape[0] // 2, rows_b.shape[0] // 2
    if not split:
        sources, jobs = [(w, r) for r in range(4) for w in range(2)], []
        for w, r in sources:
            job = [(0, tuple((o, 2 * at + w) for o, at in PLACES[r]))]
            if w == 0:
                job.append((1, tuple((5 + o, at) for o, at in PLACES[r])))
            jobs.append(job)
        ids = both
        shapes = [(n, half_b) for n in (4, 4, 2, 2, 4)] + [(n, half_a) for n in (2, 2, 1, 1, 2)]
        return project([rows_b, rows_a], weight, got, own, ids, sources, jobs, shapes, after)
    sources = [(w, r) for r in range(3) for w in range(2)]
    jobs = [[(0, tuple((o, 2 * at + w) for o, at in PLACES[r]))] for w, r in sources]
    ids = both[:6]
    shapes = [(n, half_b) for n in (4, 4, 2, 2)]
    first = project([rows_b], weight, got, own, ids, sources, jobs, shapes, after)
    sources = [(0, 0), (0, 1), (0, 2), (0, 3), (1, 3)]
    jobs = []
    for w, r in sources:
        job = [(0, tuple((0, 2 * at + w) for _, at in PLACES[r]))] if r == 3 else []
        if w == 0:
            job.append((1, tuple((1 + o, at) for o, at in PLACES[r])))
        jobs.append(job)
    ids = jnp.concatenate([columns[0], columns[1][3:]])
    shapes = [(4, half_b)] + [(n, half_a) for n in (2, 2, 1, 1, 2)]
    second = project([rows_b, rows_a], weight, got, own, ids, sources, jobs, shapes, ())
    return [*first, *second]


def combine_away(own, got_p, got_m, last_p, last_m, after):
    rows, width = own.shape[1:]

    def kernel(own_ref, gp, gm, lp, lm, *rest):
        out = rest[-1]
        out[:rows] = (f32(own_ref[1]) + f32(gm[3]) + f32(lp[1])).astype(BF)
        out[rows:] = (f32(own_ref[3]) + f32(gp[3]) + f32(lm[1])).astype(BF)

    vmem = pl.BlockSpec(memory_space=pltpu.VMEM)
    return pl.pallas_call(
        kernel,
        in_specs=[vmem] * 5 + [pl.BlockSpec(memory_space=pl.ANY)] * len(after),
        out_specs=vmem,
        out_shape=jax.ShapeDtypeStruct((2 * rows, width), BF),
        compiler_params=pltpu.CompilerParams(vmem_limit_bytes=16 * 1024 * 1024),
        cost_estimate=SMALL,
    )(own, got_p, got_m, last_p, last_m, *after)


def reduce_projection(outs, got_y, got_b, after=(), later=()):
    width = got_y.shape[2]
    b_np, b_nm, b_own = outs[2:5]
    a_fp, a_fm, a_np, a_nm, a_own = outs[5:]
    got_b = tied(got_b, got_y)
    last_b, b0, b1 = ring_second(got_b, b_np, b_nm, b_own[:2], b_own[2:])
    add = lambda part, at: f32(part) + f32(got_y[at : at + part.shape[0]])
    got_a = ring_first(add(a_fp, 0).astype(BF), add(a_fm, 2).astype(BF))
    if after:
        sent = onward((a_np, a_nm), (got_y[4:5], got_y[5:6]), got_a, after)
        last_p, last_m = tensor_perm(sent[0], x_by(1)), tensor_perm(sent[1], x_by(-1))
        a0 = add(a_own[:1], 6) + f32(got_a[1][1:]) + f32(last_p)
        a1 = add(a_own[1:], 7) + f32(got_a[0][1:]) + f32(last_m)
        away = combine_away(b_own, *got_b, *last_b, later)
    else:
        _, a0, a1 = ring_second(
            got_a, add(a_np, 4), add(a_nm, 5), add(a_own[:1], 6), add(a_own[1:], 7)
        )
        away = jnp.concatenate([b0[1], b1[1]], axis=0).astype(BF)
    got_b = tensor_perm(away, y_other)
    sum_b = jnp.concatenate([b0[0], b1[0]], axis=0) + f32(got_b)
    sum_a = jnp.concatenate([a0[0], a1[0]], axis=0)
    return sum_a.reshape(-1, width), sum_b


def square_sum(rows):
    wide = f32(rows)
    return jnp.sum(wide * wide, axis=-1).reshape(-1, 128)


def tied(value, after):
    return lax.optimization_barrier((value, after))[0]


def gram_parts(normed, captured, ids, pipe, blocks, block, total_tokens, n_out, after):
    micro = captured.shape[0]
    rows, width = normed.shape
    each, sub = rows // micro, block // 2
    count = blocks * (blocks + 1) // 2
    slots = ids.shape[0] // NZ
    many = NZ // n_out

    def kernel(cap_ref, ids_ref, pipe_ref, n_ref, *rest):
        rest = rest[len(after) :]
        outs, left, grams = rest[:n_out], rest[n_out], rest[n_out + 1]
        live = cap_ref[0]
        for m in range(1, micro):
            live = live + cap_ref[m]
        for m in range(micro):
            part = pl.ds(m * each, each)
            left[part] = (f32(n_ref[part]) * cap_ref[m]).astype(BF)
        scale = 1.0 / jnp.full((1, 1), live * total_tokens, F32)
        b = 0
        for i in range(blocks):
            g = lax.dot_general(
                left[:, i * block : (i + 1) * block],
                n_ref[:, i * block :],
                (((0,), (0,)), ((), ())),
                preferred_element_type=F32,
            )
            g = g * scale
            for j in range(blocks - i):
                grams[b] = g[:, j * block : (j + 1) * block]
                b += 1
        at = pl.ds(pl.multiple_of(pipe_ref[0] * sub, sub), sub)
        for k in range(NZ):
            for i in range(slots):
                part = grams[ids_ref[k * slots + i], at, :].astype(BF)
                outs[k // many][k % many, i] = part

    smem = pl.BlockSpec(memory_space=pltpu.SMEM)
    vmem = pl.BlockSpec(memory_space=pltpu.VMEM)
    out_shape = [jax.ShapeDtypeStruct((many, slots, sub, block), BF)] * n_out
    return pl.pallas_call(
        kernel,
        in_specs=[smem, smem, smem, vmem] + [pl.BlockSpec(memory_space=pl.ANY)] * len(after),
        out_specs=[vmem] * n_out,
        out_shape=out_shape,
        scratch_shapes=[
            pltpu.VMEM((rows, width), BF),
            pltpu.VMEM((count, block, block), F32),
        ],
        compiler_params=pltpu.CompilerParams(vmem_limit_bytes=VMEM),
        cost_estimate=SMALL,
    )(captured, ids, pipe[None], normed, *after)


def factor_parts(rows, squares, gain, captured, table, pipe, block, after):
    width = rows.shape[1]
    scale = lax.rsqrt(squares / (width * NT) + EPS).reshape(-1, 1)
    normed = (f32(rows) * scale * gain).astype(BF)
    tokens = rows.shape[0] // captured.shape[0] * NDP
    ids = table.reshape(-1)
    return gram_parts(
        normed, captured, ids, pipe, width // block, block, float(tokens), 2, after
    )


def fold(keep, got, after):
    half = keep.shape[0] // 2
    shape = (half, *keep.shape[1:])

    def kernel(keep_ref, got_ref, *rest):
        left, right = rest[len(after) :]
        for i in range(half):
            left[i] = f32(keep_ref[i]) + f32(got_ref[i])
            right[i] = (f32(keep_ref[half + i]) + f32(got_ref[half + i])).astype(BF)

    vmem = pl.BlockSpec(memory_space=pltpu.VMEM)
    return pl.pallas_call(
        kernel,
        in_specs=[vmem, vmem] + [pl.BlockSpec(memory_space=pl.ANY)] * len(after),
        out_specs=[vmem, vmem],
        out_shape=[jax.ShapeDtypeStruct(shape, F32), jax.ShapeDtypeStruct(shape, BF)],
        compiler_params=pltpu.CompilerParams(vmem_limit_bytes=16 * 1024 * 1024),
        cost_estimate=SMALL,
    )(keep, got, *after)


def plus(a, b, after):
    def kernel(a_ref, b_ref, *rest):
        rest[-1][...] = a_ref[...] + b_ref[...]

    vmem = pl.BlockSpec(memory_space=pltpu.VMEM)
    return pl.pallas_call(
        kernel,
        in_specs=[vmem, vmem] + [pl.BlockSpec(memory_space=pl.ANY)] * len(after),
        out_specs=vmem,
        out_shape=jax.ShapeDtypeStruct(a.shape, F32),
        compiler_params=pltpu.CompilerParams(vmem_limit_bytes=16 * 1024 * 1024),
        cost_estimate=SMALL,
    )(a, b, *after)


def onward(own, got_y, got, after):
    def kernel(*refs):
        ins, outs = refs[:6], refs[-2:]
        for i in range(2):
            o, y, g = ins[3 * i : 3 * i + 3]
            outs[i][...] = (f32(o[...]) + f32(y[...]) + f32(g[:1])).astype(BF)

    vmem = pl.BlockSpec(memory_space=pltpu.VMEM)
    ins = [v for i in range(2) for v in (own[i], got_y[i], got[i])]
    return pl.pallas_call(
        kernel,
        in_specs=[vmem] * 6 + [pl.BlockSpec(memory_space=pl.ANY)] * len(after),
        out_specs=[vmem] * 2,
        out_shape=[jax.ShapeDtypeStruct(own[0].shape, BF)] * 2,
        compiler_params=pltpu.CompilerParams(vmem_limit_bytes=16 * 1024 * 1024),
        cost_estimate=SMALL,
    )(*ins, *after)


def local(section_input, gain, weight, old_factor, slot_table, capture):
    pipe = lax.axis_index("pipe")
    t = lax.axis_index("tensor")
    z, yh = lax.axis_index("z"), lax.axis_index("yh")
    yl, x = t // NX, t % NX
    first = pipe == 0
    micro, each, width = section_input.shape
    half = width // 2
    w = weight[0]
    old = old_factor[0, 0]
    capacity, block, _ = old.shape
    x0 = section_input.reshape(micro * each, width)

    def pick(a, b):
        return jnp.where(first, a, b)

    ring = jnp.stack([(x + 2) % NX, (x + 1) % NX, (x + 3) % NX, x])
    other, mine = 2 * ((1 - yl) * NX + ring), 2 * (yl * NX + ring)
    got_other = swap(cut_weight(w, other + 1 - pipe))
    got_mine = swap(cut_weight(w, mine + 1 - pipe))
    params = jnp.concatenate([gain[0], capture[0].astype(F32)])
    away = swap(params)
    params = (pick(params, away), pick(away, params))
    gains = [v[:width] for v in params]
    caps = [v[width:] for v in params]
    table = jnp.maximum(slot_table, 0).reshape(NZ, NYH, capacity)
    table = jnp.where(yh == 0, table, table[:, ::-1])
    near = table
    for bit in (4, 2, 1):
        parts = near.reshape(NZ // (2 * bit), 2, bit, NYH, capacity)
        near = jnp.where(z & bit > 0, parts[:, ::-1], parts).reshape(table.shape)
    near = near.reshape(2, 2, 2, NYH, capacity).transpose(2, 1, 0, 3, 4)

    def begin(s, rows_a, after=()):
        rows_a = (f32(rows_a) * gains[s]).astype(BF)
        sent = project_first(rows_a, w, got_other, pipe == s, other + pipe, after)
        return rows_a, sent, tensor_perm(sent, y_other)

    def rest(s, rows_a, rows_b, after=()):
        rows_b = (f32(rows_b) * gains[s]).astype(BF)
        columns = (mine + pipe, other + pipe)
        return project_rest(rows_a, rows_b, w, got_other, got_mine, pipe == s, columns, after, s == 0)

    def finish(rows, squares, total):
        part = lax.dynamic_slice_in_dim(rows, pipe * half, half, 1)
        scale = lax.rsqrt(squares / (width * NT) + EPS)[:, None]
        part = (f32(part) + total * scale).astype(BF)
        other = swap(part)
        return jnp.concatenate([pick(part, other), pick(other, part)], axis=1)

    side, over = lambda t: t ^ 1, lambda t: t ^ 2
    squares = square_sum(x0)
    squares = squares + tensor_perm(squares, y_other)
    got_squares = tensor_perm(squares, side)
    rows_a, sent, got_y = begin(0, x0[:ROWS_A])
    squares = plus(squares, got_squares, [sent])
    squares0 = squares + tensor_perm(squares, over)
    flat0 = squares0.reshape(-1)
    outs = rest(0, rows_a, x0[ROWS_A:])
    keep, send = factor_parts(x0, squares0, gains[0], caps[0], near, pipe, block, outs[4:5])
    got_z = z_perm(send, 1)
    sum_a, sum_b = reduce_projection(outs, got_y, ring_first(*outs[:2]))
    x1a = finish(x0[:ROWS_A], flat0[:ROWS_A], sum_a)
    x1b = finish(x0[ROWS_A:], flat0[ROWS_A:], sum_b)
    keep0, send0 = fold(keep, got_z, [x1a])
    got_z0 = z_perm(send0, 2)

    rows_a, sent, got_y = begin(1, x1a)
    x1 = jnp.concatenate([x1a, x1b], axis=0)
    squares = square_sum(x1)
    got_squares = tensor_perm(squares, side)
    squares = plus(squares, got_squares, [sent])
    got_squares = tensor_perm(squares, over)
    outs = rest(1, rows_a, x1b, [squares, send0])
    keep0, send0 = fold(keep0, got_z0, outs[:1])
    squares = plus(squares, got_squares, outs[:1])
    squares1 = squares + tensor_perm(squares, y_other)
    flat1 = squares1.reshape(-1)
    got_b = ring_first(*outs[:2])
    got_z0 = z_perm(send0, 4)
    tot0 = keep0[0] + f32(got_z0[0])
    waits = [got_z0]
    keep, send = factor_parts(x1, squares1, gains[1], caps[1], near, pipe, block, waits)
    keep, send = fold(keep, z_perm(send, 1), [])
    got_z = z_perm(send, 2)
    early = [keep]
    keep, send = fold(keep, got_z, [])
    sum_a, sum_b = reduce_projection(outs, got_y, got_b, [keep], [])
    tot1 = keep[0] + f32(z_perm(send, 4)[0])
    x2 = finish(x1, flat1, jnp.concatenate([sum_a, sum_b], axis=0))
    out = pick(x1, x2).reshape(1, micro, each, width)
    totals = jnp.stack([tot0, tot1])
    totals = totals[:, :capacity] + f32(y_far(totals[:, capacity:].astype(BF)))
    kept, got = pick(totals[0], totals[1]), pick(totals[1], totals[0])
    got = f32(swap(got.astype(BF)))
    blocks = [pick(kept, got), pick(got, kept)]
    blocks = jnp.concatenate(blocks, axis=1)
    own = lax.dynamic_slice_in_dim(slot_table, (z * NYH + yh) * capacity, capacity)
    new = jnp.where(
        (own >= 0)[:, None, None], DECAY * old + (1.0 - DECAY) * blocks, jnp.float32(0.0)
    )
    return (out, new[None, None])


def solution(mesh):
    devices = mesh.devices.reshape(NZ, NYH, 2, NT)
    fine = jax.sharding.Mesh(devices, ("z", "yh", "pipe", "tensor"))
    dp = ("z", "yh")
    placed = (
        P(None, dp, "tensor"),
        P("pipe", "tensor"),
        P("pipe", "tensor", None),
        P("pipe", "tensor", dp, None, None),
        P(),
        P("pipe", None),
    )
    return jax.shard_map(
        local,
        mesh=fine,
        in_specs=placed,
        out_specs=(P("pipe", None, dp, "tensor"), P("pipe", "tensor", dp, None, None)),
        check_vma=False,
    )
```

```python
import jax
import jax.numpy as jnp
from jax import lax
from jax.experimental import pallas as pl
from jax.experimental.pallas import tpu as pltpu
from jax.sharding import PartitionSpec as P

EPS = 1e-06
DECAY = 0.9
BF = jnp.bfloat16
F32 = jnp.float32
NX, NYL, NZ, NYH = 4, 2, 8, 2
NT = NX * NYL
NDP = NZ * NYH
ROWS_A = 256
VMEM = 48 * 1024 * 1024
SMALL = pl.CostEstimate(flops=1024, bytes_accessed=1024, transcendentals=0)


def f32(v):
    return v.astype(F32)


def tensor_perm(value, to):
    return lax.ppermute(value, "tensor", [(t, to(t)) for t in range(NT)])


def x_by(k):
    return lambda t: (t // NX) * NX + (t % NX + k) % NX


def y_other(t):
    return t ^ NX


def swap(value):
    return lax.ppermute(value, "pipe", [(0, 1), (1, 0)])


def z_perm(value, bit):
    return lax.ppermute(value, "z", [(d, d ^ bit) for d in range(NZ)])


def y_far(value):
    return lax.ppermute(value, "yh", [(0, 1), (1, 0)])


def cut_weight(weight, columns):
    count = columns.shape[0]
    depth, width = weight.shape[0], weight.shape[1] // NT // 2

    def kernel(columns_ref, w_ref, out_ref, sems):
        copies = []
        for i in range(count):
            at = pl.multiple_of(columns_ref[i] * width, width)
            copies.append(
                pltpu.make_async_copy(w_ref.at[:, pl.ds(at, width)], out_ref.at[i], sems.at[i])
            )
        for copy in copies:
            copy.start()
        for copy in copies:
            copy.wait()

    return pl.pallas_call(
        kernel,
        in_specs=[pl.BlockSpec(memory_space=pltpu.SMEM), pl.BlockSpec(memory_space=pl.ANY)],
        out_specs=pl.BlockSpec(memory_space=pltpu.VMEM),
        out_shape=jax.ShapeDtypeStruct((count, depth, width), weight.dtype),
        scratch_shapes=[pltpu.SemaphoreType.DMA((count,))],
        compiler_params=pltpu.CompilerParams(vmem_limit_bytes=VMEM),
        cost_estimate=SMALL,
    )(columns, weight)


def project(rows, weight, got, own, columns, sources, jobs, shapes, after=()):
    count, depth = len(jobs), rows[0].shape[1]
    width = got[0].shape[2]
    n_rows, many, n_out = len(rows), len(got), len(shapes)
    table = jnp.concatenate([own.astype(jnp.int32)[None], columns])

    def kernel(table_ref, w_ref, *rest):
        rest = rest[len(after) :]
        got_refs, rest = rest[:many], rest[many:]
        row_refs, outs = rest[:n_rows], rest[n_rows : n_rows + n_out]
        blocks, sems = rest[n_rows + n_out :]
        mine = table_ref[0] > 0

        @pl.when(mine)
        def _():
            for i in range(count):
                at = pl.multiple_of(table_ref[1 + i] * width, width)
                pltpu.make_async_copy(
                    w_ref.at[:, pl.ds(at, width)], blocks.at[i], sems.at[i]
                ).start()

        @pl.when(jnp.logical_not(mine))
        def _():
            for i in range(count):
                pltpu.make_async_copy(
                    got_refs[sources[i][0]].at[sources[i][1]], blocks.at[i], sems.at[i]
                ).start()

        for i, job in enumerate(jobs):
            pltpu.make_async_copy(got_refs[0].at[0], blocks.at[i], sems.at[i]).wait()
            for r, places in job:
                y = jnp.dot(row_refs[r][...], blocks[i], preferred_element_type=F32).astype(BF)
                half = y.shape[0] // 2
                for h, (o, at) in enumerate(places):
                    outs[o][at] = y[h * half : (h + 1) * half]

    out_shapes = [jax.ShapeDtypeStruct((*s, width), BF) for s in shapes]
    vmem = pl.BlockSpec(memory_space=pltpu.VMEM)
    anywhere = pl.BlockSpec(memory_space=pl.ANY)
    return pl.pallas_call(
        kernel,
        in_specs=[pl.BlockSpec(memory_space=pltpu.SMEM)]
        + [anywhere] * (1 + len(after) + many)
        + [vmem] * n_rows,
        out_specs=[vmem] * n_out,
        out_shape=out_shapes,
        scratch_shapes=[
            pltpu.VMEM((count, depth, width), BF),
            pltpu.SemaphoreType.DMA((count,)),
        ],
        compiler_params=pltpu.CompilerParams(vmem_limit_bytes=VMEM),
        cost_estimate=SMALL,
    )(table, weight, *after, *got, *rows)


def ring_first(first_p, first_m):
    return tensor_perm(first_p, x_by(1)), tensor_perm(first_m, x_by(-1))


def ring_second(got, next_p, next_m, own0, own1):
    got_p, got_m = got
    n = got_p.shape[0] // 2
    last_p = tensor_perm((f32(next_p) + f32(got_p[:n])).astype(BF), x_by(1))
    last_m = tensor_perm((f32(next_m) + f32(got_m[:n])).astype(BF), x_by(-1))
    h0 = f32(own0) + f32(got_m[n:]) + f32(last_p)
    h1 = f32(own1) + f32(got_p[n:]) + f32(last_m)
    return (last_p, last_m), h0, h1


PLACES = [((0, 0), (1, 0)), ((2, 0), (0, 1)), ((1, 1), (3, 0)), ((4, 0), (4, 1))]
FLAT = [0, 2, 4, 5, 6]


def project_first(rows_a, weight, got_other, own, columns_other, after):
    jobs = [[(0, tuple((0, FLAT[o] + at) for o, at in places))] for places in PLACES]
    shape = (8, rows_a.shape[0] // 2)
    sources = [(0, r) for r in range(len(jobs))]
    columns = (columns_other, sources, jobs, [shape], after)
    return project([rows_a], weight, [got_other], own, *columns)[0]


def project_rest(rows_a, rows_b, weight, got_other, got_mine, own, columns, after, split):
    got = [got_mine, got_other]
    both = jnp.stack(columns, axis=1).reshape(-1)
    half_a, half_b = rows_a.shape[0] // 2, rows_b.shape[0] // 2
    if not split:
        sources, jobs = [(w, r) for r in range(4) for w in range(2)], []
        for w, r in sources:
            job = [(0, tuple((o, 2 * at + w) for o, at in PLACES[r]))]
            if w == 0:
                job.append((1, tuple((5 + o, at) for o, at in PLACES[r])))
            jobs.append(job)
        ids = both
        shapes = [(n, half_b) for n in (4, 4, 2, 2, 4)] + [(n, half_a) for n in (2, 2, 1, 1, 2)]
        return project([rows_b, rows_a], weight, got, own, ids, sources, jobs, shapes, after)
    sources = [(w, r) for r in range(3) for w in range(2)]
    jobs = [[(0, tuple((o, 2 * at + w) for o, at in PLACES[r]))] for w, r in sources]
    ids = both[:6]
    shapes = [(n, half_b) for n in (4, 4, 2, 2)]
    first = project([rows_b], weight, got, own, ids, sources, jobs, shapes, after)
    sources = [(0, 0), (0, 1), (0, 2), (0, 3), (1, 3)]
    jobs = []
    for w, r in sources:
        job = [(0, tuple((0, 2 * at + w) for _, at in PLACES[r]))] if r == 3 else []
        if w == 0:
            job.append((1, tuple((1 + o, at) for o, at in PLACES[r])))
        jobs.append(job)
    ids = jnp.concatenate([columns[0], columns[1][3:]])
    shapes = [(4, half_b)] + [(n, half_a) for n in (2, 2, 1, 1, 2)]
    second = project([rows_b, rows_a], weight, got, own, ids, sources, jobs, shapes, ())
    return [*first, *second]


def combine_away(own, got_p, got_m, last_p, last_m, after):
    rows, width = own.shape[1:]

    def kernel(own_ref, gp, gm, lp, lm, *rest):
        out = rest[-1]
        out[:rows] = (f32(own_ref[1]) + f32(gm[3]) + f32(lp[1])).astype(BF)
        out[rows:] = (f32(own_ref[3]) + f32(gp[3]) + f32(lm[1])).astype(BF)

    vmem = pl.BlockSpec(memory_space=pltpu.VMEM)
    return pl.pallas_call(
        kernel,
        in_specs=[vmem] * 5 + [pl.BlockSpec(memory_space=pl.ANY)] * len(after),
        out_specs=vmem,
        out_shape=jax.ShapeDtypeStruct((2 * rows, width), BF),
        compiler_params=pltpu.CompilerParams(vmem_limit_bytes=16 * 1024 * 1024),
        cost_estimate=SMALL,
    )(own, got_p, got_m, last_p, last_m, *after)


def reduce_projection(outs, got_y, got_b, after=(), later=()):
    width = got_y.shape[2]
    b_np, b_nm, b_own = outs[2:5]
    a_fp, a_fm, a_np, a_nm, a_own = outs[5:]
    got_b = tied(got_b, got_y)
    last_b, b0, b1 = ring_second(got_b, b_np, b_nm, b_own[:2], b_own[2:])
    add = lambda part, at: f32(part) + f32(got_y[at : at + part.shape[0]])
    got_a = ring_first(add(a_fp, 0).astype(BF), add(a_fm, 2).astype(BF))
    if after:
        sent = onward((a_np, a_nm), (got_y[4:5], got_y[5:6]), got_a, after)
        last_p, last_m = tensor_perm(sent[0], x_by(1)), tensor_perm(sent[1], x_by(-1))
        a0 = add(a_own[:1], 6) + f32(got_a[1][1:]) + f32(last_p)
        a1 = add(a_own[1:], 7) + f32(got_a[0][1:]) + f32(last_m)
        away = combine_away(b_own, *got_b, *last_b, later)
    else:
        _, a0, a1 = ring_second(
            got_a, add(a_np, 4), add(a_nm, 5), add(a_own[:1], 6), add(a_own[1:], 7)
        )
        away = jnp.concatenate([b0[1], b1[1]], axis=0).astype(BF)
    got_b = tensor_perm(away, y_other)
    sum_b = jnp.concatenate([b0[0], b1[0]], axis=0) + f32(got_b)
    sum_a = jnp.concatenate([a0[0], a1[0]], axis=0)
    return sum_a.reshape(-1, width), sum_b


def square_sum(rows):
    wide = f32(rows)
    return jnp.sum(wide * wide, axis=-1).reshape(-1, 128)


def tied(value, after):
    return lax.optimization_barrier((value, after))[0]


def gram_parts(normed, captured, ids, pipe, blocks, block, total_tokens, n_out, after):
    micro = captured.shape[0]
    rows, width = normed.shape
    each, sub = rows // micro, block // 2
    count = blocks * (blocks + 1) // 2
    slots = ids.shape[0] // NZ
    many = NZ // n_out

    def kernel(cap_ref, ids_ref, pipe_ref, n_ref, *rest):
        rest = rest[len(after) :]
        outs, left, grams = rest[:n_out], rest[n_out], rest[n_out + 1]
        live = cap_ref[0]
        for m in range(1, micro):
            live = live + cap_ref[m]
        for m in range(micro):
            part = pl.ds(m * each, each)
            left[part] = (f32(n_ref[part]) * cap_ref[m]).astype(BF)
        scale = 1.0 / jnp.full((1, 1), live * total_tokens, F32)
        b = 0
        for i in range(blocks):
            g = lax.dot_general(
                left[:, i * block : (i + 1) * block],
                n_ref[:, i * block :],
                (((0,), (0,)), ((), ())),
                preferred_element_type=F32,
            )
            g = g * scale
            for j in range(blocks - i):
                grams[b] = g[:, j * block : (j + 1) * block]
                b += 1
        at = pl.ds(pl.multiple_of(pipe_ref[0] * sub, sub), sub)
        for k in range(NZ):
            for i in range(slots):
                part = grams[ids_ref[k * slots + i], at, :].astype(BF)
                outs[k // many][k % many, i] = part

    smem = pl.BlockSpec(memory_space=pltpu.SMEM)
    vmem = pl.BlockSpec(memory_space=pltpu.VMEM)
    out_shape = [jax.ShapeDtypeStruct((many, slots, sub, block), BF)] * n_out
    return pl.pallas_call(
        kernel,
        in_specs=[smem, smem, smem, vmem] + [pl.BlockSpec(memory_space=pl.ANY)] * len(after),
        out_specs=[vmem] * n_out,
        out_shape=out_shape,
        scratch_shapes=[
            pltpu.VMEM((rows, width), BF),
            pltpu.VMEM((count, block, block), F32),
        ],
        compiler_params=pltpu.CompilerParams(vmem_limit_bytes=VMEM),
        cost_estimate=SMALL,
    )(captured, ids, pipe[None], normed, *after)


def factor_parts(rows, squares, gain, captured, table, pipe, block, after):
    width = rows.shape[1]
    scale = lax.rsqrt(squares / (width * NT) + EPS).reshape(-1, 1)
    normed = (f32(rows) * scale * gain).astype(BF)
    tokens = rows.shape[0] // captured.shape[0] * NDP
    ids = table.reshape(-1)
    return gram_parts(
        normed, captured, ids, pipe, width // block, block, float(tokens), 2, after
    )


def fold(keep, got, after):
    half = keep.shape[0] // 2
    shape = (half, *keep.shape[1:])

    def kernel(keep_ref, got_ref, *rest):
        left, right = rest[len(after) :]
        for i in range(half):
            left[i] = f32(keep_ref[i]) + f32(got_ref[i])
            right[i] = (f32(keep_ref[half + i]) + f32(got_ref[half + i])).astype(BF)

    vmem = pl.BlockSpec(memory_space=pltpu.VMEM)
    return pl.pallas_call(
        kernel,
        in_specs=[vmem, vmem] + [pl.BlockSpec(memory_space=pl.ANY)] * len(after),
        out_specs=[vmem, vmem],
        out_shape=[jax.ShapeDtypeStruct(shape, F32), jax.ShapeDtypeStruct(shape, BF)],
        compiler_params=pltpu.CompilerParams(vmem_limit_bytes=16 * 1024 * 1024),
        cost_estimate=SMALL,
    )(keep, got, *after)


def plus(a, b, after):
    def kernel(a_ref, b_ref, *rest):
        rest[-1][...] = a_ref[...] + b_ref[...]

    vmem = pl.BlockSpec(memory_space=pltpu.VMEM)
    return pl.pallas_call(
        kernel,
        in_specs=[vmem, vmem] + [pl.BlockSpec(memory_space=pl.ANY)] * len(after),
        out_specs=vmem,
        out_shape=jax.ShapeDtypeStruct(a.shape, F32),
        compiler_params=pltpu.CompilerParams(vmem_limit_bytes=16 * 1024 * 1024),
        cost_estimate=SMALL,
    )(a, b, *after)


def onward(own, got_y, got, after):
    def kernel(*refs):
        ins, outs = refs[:6], refs[-2:]
        for i in range(2):
            o, y, g = ins[3 * i : 3 * i + 3]
            outs[i][...] = (f32(o[...]) + f32(y[...]) + f32(g[:1])).astype(BF)

    vmem = pl.BlockSpec(memory_space=pltpu.VMEM)
    ins = [v for i in range(2) for v in (own[i], got_y[i], got[i])]
    return pl.pallas_call(
        kernel,
        in_specs=[vmem] * 6 + [pl.BlockSpec(memory_space=pl.ANY)] * len(after),
        out_specs=[vmem] * 2,
        out_shape=[jax.ShapeDtypeStruct(own[0].shape, BF)] * 2,
        compiler_params=pltpu.CompilerParams(vmem_limit_bytes=16 * 1024 * 1024),
        cost_estimate=SMALL,
    )(*ins, *after)


def local(section_input, gain, weight, old_factor, slot_table, capture):
    pipe = lax.axis_index("pipe")
    t = lax.axis_index("tensor")
    z, yh = lax.axis_index("z"), lax.axis_index("yh")
    yl, x = t // NX, t % NX
    first = pipe == 0
    micro, each, width = section_input.shape
    half = width // 2
    w = weight[0]
    old = old_factor[0, 0]
    capacity, block, _ = old.shape
    x0 = section_input.reshape(micro * each, width)

    def pick(a, b):
        return jnp.where(first, a, b)

    ring = jnp.stack([(x + 2) % NX, (x + 1) % NX, (x + 3) % NX, x])
    other, mine = 2 * ((1 - yl) * NX + ring), 2 * (yl * NX + ring)
    got_other = swap(cut_weight(w, other + 1 - pipe))
    got_mine = swap(cut_weight(w, mine + 1 - pipe))
    params = jnp.concatenate([gain[0], capture[0].astype(F32)])
    away = swap(params)
    params = (pick(params, away), pick(away, params))
    gains = [v[:width] for v in params]
    caps = [v[width:] for v in params]
    table = jnp.maximum(slot_table, 0).reshape(NZ, NYH, capacity)
    table = jnp.where(yh == 0, table, table[:, ::-1])
    near = table
    for bit in (4, 2, 1):
        parts = near.reshape(NZ // (2 * bit), 2, bit, NYH, capacity)
        near = jnp.where(z & bit > 0, parts[:, ::-1], parts).reshape(table.shape)
    near = near.reshape(2, 2, 2, NYH, capacity).transpose(2, 1, 0, 3, 4)

    def begin(s, rows_a, after=()):
        rows_a = (f32(rows_a) * gains[s]).astype(BF)
        sent = project_first(rows_a, w, got_other, pipe == s, other + pipe, after)
        return rows_a, sent, tensor_perm(sent, y_other)

    def rest(s, rows_a, rows_b, after=()):
        rows_b = (f32(rows_b) * gains[s]).astype(BF)
        columns = (mine + pipe, other + pipe)
        return project_rest(rows_a, rows_b, w, got_other, got_mine, pipe == s, columns, after, s == 0)

    def finish(rows, squares, total):
        part = lax.dynamic_slice_in_dim(rows, pipe * half, half, 1)
        scale = lax.rsqrt(squares / (width * NT) + EPS)[:, None]
        part = (f32(part) + total * scale).astype(BF)
        other = swap(part)
        return jnp.concatenate([pick(part, other), pick(other, part)], axis=1)

    side, over = lambda t: t ^ 1, lambda t: t ^ 2
    squares = square_sum(x0)
    squares = squares + tensor_perm(squares, y_other)
    got_squares = tensor_perm(squares, side)
    rows_a, sent, got_y = begin(0, x0[:ROWS_A])
    squares = plus(squares, got_squares, [sent])
    squares0 = squares + tensor_perm(squares, over)
    flat0 = squares0.reshape(-1)
    outs = rest(0, rows_a, x0[ROWS_A:])
    keep, send = factor_parts(x0, squares0, gains[0], caps[0], near, pipe, block, outs[4:5])
    got_z = z_perm(send, 1)
    sum_a, sum_b = reduce_projection(outs, got_y, ring_first(*outs[:2]))
    x1a = finish(x0[:ROWS_A], flat0[:ROWS_A], sum_a)
    x1b = finish(x0[ROWS_A:], flat0[ROWS_A:], sum_b)
    keep0, send0 = fold(keep, got_z, [x1a])
    got_z0 = z_perm(send0, 2)

    rows_a, sent, got_y = begin(1, x1a)
    x1 = jnp.concatenate([x1a, x1b], axis=0)
    squares = square_sum(x1)
    got_squares = tensor_perm(squares, side)
    squares = plus(squares, got_squares, [sent])
    got_squares = tensor_perm(squares, over)
    outs = rest(1, rows_a, x1b, [squares, send0])
    keep0, send0 = fold(keep0, got_z0, outs[:1])
    squares = plus(squares, got_squares, outs[:1])
    squares1 = squares + tensor_perm(squares, y_other)
    flat1 = squares1.reshape(-1)
    got_b = ring_first(*outs[:2])
    got_z0 = z_perm(send0, 4)
    tot0 = keep0[0] + f32(got_z0[0])
    waits = [got_z0]
    keep, send = factor_parts(x1, squares1, gains[1], caps[1], near, pipe, block, waits)
    keep, send = fold(keep, z_perm(send, 1), [])
    got_z = z_perm(send, 2)
    early = [keep]
    keep, send = fold(keep, got_z, [])
    sum_a, sum_b = reduce_projection(outs, got_y, got_b, [keep], [])
    tot1 = keep[0] + f32(z_perm(send, 4)[0])
    x2 = finish(x1, flat1, jnp.concatenate([sum_a, sum_b], axis=0))
    out = pick(x1, x2).reshape(1, micro, each, width)
    totals = jnp.stack([tot0, tot1])
    totals = totals[:, :capacity] + f32(y_far(totals[:, capacity:].astype(BF)))
    kept, got = pick(totals[0], totals[1]), pick(totals[1], totals[0])
    got = f32(swap(got.astype(BF)))
    blocks = [pick(kept, got), pick(got, kept)]
    blocks = jnp.concatenate(blocks, axis=1)
    own = lax.dynamic_slice_in_dim(slot_table, (z * NYH + yh) * capacity, capacity)
    new = jnp.where(
        (own >= 0)[:, None, None], DECAY * old + (1.0 - DECAY) * blocks, jnp.float32(0.0)
    )
    return (out, new[None, None])


def solution(mesh):
    devices = mesh.devices.reshape(NZ, NYH, 2, NT)
    fine = jax.sharding.Mesh(devices, ("z", "yh", "pipe", "tensor"))
    dp = ("z", "yh")
    placed = (
        P(None, dp, "tensor"),
        P("pipe", "tensor"),
        P("pipe", "tensor", None),
        P("pipe", "tensor", dp, None, None),
        P(),
        P("pipe", None),
    )
    return jax.shard_map(
        local,
        mesh=fine,
        in_specs=placed,
        out_specs=(P("pipe", None, dp, "tensor"), P("pipe", "tensor", dp, None, None)),
        check_vma=False,
    )
```
